32 devices in a mesh: fsdp: 8 (over y, x, core), seq: 4 (over z).
Axes of the slice: x: 2, y: 2, z: 4, core: 2. Of those that a mesh axis runs over, the one named last changes fastest.
Arguments:
- layer_input: bfloat16 [8, 2, 1024, 768], P('fsdp', None, 'seq'), may hold values from -6 to 6
- segment_ids: int32 [8, 2, 1024], P('fsdp'), may hold values from 0 to 2, as said below
- gain_in: bfloat16 [768], P('fsdp'), may hold values from 0.5 to 1.5
- in_weight: bfloat16 [768, 3352], P('fsdp'), may hold values from -0.21875 to 0.21875
- conv_weight: bfloat16 [1792, 4], P('fsdp'), may hold values from -3 to 3
- conv_bias: bfloat16 [1792], P('fsdp'), may hold values from -0.5 to 0.5
- dt_bias: bfloat16 [24], replicated, may hold values from -7 to -2.296875
- a_log: bfloat16 [24], replicated, may hold values from 0 to 2.765625
- skip_gain: bfloat16 [24], replicated, may hold values from 0.5 to 1.5
- gain_out: bfloat16 [1536], P('fsdp'), may hold values from 0.5 to 1.5
- out_weight: bfloat16 [1536, 768], P('fsdp'), may hold values from -0.15625 to 0.15625
- cotangent: bfloat16 [8, 2, 1024, 768], P('fsdp', None, 'seq'), may hold values from -6 to 6
Outputs:
- layer_output: bfloat16 [8, 2, 1024, 768], P('fsdp', None, 'seq')
- input_grad: float32 [8, 2, 1024, 768], P('fsdp', None, 'seq')
- grad_gain_in: float32 [768], P('fsdp')
- grad_in_weight: float32 [768, 3352], P('fsdp')
- grad_conv_weight: float32 [1792, 4], P('fsdp')
- grad_conv_bias: float32 [1792], P('fsdp')
- grad_dt_bias: float32 [24], replicated
- grad_a_log: float32 [24], replicated
- grad_skip_gain: float32 [24], replicated
- grad_gain_out: float32 [1536], P('fsdp')
- grad_out_weight: float32 [1536, 768], P('fsdp')
The draws below stay inside these ranges and needn't reach their ends.
Inputs may be any that keep to these rules, and one draw needn't show every extreme that they name: `segment_ids`: along each sequence the segment numbers start at 0 and never fall; segment 1 begins within the first 256 positions and segment 2 within the last 256, so all three are present.
All inputs are finite; a program needn't handle non-finite values.
Results may differ from the reference program's by a relative error of at most 0.012.
Values may be sent and summed in bfloat16 or wider, within the bound.
No kernel may reach another device: no remote copies, remote signals or barrier semaphores. Data moves between devices by JAX's collectives and lax.ppermute only.
A program may use at most 128 MiB of HBM per device.

```python
import jax
import jax.numpy as jnp
from jax import lax

D = 768
INNER = 1536
KERNEL = 4
SPAN = 256
MB = 2
PART_TOK = 256
HEADS = 24
CONV_CH = 1792
PROJ = 3352
LEN = 1024
SEQS = 8


def draw_segment_ids(key, part):
    first_key, second_key = jax.random.split(jax.random.fold_in(key, 17))
    least = max(1, min(200, PART_TOK // 2))
    begin_one = jax.random.randint(first_key, (SEQS, MB, 1), least, PART_TOK)
    begin_two = LEN - jax.random.randint(second_key, (SEQS, MB, 1), least, PART_TOK)
    positions = jnp.arange(LEN, dtype=jnp.int32)[None, None, :]
    return (positions >= begin_one).astype(jnp.int32) + (positions >= begin_two).astype(jnp.int32)


def levels(own_key, dims, pieces, low, top_value):
    loudness, own = 1.0, jax.random.fold_in(own_key, 6)
    for position, shards_of in pieces:
        steps = jnp.exp(jax.random.uniform(jax.random.fold_in(own, position), (shards_of,), jnp.float32, low / len(pieces), top_value / len(pieces)))
        loudness = loudness * jnp.repeat(steps, dims[position] // shards_of).reshape([-1 if axis == position else 1 for axis in range(len(dims))])
    return loudness


def normal_values(rng, extent, scale, most, cuts=(), kind=jnp.bfloat16):
    gain = levels(rng, extent, cuts, -0.22, 0.18) if cuts else 1.0
    values = jax.random.normal(rng, extent, jnp.float32) * scale * gain
    return jnp.minimum(jnp.maximum(values, -most), most).astype(kind)


def setup_inputs(seed: int = 0) -> dict:
    streams_of = jax.random.split(jax.random.key(seed), 13)
    return {
        "layer_input": normal_values(streams_of[0], (SEQS, MB, LEN, D), 1.0, 6.0, ((0, 8), (2, 4))),
        "segment_ids": draw_segment_ids(jax.random.fold_in(streams_of[12], 71), 0),
        "gain_in": jnp.clip(1.0 + 0.1 * jax.random.normal(streams_of[2], (D,), jnp.float32), 0.5, 1.5).astype(jnp.bfloat16),
        "in_weight": normal_values(streams_of[3], (D, PROJ), D ** -0.5, 0.21875, ((0, 8),)),
        "conv_weight": normal_values(streams_of[4], (CONV_CH, KERNEL), KERNEL ** -0.5, 3.0, ((0, 8),)),
        "conv_bias": jnp.clip(jax.random.uniform(streams_of[5], (CONV_CH,), jnp.float32, -0.5, 0.5) * levels(streams_of[5], (CONV_CH,), ((0, 8),), -0.4, 0.0), -0.5, 0.5).astype(jnp.bfloat16),
        "dt_bias": jnp.clip(jax.random.uniform(streams_of[6], (HEADS,), jnp.float32, -7.0, -2.296875), -7.0, -2.296875).astype(jnp.bfloat16),
        "a_log": jnp.clip(jax.random.uniform(streams_of[7], (HEADS,), jnp.float32, 0.0, 2.765625), 0.0, 2.765625).astype(jnp.bfloat16),
        "skip_gain": jnp.clip(jax.random.uniform(streams_of[8], (HEADS,), jnp.float32, 0.5, 1.5), 0.5, 1.5).astype(jnp.bfloat16),
        "gain_out": jnp.clip(1.0 + 0.1 * jax.random.normal(streams_of[9], (INNER,), jnp.float32), 0.5, 1.5).astype(jnp.bfloat16),
        "out_weight": normal_values(streams_of[10], (INNER, D), INNER ** -0.5, 0.15625, ((0, 8),)),
        "cotangent": normal_values(streams_of[11], (SEQS, MB, LEN, D), 1.0, 6.0, ((0, 8), (2, 4))),
    }


EPS_NORM = 1e-05
HIGHEST_PRECISION = lax.Precision.HIGHEST

@jax.custom_vjp
def low(v):
    return lax.optimization_barrier(v.astype(jnp.bfloat16)).astype(jnp.float32)

@jax.custom_vjp
def low_back(v):
    return v

def low_keep(v):
    return (low(v), None)

def low_pass(kept, grad):
    return (grad,)

def back_keep(v):
    return (v, None)

def back_low(kept, grad):
    return (low(grad),)
low.defvjp(low_keep, low_pass)
low_back.defvjp(back_keep, back_low)

def front_norm(tokens_in, gain_vec):
    meansq = lax.optimization_barrier(jnp.mean(tokens_in * tokens_in, axis=-1, keepdims=True))
    return tokens_in * lax.rsqrt(meansq + EPS_NORM) * gain_vec

def gated_norm(mixed_rows, gating, gain_vec):
    gated = mixed_rows * jax.nn.silu(gating)
    meansq = lax.optimization_barrier(jnp.mean(gated * gated, axis=-1, keepdims=True))
    return gated * lax.rsqrt(meansq + EPS_NORM) * gain_vec

def causal_conv(values, kernel_w, bias_vec, seg_ids):
    length = values.shape[0]
    tap_count = kernel_w.shape[1]
    running = bias_vec[None, :] + kernel_w[:, tap_count - 1][None, :] * values
    for offset in range(1, tap_count):
        shifted = jnp.concatenate([jnp.zeros((offset, values.shape[1]), values.dtype), values[:length - offset]], 0)
        earlier = jnp.concatenate([jnp.full((offset,), -1, jnp.int32), seg_ids[:length - offset]], 0)
        keep_mask = (earlier == seg_ids).astype(values.dtype)
        running = running + kernel_w[:, tap_count - 1 - offset][None, :] * shifted * keep_mask[:, None]
    return running

def scan_blocks(x_heads, step_size, rates, b_mat, c_mat, seg_ids):
    length, head_count, head_width = x_heads.shape
    state_size = b_mat.shape[1]
    block_count = length // SPAN
    x_blocks = x_heads.reshape(block_count, SPAN, head_count, head_width)
    dt_blocks = step_size.reshape(block_count, SPAN, head_count)
    b_blocks = b_mat.reshape(block_count, SPAN, state_size)
    c_blocks = c_mat.reshape(block_count, SPAN, state_size)
    s_blocks = seg_ids.reshape(block_count, SPAN)
    rows_iota = lax.broadcasted_iota(jnp.int32, (SPAN, SPAN), 0)
    cols_iota = lax.broadcasted_iota(jnp.int32, (SPAN, SPAN), 1)

    def block_step(carry, item):
        carried_state, last_seg = carry
        x_blk, dt_blk, b_blk, c_blk, seg_blk = item
        logs = jnp.cumsum(dt_blk * rates[None, :], axis=0)
        inside = (rows_iota >= cols_iota) & (seg_blk[:, None] == seg_blk[None, :])
        logs_t = logs.T
        diffs = jnp.where(inside[None], logs_t[:, :, None] - logs_t[:, None, :], -jnp.inf)
        scores = jnp.dot(c_blk, b_blk.T, precision=HIGHEST_PRECISION)
        weights = scores[None] * jnp.exp(diffs) * dt_blk.T[:, None, :]
        y_inner = jnp.einsum('hij,jhp->ihp', weights, x_blk, precision=HIGHEST_PRECISION)
        carried = (seg_blk == last_seg).astype(jnp.float32)
        y_outer = jnp.einsum('in,hpn->ihp', c_blk, carried_state, precision=HIGHEST_PRECISION)
        y_outer = y_outer * (jnp.exp(logs) * carried[:, None])[:, :, None]
        tail_w = jnp.exp(logs[-1][None, :] - logs) * dt_blk * (seg_blk == seg_blk[-1]).astype(jnp.float32)[:, None]
        fresh = jnp.einsum('jh,jhp,jn->hpn', tail_w, x_blk, b_blk, precision=HIGHEST_PRECISION)
        keep_flag = (seg_blk[-1] == last_seg).astype(jnp.float32)
        new_state = fresh + (jnp.exp(logs[-1]) * keep_flag)[:, None, None] * carried_state
        return ((new_state, seg_blk[-1]), y_inner + y_outer)
    start_state = jnp.zeros((head_count, head_width, state_size), jnp.float32)
    carry_out, y_blocks = lax.scan(jax.checkpoint(block_step), (start_state, jnp.int32(-1)), (x_blocks, dt_blocks, b_blocks, c_blocks, s_blocks))
    return y_blocks.reshape(length, head_count, head_width)

def mixer_heads(seg_ids, x_pre, bc_pre, dt_raw, conv_wx, conv_bx, conv_wbc, conv_bbc, dt_bias, a_log, skip_gain):
    x_act = jax.nn.silu(causal_conv(x_pre, conv_wx, conv_bx, seg_ids))
    bc_act = jax.nn.silu(causal_conv(bc_pre, conv_wbc, conv_bbc, seg_ids))
    state_size = bc_pre.shape[1] // 2
    head_count = dt_raw.shape[1]
    x_heads = x_act.reshape(x_act.shape[0], head_count, x_act.shape[1] // head_count)
    step_size = jax.nn.softplus(dt_raw + dt_bias[None, :])
    rates = -jnp.exp(a_log)
    scanned = scan_blocks(x_heads, step_size, rates, bc_act[:, :state_size], bc_act[:, state_size:], seg_ids)
    return scanned + skip_gain[None, :, None] * x_heads

def mamba_layer(seg_ids, tokens_in, gain_vec, in_mat, conv_w, conv_b, dt_bias, a_log, skip_gain, gain_back, out_mat):
    normed = low(front_norm(tokens_in, gain_vec))
    projected = low_back(jnp.dot(normed, in_mat, precision=HIGHEST_PRECISION))
    gating = projected[:, :INNER]
    conv_in = low(projected[:, INNER:INNER + CONV_CH])
    dt_raw = low(projected[:, INNER + CONV_CH:])
    mixed = mixer_heads(seg_ids, conv_in[:, :INNER], conv_in[:, INNER:], dt_raw, conv_w[:INNER], conv_b[:INNER], conv_w[INNER:], conv_b[INNER:], dt_bias, a_log, skip_gain)
    mixed = low_back(low(mixed.reshape(tokens_in.shape[0], INNER)))
    out_normed = low(gated_norm(mixed, gating, gain_back))
    return tokens_in + jnp.dot(out_normed, out_mat, precision=HIGHEST_PRECISION)

def reference(layer_input, segment_ids, gain_in, in_weight, conv_weight, conv_bias, dt_bias, a_log, skip_gain, gain_out, out_weight, cotangent):
    params = (gain_in.astype(jnp.float32), in_weight.astype(jnp.float32), conv_weight.astype(jnp.float32), conv_bias.astype(jnp.float32), dt_bias.astype(jnp.float32), a_log.astype(jnp.float32), skip_gain.astype(jnp.float32), gain_out.astype(jnp.float32), out_weight.astype(jnp.float32))
    inputs_all = layer_input.reshape(SEQS * MB, LEN, D).astype(jnp.float32)
    segs_all = segment_ids.reshape(SEQS * MB, LEN)
    cots_all = cotangent.reshape(SEQS * MB, LEN, D).astype(jnp.float32)

    def one_sequence(totals, item):
        tokens_in, seg_ids, cot_rows = item

        def layer_call(tok_val, p_gain, p_in, p_cw, p_cb, p_dtb, p_alog, p_skip, p_gout, p_out):
            return mamba_layer(seg_ids, tok_val, p_gain, p_in, p_cw, p_cb, p_dtb, p_alog, p_skip, p_gout, p_out)
        result, pullback = jax.vjp(layer_call, tokens_in, params[0], params[1], params[2], params[3], params[4], params[5], params[6], params[7], params[8])
        grads = pullback(cot_rows)
        new_totals = tuple((before + added for before, added in zip(totals, grads[1:])))
        return (new_totals, (result.astype(jnp.bfloat16), grads[0]))
    start_totals = tuple((jnp.zeros_like(param_val) for param_val in params))
    totals, stacked = lax.scan(one_sequence, start_totals, (inputs_all, segs_all, cots_all))
    outputs_all = stacked[0].reshape(SEQS, MB, LEN, D)
    input_grads = stacked[1].reshape(SEQS, MB, LEN, D)
    return (outputs_all, input_grads, totals[0], totals[1], totals[2], totals[3], totals[4], totals[5], totals[6], totals[7], totals[8])
```

```python
from functools import partial

import jax
import jax.numpy as jnp
from jax import lax
from jax.sharding import PartitionSpec as P

INNER = 1536
HEADDIM = 64
SPAN = 256


EPS_NORM = 1e-05
HIGHEST_PRECISION = lax.Precision.HIGHEST


def front_norm(tokens_in, gain_vec):
    meansq = jnp.mean(tokens_in * tokens_in, axis=-1, keepdims=True)
    return tokens_in * lax.rsqrt(meansq + EPS_NORM) * gain_vec


def gated_norm(mixed_rows, gating, gain_vec):
    gated = mixed_rows * jax.nn.silu(gating)
    meansq = jnp.mean(gated * gated, axis=-1, keepdims=True)
    return gated * lax.rsqrt(meansq + EPS_NORM) * gain_vec


def causal_conv(values, kernel_w, bias_vec, seg_ids):
    length = values.shape[0]
    tap_count = kernel_w.shape[1]
    running = bias_vec[None, :] + kernel_w[:, tap_count - 1][None, :] * values
    for offset in range(1, tap_count):
        shifted = jnp.concatenate(
            [jnp.zeros((offset, values.shape[1]), values.dtype), values[: length - offset]], 0
        )
        earlier = jnp.concatenate(
            [jnp.full((offset,), -1, jnp.int32), seg_ids[: length - offset]], 0
        )
        keep_mask = (earlier == seg_ids).astype(values.dtype)
        running = (
            running + kernel_w[:, tap_count - 1 - offset][None, :] * shifted * keep_mask[:, None]
        )
    return running


def scan_blocks(x_heads, step_size, rates, b_mat, c_mat, seg_ids):
    length, head_count, head_width = x_heads.shape
    state_size = b_mat.shape[1]
    block_count = length // SPAN
    x_blocks = x_heads.reshape(block_count, SPAN, head_count, head_width)
    dt_blocks = step_size.reshape(block_count, SPAN, head_count)
    b_blocks = b_mat.reshape(block_count, SPAN, state_size)
    c_blocks = c_mat.reshape(block_count, SPAN, state_size)
    s_blocks = seg_ids.reshape(block_count, SPAN)
    rows_iota = lax.broadcasted_iota(jnp.int32, (SPAN, SPAN), 0)
    cols_iota = lax.broadcasted_iota(jnp.int32, (SPAN, SPAN), 1)

    def block_step(carry, item):
        carried_state, last_seg = carry
        x_blk, dt_blk, b_blk, c_blk, seg_blk = item
        logs = jnp.dot(
            (rows_iota >= cols_iota).astype(jnp.float32),
            dt_blk * rates[None, :],
            precision=HIGHEST_PRECISION,
        )
        inside = (rows_iota >= cols_iota) & (seg_blk[:, None] == seg_blk[None, :])
        logs_t = logs.T
        diffs = jnp.where(inside[None], logs_t[:, :, None] - logs_t[:, None, :], -jnp.inf)
        scores = jnp.dot(c_blk, b_blk.T, precision=HIGHEST_PRECISION)
        weights = scores[None] * jnp.exp(diffs) * dt_blk.T[:, None, :]
        y_inner = jnp.einsum("hij,jhp->ihp", weights, x_blk, precision=HIGHEST_PRECISION)
        carried = (seg_blk == last_seg).astype(jnp.float32)
        y_outer = jnp.einsum("in,hpn->ihp", c_blk, carried_state, precision=HIGHEST_PRECISION)
        y_outer = y_outer * (jnp.exp(logs) * carried[:, None])[:, :, None]
        tail_w = (
            jnp.exp(logs[-1][None, :] - logs)
            * dt_blk
            * (seg_blk == seg_blk[-1]).astype(jnp.float32)[:, None]
        )
        fresh = jnp.einsum("jh,jhp,jn->hpn", tail_w, x_blk, b_blk, precision=HIGHEST_PRECISION)
        keep_flag = (seg_blk[-1] == last_seg).astype(jnp.float32)
        new_state = fresh + (jnp.exp(logs[-1]) * keep_flag)[:, None, None] * carried_state
        return ((new_state, seg_blk[-1]), y_inner + y_outer)

    start_state = jnp.zeros((head_count, head_width, state_size), jnp.float32)
    carry_out, y_blocks = lax.scan(
        jax.checkpoint(block_step),
        (start_state, jnp.int32(-1)),
        (x_blocks, dt_blocks, b_blocks, c_blocks, s_blocks),
    )
    return y_blocks.reshape(length, head_count, head_width)


def mixer_heads(
    seg_ids, x_pre, bc_pre, dt_raw, conv_wx, conv_bx, conv_wbc, conv_bbc, dt_bias, a_log, skip_gain
):
    x_act = jax.nn.silu(causal_conv(x_pre, conv_wx, conv_bx, seg_ids))
    bc_act = jax.nn.silu(causal_conv(bc_pre, conv_wbc, conv_bbc, seg_ids))
    state_size = bc_pre.shape[1] // 2
    head_count = dt_raw.shape[1]
    x_heads = x_act.reshape(x_act.shape[0], head_count, x_act.shape[1] // head_count)
    step_size = jax.nn.softplus(dt_raw + dt_bias[None, :])
    rates = -jnp.exp(a_log)
    scanned = scan_blocks(
        x_heads, step_size, rates, bc_act[:, :state_size], bc_act[:, state_size:], seg_ids
    )
    return scanned + skip_gain[None, :, None] * x_heads


def on_device(
    layer_input,
    segment_ids,
    gain_in,
    in_weight,
    conv_weight,
    conv_bias,
    dt_bias,
    a_log,
    skip_gain,
    gain_out,
    out_weight,
    cotangent,
):
    gain_whole, in_whole = (
        lax.all_gather(gain_in, "fsdp", axis=0, tiled=True),
        lax.all_gather(in_weight, "fsdp", axis=0, tiled=True),
    )
    convw_whole, convb_whole, gout_whole, out_whole = (
        lax.all_gather(conv_weight, "fsdp", axis=0, tiled=True),
        lax.all_gather(conv_bias, "fsdp", axis=0, tiled=True),
        lax.all_gather(gain_out, "fsdp", axis=0, tiled=True),
        lax.all_gather(out_weight, "fsdp", axis=0, tiled=True),
    )
    micro_count = layer_input.shape[1]
    part_len = layer_input.shape[2]
    head_count = dt_bias.shape[0]
    conv_chans = convw_whole.shape[0]
    tap_count = convw_whole.shape[1]
    local_heads = head_count // lax.axis_size("seq")
    head_start = lax.axis_index("seq") * local_heads
    chan_start = head_start * HEADDIM
    local_chans = local_heads * HEADDIM
    gain_front = gain_whole.astype(jnp.float32)
    gain_back = gout_whole.astype(jnp.float32)
    convw_float = convw_whole.astype(jnp.float32)
    convb_float = convb_whole.astype(jnp.float32)
    params_local = (
        lax.dynamic_slice_in_dim(convw_float, chan_start, local_chans, 0),
        lax.dynamic_slice_in_dim(convb_float, chan_start, local_chans, 0),
        convw_float[INNER:],
        convb_float[INNER:],
        lax.dynamic_slice_in_dim(dt_bias.astype(jnp.float32), head_start, local_heads, 0),
        lax.dynamic_slice_in_dim(a_log.astype(jnp.float32), head_start, local_heads, 0),
        lax.dynamic_slice_in_dim(skip_gain.astype(jnp.float32), head_start, local_heads, 0),
    )
    grad_front_gain = jnp.zeros_like(gain_front)
    grad_in_mat = jnp.zeros(in_whole.shape, jnp.float32)
    grad_back_gain = jnp.zeros_like(gain_back)
    grad_out_mat = jnp.zeros(out_whole.shape, jnp.float32)
    grad_local = tuple((jnp.zeros_like(param_val) for param_val in params_local))
    outputs_list = []
    input_grads = []
    for micro_idx in range(micro_count):
        tokens_in = layer_input[0, micro_idx].astype(jnp.float32)
        seg_ids = segment_ids[0, micro_idx]
        normed_float, front_pull = jax.vjp(front_norm, tokens_in, gain_front)
        normed = normed_float.astype(jnp.bfloat16)
        projected = jnp.dot(normed, in_whole, preferred_element_type=jnp.float32)
        gating = projected[:, :INNER]
        x_send = (
            projected[:, INNER : 2 * INNER]
            .astype(jnp.bfloat16)
            .reshape(part_len, head_count, HEADDIM)
        )
        bc_send = projected[:, 2 * INNER : INNER + conv_chans].astype(jnp.bfloat16)
        dt_send = projected[:, INNER + conv_chans :].astype(jnp.bfloat16)
        bc_whole = lax.all_gather(bc_send, "seq", axis=0, tiled=True)
        x_group, dt_group = (
            lax.all_to_all(x_send, "seq", split_axis=1, concat_axis=0, tiled=True),
            lax.all_to_all(dt_send, "seq", split_axis=1, concat_axis=0, tiled=True),
        )
        seq_len = x_group.shape[0]
        mixed_float, mixer_pull = jax.vjp(
            partial(mixer_heads, seg_ids),
            x_group.reshape(seq_len, local_chans).astype(jnp.float32),
            bc_whole.astype(jnp.float32),
            dt_group.astype(jnp.float32),
            params_local[0],
            params_local[1],
            params_local[2],
            params_local[3],
            params_local[4],
            params_local[5],
            params_local[6],
        )
        mixed_tokens = lax.all_to_all(
            mixed_float.astype(jnp.bfloat16), "seq", split_axis=0, concat_axis=1, tiled=True
        )
        mixed_rows = mixed_tokens.reshape(part_len, INNER).astype(jnp.float32)
        outnorm_float, back_pull = jax.vjp(gated_norm, mixed_rows, gating, gain_back)
        out_normed = outnorm_float.astype(jnp.bfloat16)
        result = tokens_in + jnp.dot(out_normed, out_whole, preferred_element_type=jnp.float32)
        outputs_list.append(result.astype(jnp.bfloat16))
        cot_rows = cotangent[0, micro_idx]
        grad_out_mat = grad_out_mat + jnp.dot(
            out_normed.T, cot_rows, preferred_element_type=jnp.float32
        )
        grad_outnorm = jnp.dot(cot_rows, out_whole.T, preferred_element_type=jnp.float32)
        grad_mixed, grad_gating, grad_gainback = back_pull(grad_outnorm)
        grad_back_gain = grad_back_gain + grad_gainback
        grad_group = lax.all_to_all(
            grad_mixed.astype(jnp.bfloat16).reshape(part_len, head_count, HEADDIM),
            "seq",
            split_axis=1,
            concat_axis=0,
            tiled=True,
        )
        mixer_grads = mixer_pull(grad_group.astype(jnp.float32))
        grad_local = tuple((before + added for before, added in zip(grad_local, mixer_grads[3:])))
        grad_xtok, grad_dttok = (
            lax.all_to_all(
                mixer_grads[0].astype(jnp.bfloat16).reshape(seq_len, local_heads, HEADDIM),
                "seq",
                split_axis=0,
                concat_axis=1,
                tiled=True,
            ),
            lax.all_to_all(
                mixer_grads[2].astype(jnp.bfloat16), "seq", split_axis=0, concat_axis=1, tiled=True
            ),
        )
        grad_bctok = lax.psum_scatter(
            mixer_grads[1].astype(jnp.bfloat16), "seq", scatter_dimension=0, tiled=True
        )
        grad_proj = jnp.concatenate(
            [
                grad_gating.astype(jnp.bfloat16),
                grad_xtok.reshape(part_len, INNER),
                grad_bctok,
                grad_dttok,
            ],
            axis=1,
        )
        grad_in_mat = grad_in_mat + jnp.dot(normed.T, grad_proj, preferred_element_type=jnp.float32)
        grad_normed = jnp.dot(grad_proj, in_whole.T, preferred_element_type=jnp.float32)
        grad_tokens, grad_gainfront = front_pull(grad_normed)
        grad_front_gain = grad_front_gain + grad_gainfront
        input_grads.append(cot_rows.astype(jnp.float32) + grad_tokens)
    layer_output = jnp.stack(outputs_list, 0)[None]
    input_grad = jnp.stack(input_grads, 0)[None]
    grad_convw = jnp.concatenate(
        [
            lax.dynamic_update_slice_in_dim(
                jnp.zeros((INNER, tap_count), jnp.float32), grad_local[0], chan_start, 0
            ),
            grad_local[2],
        ],
        0,
    )
    grad_convb = jnp.concatenate(
        [
            lax.dynamic_update_slice_in_dim(
                jnp.zeros((INNER,), jnp.float32), grad_local[1], chan_start, 0
            ),
            grad_local[3],
        ],
        0,
    )
    zero_heads = jnp.zeros((head_count,), jnp.float32)
    grad_dtb = lax.dynamic_update_slice_in_dim(zero_heads, grad_local[4], head_start, 0)
    grad_alog = lax.dynamic_update_slice_in_dim(zero_heads, grad_local[5], head_start, 0)
    grad_skip = lax.dynamic_update_slice_in_dim(zero_heads, grad_local[6], head_start, 0)
    partials = (
        lax.psum_scatter(grad_front_gain, "fsdp", scatter_dimension=0, tiled=True),
        lax.psum_scatter(grad_in_mat, "fsdp", scatter_dimension=0, tiled=True),
        lax.psum_scatter(grad_convw, "fsdp", scatter_dimension=0, tiled=True),
        lax.psum_scatter(grad_convb, "fsdp", scatter_dimension=0, tiled=True),
        lax.psum_scatter(grad_back_gain, "fsdp", scatter_dimension=0, tiled=True),
        lax.psum_scatter(grad_out_mat, "fsdp", scatter_dimension=0, tiled=True),
    )
    shares = lax.psum(
        (partials[0], partials[1], partials[2], partials[3], partials[4], partials[5]), "seq"
    )
    head_sums = lax.psum((grad_dtb, grad_alog, grad_skip), ("fsdp", "seq"))
    return (
        layer_output,
        input_grad,
        shares[0],
        shares[1],
        shares[2],
        shares[3],
        head_sums[0],
        head_sums[1],
        head_sums[2],
        shares[4],
        shares[5],
    )


def solution(mesh):
    placed = (
        P("fsdp", None, "seq", None),
        P("fsdp", None, None),
        P("fsdp"),
        P("fsdp", None),
        P("fsdp", None),
        P("fsdp"),
        P(),
        P(),
        P(),
        P("fsdp"),
        P("fsdp", None),
        P("fsdp", None, "seq", None),
    )
    return jax.shard_map(
        on_device,
        mesh=mesh,
        in_specs=placed,
        out_specs=(
            P("fsdp", None, "seq", None),
            P("fsdp", None, "seq", None),
            P("fsdp"),
            P("fsdp", None),
            P("fsdp", None),
            P("fsdp"),
            P(),
            P(),
            P(),
            P("fsdp"),
            P("fsdp", None),
        ),
        check_vma=False,
    )
```

```python
from functools import partial

import jax
import jax.numpy as jnp
from jax import lax
from jax.experimental import pallas as pl
from jax.experimental.pallas import tpu as pltpu
from jax.sharding import PartitionSpec as P

SPAN = 256
HEADDIM = 64
LANES = 128
HALO = 16
WIDE = 256
EPS_NORM = 1e-05
OFF = -10000.0
F32 = jnp.float32
BF16 = jnp.bfloat16


def nn(a, b):
    return lax.dot_general(a, b, (((1,), (0,)), ((), ())), preferred_element_type=F32)


def nt(a, b):
    return lax.dot_general(a, b, (((1,), (1,)), ((), ())), preferred_element_type=F32)


def tn(a, b):
    return lax.dot_general(a, b, (((0,), (0,)), ((), ())), preferred_element_type=F32)


def iota(shape, dim):
    return lax.broadcasted_iota(jnp.int32, shape, dim)


def ones_where(cond):
    return jnp.where(cond, 1.0, 0.0)


def split2(v):
    high = v.astype(BF16)
    low = (v - high.astype(F32)).astype(BF16)
    return jnp.concatenate([high, low], axis=1)


def spread_map(start, width):
    shape = (2 * LANES, width)
    return ones_where((iota(shape, 0) & (LANES - 1)) == ((iota(shape, 1) + start) >> 6)).astype(BF16)


def gather_map(start, width):
    shape = (width, LANES)
    return ones_where(((iota(shape, 0) + start) >> 6) == iota(shape, 1)).astype(BF16)


def to_heads(v, start):
    high = v.astype(BF16)
    rest = v - high.astype(F32)
    mid = rest.astype(BF16)
    picks = gather_map(start, v.shape[1])
    return nn(high, picks) + nn(mid, picks)


def running_sum(tri, v):
    high = v.astype(BF16)
    rest = v - high.astype(F32)
    mid = rest.astype(BF16)
    low = (rest - mid.astype(F32)).astype(BF16)
    return nn(tri, high) + nn(tri, mid) + nn(tri, low)


def silu_slope(v, sig):
    return sig * (1.0 + v * (1.0 - sig))


def softplus(v):
    return jnp.maximum(v, 0.0) + jnp.log1p(jnp.exp(-jnp.abs(v)))


def row_masks(seg_ref, taps):
    here = seg_ref[pl.ds(HALO, SPAN), :]
    return [ones_where(seg_ref[pl.ds(HALO - j, SPAN), :] == here) for j in range(1, taps)]


def conv_pre(ext_ref, cols, convw_ref, masks):
    taps = len(masks) + 1
    total = convw_ref[taps : taps + 1, cols] + convw_ref[taps - 1 : taps, cols] * ext_ref[pl.ds(HALO, SPAN), :]
    for j in range(1, taps):
        total = total + convw_ref[taps - 1 - j : taps - j, cols] * (
            ext_ref[pl.ds(HALO - j, SPAN), :] * masks[j - 1]
        )
    return total


def vmem_call(body, out_shape, n_smem=0, n_in=0, scratch=(), mib=40, flops=0, moved=0, trans=0):
    vm = pl.BlockSpec(memory_space=pltpu.VMEM)
    sm = pl.BlockSpec(memory_space=pltpu.SMEM)
    return pl.pallas_call(
        body,
        out_shape=out_shape,
        in_specs=[sm] * n_smem + [vm] * n_in,
        out_specs=jax.tree.map(lambda _: vm, out_shape),
        scratch_shapes=list(scratch),
        compiler_params=pltpu.CompilerParams(vmem_limit_bytes=mib * 1024 * 1024),
        cost_estimate=pl.CostEstimate(flops=flops, bytes_accessed=moved, transcendentals=trans),
    )


def sds(shape, dtype):
    return jax.ShapeDtypeStruct(shape, dtype)


def norm_body(x_ref, halo_ref, gain_ref, out_ref):
    main = x_ref.shape[0]
    for ref, first in ((x_ref, 0), (halo_ref, main)):
        v = ref[...].astype(F32)
        scale = lax.rsqrt(jnp.mean(v * v, axis=1, keepdims=True) + EPS_NORM)
        out_ref[pl.ds(first, ref.shape[0]), :] = (v * scale * gain_ref[...]).astype(BF16)


def place(idx, piece_refs, layout, chunk, dst):
    for ref, (k, off) in zip(piece_refs, layout):
        first = (idx ^ k) * chunk + off
        dst(first, off, ref)


def proj_body(layout, batch, inner, state, *refs):
    idx_ref, normed_ref, convw_ref, heads_ref, seg_ref = refs[:5]
    pieces = refs[5 : 5 + len(layout)]
    (w_ref, convin_ref, dtraw_ref, x_ref, bc_ref, xdt_ref, dt_ref, s_ref, st_ref, fresh_ref, send_ref, decay_ref) = refs[
        5 + len(layout) : 17 + len(layout)
    ]
    ext_ref, tail_ref = refs[17 + len(layout) :]
    chunk = w_ref.shape[0] // (1 if len(layout) == 1 else 8)
    for ref, (k, off) in zip(pieces, layout):
        rows = ref.shape[0]
        first = pl.multiple_of((idx_ref[0] ^ k) * chunk + off, HALO)
        w_ref[pl.ds(first, rows), :] = ref[...]
    conv_chans = inner + 2 * state
    taps = 4
    normed = normed_ref[...]
    raw = nn(normed, w_ref[:, conv_chans : conv_chans + LANES])
    tri = ones_where(iota((SPAN, SPAN), 0) >= iota((SPAN, SPAN), 1)).astype(BF16)
    all_masks = []
    for b in range(batch):
        seg = seg_ref.at[b]
        all_masks.append(row_masks(seg, taps))
        dt_raw = raw[b * SPAN : (b + 1) * SPAN].astype(BF16).astype(F32)
        dtraw_ref[b] = dt_raw
        dt = softplus(dt_raw + heads_ref[0:1, :])
        dt_ref[b] = dt
        rate = -jnp.exp(heads_ref[1:2, :])
        logs = running_sum(tri, dt * rate)
        s_ref[b] = logs
        st_ref[b] = logs.T
        last = logs[SPAN - 1 : SPAN, :]
        same_last = ones_where(seg[pl.ds(HALO, SPAN), :] == seg[HALO + SPAN - 1 : HALO + SPAN, :])
        tail_ref[b] = split2(jnp.exp(last - logs) * same_last)
        keep = ones_where(seg[HALO + SPAN - 1 : HALO + SPAN, :] == seg[HALO - 1 : HALO, :])
        factor = jnp.broadcast_to(jnp.exp(last) * keep, (8, LANES))
        for c0 in range(0, inner, WIDE):
            decay_ref[b, :, c0 : c0 + WIDE] = nn(split2(factor), spread_map(c0, WIDE))
    for c0 in [inner] + list(range(0, inner, WIDE)):
        cols = slice(c0, c0 + WIDE)
        projected = nn(normed, w_ref[:, cols]).astype(BF16)
        for b in range(batch):
            halo0 = batch * SPAN + b * HALO
            top = projected[halo0 : halo0 + HALO]
            rest = projected[b * SPAN : (b + 1) * SPAN]
            convin_ref[b, 0:HALO, cols] = top
            convin_ref[b, HALO : HALO + SPAN, cols] = rest
            ext_ref[0:HALO, :] = top.astype(F32)
            ext_ref[HALO : HALO + SPAN, :] = rest.astype(F32)
            pre = conv_pre(ext_ref, cols, convw_ref, all_masks[b])
            act = pre * jax.nn.sigmoid(pre)
            if c0 == inner:
                bc_ref[b] = act.astype(BF16)
            else:
                spread = spread_map(c0, WIDE)
                x_ref[b, :, cols] = act
                xdt = (nn(split2(dt_ref[b]), spread) * act).astype(BF16)
                xdt_ref[b, :, cols] = xdt
                xt = (nn(tail_ref[b], spread) * xdt.astype(F32)).astype(BF16)
                fresh = tn(bc_ref[b, :, 0:state], xt)
                fresh_ref[b, :, cols] = fresh
                send_ref[b, :, cols] = fresh.astype(BF16)


def inside_mask(seg_ref, segr_ref):
    rows, cols = iota((SPAN, SPAN), 0), iota((SPAN, SPAN), 1)
    return (rows >= cols) & (seg_ref[pl.ds(HALO, SPAN), :] == segr_ref[...])


def inside_mask_t(seg_ref, segr_ref):
    rows, cols = iota((SPAN, SPAN), 0), iota((SPAN, SPAN), 1)
    return (rows <= cols) & (seg_ref[pl.ds(HALO, SPAN), :] == segr_ref[...])


def head_halves(block):
    low = iota(block.shape, 1) < HEADDIM
    zero = jnp.zeros_like(block)
    return jnp.where(low, block, zero), jnp.where(low, zero, block)


def intra_body(state, bc_ref, xdt_ref, s_ref, st_ref, seg_ref, segr_ref, y_ref):
    scores = nt(bc_ref[:, state : 2 * state], bc_ref[:, 0:state])
    scores = jnp.where(inside_mask(seg_ref, segr_ref), scores, 0.0)
    for pair in range(xdt_ref.shape[1] // LANES):
        cols = slice(pair * LANES, (pair + 1) * LANES)
        total = None
        for half, values in enumerate(head_halves(xdt_ref[:, cols])):
            h = 2 * pair + half
            decay = jnp.exp(jnp.minimum(s_ref[:, h : h + 1] - st_ref[h : h + 1, :], 0.0))
            part = nn((scores * decay).astype(BF16), values)
            total = part if total is None else total + part
        y_ref[:, cols] = total


def dense_body(layout, inner, *refs):
    idx_ref, normed_ref, cot_ref = refs[:3]
    pieces = refs[3 : 3 + len(layout)]
    wout_ref, wgate_ref, gating_ref, dout_ref = refs[3 + len(layout) :]
    depth = wgate_ref.shape[0]
    shards = 1 if len(layout) == 1 else 8
    ochunk, gchunk = inner // shards, depth // shards
    half_cols = inner // 2
    for ref, (k, off) in zip(pieces, layout):
        owner = idx_ref[0] ^ k
        size = ref.shape[0]
        for lo, hi, kind in ((0, ochunk, 0), (ochunk, ochunk + gchunk, 1), (ochunk + gchunk, ochunk + 2 * gchunk, 2)):
            a, z = max(lo, off), min(hi, off + size)
            if a >= z:
                continue
            value = ref[a - off : z - off, :]
            if kind == 0:
                wout_ref[pl.ds(pl.multiple_of(owner * ochunk + (a - lo), HALO), z - a), :] = value
            else:
                wgate_ref[
                    pl.ds(pl.multiple_of(owner * gchunk + (a - lo), HALO), z - a),
                    (kind - 1) * half_cols : kind * half_cols,
                ] = value
    normed = normed_ref[0 : cot_ref.shape[0], :]
    cot = cot_ref[...]
    for c0 in range(0, inner, WIDE):
        gating_ref[:, c0 : c0 + WIDE] = nn(normed, wgate_ref[:, c0 : c0 + WIDE])
        dout_ref[:, c0 : c0 + WIDE] = nt(cot, wout_ref[c0 : c0 + WIDE, :])


def gate_body(state, base, *refs):
    (yin_ref, carry_ref, bc_ref, s_ref, seg_ref, x_ref, gating_ref, dout_ref, gain_ref, heads_ref) = refs[:10]
    (outn_ref, dy_ref, ey_ref, dgat_ref, rowterm_ref, grad_ref, send_ref, small_ref) = refs[10:18]
    y_ref, gated_ref = refs[18:]
    inner = x_ref.shape[1]
    rows = pl.ds(base, SPAN)
    c_mat = bc_ref[:, state : 2 * state]
    carried = ones_where(seg_ref[pl.ds(HALO, SPAN), :] == seg_ref[HALO - 1 : HALO, :])
    factor = split2(jnp.exp(s_ref[...]) * carried)
    skip = split2(jnp.broadcast_to(heads_ref[2:3, :], (8, LANES)))
    sumsq = jnp.zeros((SPAN, 1), F32)
    sumeg = jnp.zeros((SPAN, 1), F32)
    for c0 in range(0, inner, WIDE):
        cols = slice(c0, c0 + WIDE)
        spread = spread_map(c0, WIDE)
        y = yin_ref[:, cols] + nn(factor, spread) * nn(c_mat, carry_ref[:, cols])
        y_ref[:, cols] = y
        mixed = (y + nn(skip, spread)[0:1, :] * x_ref[:, cols]).astype(BF16).astype(F32)
        gate = gating_ref[rows, cols]
        gated = mixed * (gate * jax.nn.sigmoid(gate))
        gated_ref[:, cols] = gated
        sumsq = sumsq + jnp.sum(gated * gated, axis=1, keepdims=True)
        sumeg = sumeg + jnp.sum(dout_ref[rows, cols] * gain_ref[:, cols] * gated, axis=1, keepdims=True)
    r = lax.rsqrt(sumsq / inner + EPS_NORM)
    coef = r * r * r * (sumeg / inner)
    terms = jnp.zeros((SPAN, LANES), F32)
    for c0 in range(0, inner, WIDE):
        cols = slice(c0, c0 + WIDE)
        spread = spread_map(c0, WIDE)
        gated = gated_ref[:, cols]
        gain = gain_ref[:, cols]
        dout = dout_ref[rows, cols]
        normal = gated * r
        outn_ref[:, cols] = (normal * gain).astype(BF16)
        y = y_ref[:, cols]
        x = x_ref[:, cols]
        d_gated = r * (dout * gain) - gated * coef
        gate = gating_ref[rows, cols]
        sig = jax.nn.sigmoid(gate)
        mixed = (y + nn(skip, spread)[0:1, :] * x).astype(BF16).astype(F32)
        dgat_ref[:, cols] = (d_gated * mixed * silu_slope(gate, sig)).astype(BF16)
        dy = (d_gated * (gate * sig)).astype(BF16)
        dy_ref[:, cols] = dy
        dyf = dy.astype(F32)
        ey = (nn(factor, spread) * dyf).astype(BF16)
        ey_ref[:, cols] = ey
        terms = terms + to_heads(dyf * y, c0)
        grad = tn(c_mat, ey)
        grad_ref[:, cols] = grad
        send_ref[:, cols] = grad.astype(BF16)
        small_ref[0:1, cols] = jnp.sum(dout * normal, axis=0, keepdims=True)
        small_ref[1:2, cols] = jnp.sum(dyf * x, axis=0, keepdims=True)
        small_ref[2:8, cols] = jnp.zeros((6, WIDE), F32)
    rowterm_ref[...] = terms


def intra_back_body(state, *refs):
    (bc_ref, xdt_ref, dy_ref, ey_ref, carry_ref, s_ref, st_ref, seg_ref, segr_ref) = refs[:9]
    dxdt_ref, dbc_ref = refs[9:11]
    acc_ref = refs[11]
    b_mat = bc_ref[:, 0:state]
    c_mat = bc_ref[:, state : 2 * state]
    mask = inside_mask_t(seg_ref, segr_ref)
    scores = jnp.where(mask, nt(b_mat, c_mat), 0.0)
    for pair in range(xdt_ref.shape[1] // LANES):
        cols = slice(pair * LANES, (pair + 1) * LANES)
        total = None
        dy_block = dy_ref[:, cols]
        for half, (values, grads) in enumerate(zip(head_halves(xdt_ref[:, cols]), head_halves(dy_block))):
            h = 2 * pair + half
            decay = jnp.exp(jnp.minimum(st_ref[h : h + 1, :] - s_ref[:, h : h + 1], 0.0))
            part = nn((scores * decay).astype(BF16), grads)
            total = part if total is None else total + part
            d_weight = nt(values, dy_block) * decay
            if h == 0:
                acc_ref[...] = d_weight
            else:
                acc_ref[...] += d_weight
        dxdt_ref[:, cols] = total
    d_scores = jnp.where(mask, acc_ref[...], 0.0).astype(BF16)
    dbc_ref[:, 0:state] = nn(d_scores, c_mat)
    dbc_ref[:, state : 2 * state] = tn(d_scores, b_mat) + nt(ey_ref[...], carry_ref[...])


def mixer_back_body(state, *refs):
    (convin_ref, dtraw_ref, x_ref, bc_ref, xdt_ref, dt_ref, s_ref, seg_ref, convw_ref, heads_ref) = refs[:10]
    (dxdt_ref, dbc_ref, dy_ref, rowterm_ref, carry_ref, dcarry_ref) = refs[10:16]
    (dmain_ref, dhalo_ref, small_ref, hsmall_ref) = refs[16:20]
    ext_ref, dpre_ref, dconv_ref = refs[20:]
    inner = x_ref.shape[1]
    taps = 4
    conv_chans = inner + 2 * state
    masks = row_masks(seg_ref, taps)
    b_mat = bc_ref[:, 0:state]
    logs = s_ref[...]
    dt = dt_ref[...]
    rate = -jnp.exp(heads_ref[1:2, :])
    last = logs[SPAN - 1 : SPAN, :]
    same_last = ones_where(seg_ref[pl.ds(HALO, SPAN), :] == seg_ref[HALO + SPAN - 1 : HALO + SPAN, :])
    keep = ones_where(seg_ref[HALO + SPAN - 1 : HALO + SPAN, :] == seg_ref[HALO - 1 : HALO, :])
    tail = split2(jnp.exp(last - logs) * same_last)
    dt2 = split2(dt)
    skip = split2(jnp.broadcast_to(heads_ref[2:3, :], (8, LANES)))
    col_term = jnp.zeros((SPAN, LANES), F32)
    direct = jnp.zeros((SPAN, LANES), F32)
    last_term = jnp.zeros((8, LANES), F32)
    d_b = dbc_ref[:, 0:state]
    dconv_ref[HALO + SPAN : HALO + SPAN + HALO, :] = jnp.zeros((HALO, WIDE), F32)
    dpre_ref[0:HALO, :] = jnp.zeros((HALO, WIDE), F32)
    dpre_ref[HALO + SPAN : HALO + SPAN + HALO, :] = jnp.zeros((HALO, WIDE), F32)
    small_ref[taps + 1 : 8, :] = jnp.zeros((7 - taps, conv_chans), F32)

    def conv_back(cols, d_act):
        ext_ref[...] = convin_ref[:, cols].astype(F32)
        pre = conv_pre(ext_ref, cols, convw_ref, masks)
        d_pre = d_act * silu_slope(pre, jax.nn.sigmoid(pre))
        small_ref[taps : taps + 1, cols] = jnp.sum(d_pre, axis=0, keepdims=True)
        small_ref[taps - 1 : taps, cols] = jnp.sum(d_pre * ext_ref[pl.ds(HALO, SPAN), :], axis=0, keepdims=True)
        dpre_ref[pl.ds(HALO, SPAN), :] = d_pre
        total = convw_ref[taps - 1 : taps, cols] * dpre_ref[pl.ds(0, HALO + SPAN), :]
        for j in range(1, taps):
            masked = d_pre * masks[j - 1]
            small_ref[taps - 1 - j : taps - j, cols] = jnp.sum(
                masked * ext_ref[pl.ds(HALO - j, SPAN), :], axis=0, keepdims=True
            )
            dconv_ref[pl.ds(0, HALO), :] = jnp.zeros((HALO, WIDE), F32)
            dconv_ref[pl.ds(HALO, SPAN), :] = masked
            total = total + convw_ref[taps - 1 - j : taps - j, cols] * dconv_ref[pl.ds(j, HALO + SPAN), :]
        total = total.astype(BF16)
        dhalo_ref[:, cols] = total[0:HALO]
        dmain_ref[:, cols] = total[HALO : HALO + SPAN]

    for c0 in range(0, inner, WIDE):
        cols = slice(c0, c0 + WIDE)
        spread = spread_map(c0, WIDE)
        d_carry = dcarry_ref[:, cols]
        tails = nn(tail, spread)
        xdt = xdt_ref[:, cols].astype(F32)
        d_tail = tails * nn(b_mat, d_carry)
        d_xdt = dxdt_ref[:, cols] + d_tail
        x = x_ref[:, cols]
        col_term = col_term + to_heads(xdt * d_xdt, c0)
        direct = direct + to_heads(x * d_xdt, c0)
        from_tail = jnp.sum(xdt * d_tail, axis=0, keepdims=True)
        through = jnp.sum(d_carry.astype(F32) * carry_ref[:, cols].astype(F32), axis=0, keepdims=True)
        both = to_heads(jnp.concatenate([from_tail, through, jnp.zeros((6, WIDE), F32)], axis=0), c0)
        last_term = last_term + both
        d_b = d_b + nt((tails * xdt).astype(BF16), d_carry)
        d_x = nn(dt2, spread) * d_xdt + nn(skip, spread)[0:1, :] * dy_ref[:, cols].astype(F32)
        conv_back(cols, d_x)
    conv_back(slice(inner, conv_chans), jnp.concatenate([d_b, dbc_ref[:, state : 2 * state]], axis=1))
    at_end = last_term[0:1, :] + last_term[1:2, :] * (jnp.exp(last) * keep)
    upper = ones_where(iota((SPAN, SPAN), 0) <= iota((SPAN, SPAN), 1)).astype(BF16)
    d_logs = running_sum(upper, rowterm_ref[...] - col_term) + at_end
    d_dt = direct + rate * d_logs
    d_raw = d_dt * jax.nn.sigmoid(dtraw_ref[...] + heads_ref[0:1, :])
    dmain_ref[:, conv_chans : conv_chans + LANES] = d_raw.astype(BF16)
    dhalo_ref[:, conv_chans : conv_chans + LANES] = jnp.zeros((HALO, LANES), BF16)
    hsmall_ref[0:1, :] = jnp.sum(d_raw, axis=0, keepdims=True)
    hsmall_ref[1:2, :] = jnp.sum(dt * d_logs, axis=0, keepdims=True) * rate
    hsmall_ref[2:8, :] = jnp.zeros((6, LANES), F32)


def out_body(shards, *refs):
    (idx_ref, on0_ref, on1_ref, cot_ref, xin_ref, wout_ref, dg0_ref, dg1_ref, normed_ref, wgate_ref) = refs[:10]
    outs = refs[10:-2]
    even_ref, odd_ref = (outs[0], outs[1]) if shards > 1 else (outs[0], None)
    lout_ref, dng_ref = outs[-2:]
    gout_ref, ggate_ref = refs[-2:]
    main = cot_ref.shape[0]
    inner, width = wout_ref.shape
    outn = jnp.concatenate([on0_ref[...], on1_ref[...]], axis=0)
    dgat = jnp.concatenate([dg0_ref[...], dg1_ref[...]], axis=0)
    cot = cot_ref[...]
    normed = normed_ref[0:main, :]
    gout_ref[...] = tn(outn, cot)
    for c0 in range(0, inner, width):
        ggate_ref[:, c0 : c0 + width] = tn(normed, dgat[:, c0 : c0 + width])
    ochunk, gchunk = inner // shards, width // shards
    for k in range(shards):
        owner = idx_ref[0] ^ k
        ref, slot = (even_ref, k // 2) if k % 2 == 0 else (odd_ref, k // 2)
        ref[slot, 0:ochunk, :] = gout_ref[pl.ds(pl.multiple_of(owner * ochunk, HALO), ochunk), :].astype(BF16)
        for side in range(2):
            ref[slot, ochunk + side * gchunk : ochunk + (side + 1) * gchunk, :] = ggate_ref[
                pl.ds(pl.multiple_of(owner * gchunk, HALO), gchunk), side * width : (side + 1) * width
            ].astype(BF16)
    lout_ref[...] = (xin_ref[...].astype(F32) + nn(outn, wout_ref[...])).astype(BF16)
    dng_ref[...] = nt(dgat, wgate_ref[...])


def join_rows(m0_ref, m1_ref, h0_ref, h1_ref, all_ref):
    all_ref[0:SPAN, :] = m0_ref[...]
    all_ref[SPAN : 2 * SPAN, :] = m1_ref[...]
    all_ref[2 * SPAN : 2 * SPAN + HALO, :] = h0_ref[...]
    all_ref[2 * SPAN + HALO : 2 * SPAN + 2 * HALO, :] = h1_ref[...]


def in_grad_body(shards, *refs):
    idx_ref, m0_ref, m1_ref, h0_ref, h1_ref, normed_ref = refs[:6]
    outs = refs[6:-2]
    all_ref, grad_ref = refs[-2:]
    join_rows(m0_ref, m1_ref, h0_ref, h1_ref, all_ref)
    depth, width = grad_ref.shape
    for c0 in range(0, width, 384):
        grad_ref[:, c0 : c0 + 384] = tn(normed_ref[...], all_ref[:, c0 : c0 + 384])
    chunk = depth // shards
    for k in range(shards):
        first = pl.multiple_of((idx_ref[0] ^ k) * chunk, HALO)
        outs[k % 2][k // 2] = grad_ref[pl.ds(first, chunk), :].astype(BF16)


def in_back_body(m0_ref, m1_ref, h0_ref, h1_ref, w_ref, dng_ref, cot_ref, xin_ref, halo_ref, gain_ref, *outs):
    igrad_ref, hgrad_ref, ggain_ref, all_ref = outs
    main = cot_ref.shape[0]
    join_rows(m0_ref, m1_ref, h0_ref, h1_ref, all_ref)
    d_normed = nt(all_ref[...], w_ref[...])
    gain = gain_ref[...]

    def back(dn, v):
        q = lax.rsqrt(jnp.mean(v * v, axis=1, keepdims=True) + EPS_NORM)
        e = dn * gain
        back_x = q * e - v * (q * q * q * jnp.mean(e * v, axis=1, keepdims=True))
        return back_x, jnp.sum(dn * v * q, axis=0, keepdims=True)

    g_main, gg_main = back(d_normed[0:main] + dng_ref[...], xin_ref[...].astype(F32))
    g_halo, gg_halo = back(d_normed[main:], halo_ref[...].astype(F32))
    igrad_ref[...] = cot_ref[...].astype(F32) + g_main
    hgrad_ref[...] = g_halo
    ggain_ref[...] = gg_main + gg_halo


def xor_pairs(size, k):
    return [(i, i ^ k) for i in range(size)]


def gather_layout(rows, shards):
    return shards == 8 and rows % (2 * HALO) == 0


def gather_pieces(shard):
    swap = lambda v, k: lax.ppermute(v, "fsdp", xor_pairs(8, k))
    half = shard.shape[0] // 2
    side, down = swap(shard, 2), swap(shard, 4)
    far_top, far_low = swap(down[:half], 2), swap(side[half:], 4)
    own = [(shard, 0, 0), (side, 2, 0), (down, 4, 0), (far_top, 6, 0), (far_low, 6, half)]
    other = [(swap(v, 1), k + 1, off) for v, k, off in own]
    return own + other


def scatter_sum(even, odd):
    swap = lambda v, k: lax.ppermute(v, "fsdp", xor_pairs(8, k))
    half = even.shape[1] // 2
    part = even.astype(F32) + swap(odd, 1).astype(F32)
    low = part.astype(BF16)
    far_top, far_low = swap(low[3, :half], 2), swap(low[3, half:], 4)
    down = part[2].at[:half].add(far_top.astype(F32)).astype(BF16)
    side = part[1].at[half:].add(far_low.astype(F32)).astype(BF16)
    return part[0] + swap(side, 2).astype(F32) + swap(down, 4).astype(F32)


def seq_sum(v, size):
    if size != 4:
        return lax.psum(v, "seq")
    z = lax.axis_index("seq")
    swap = lambda a, k: lax.ppermute(a, "seq", xor_pairs(4, k))
    rows = v.shape[0] // 4
    cut = lambda k: lax.dynamic_slice_in_dim(v, (z ^ k) * rows, rows, 0)
    mine = cut(0)
    for k in (3, 2, 1):
        mine = mine + swap(cut(k).astype(BF16), k).astype(F32)
    mine = mine.astype(BF16)
    whole = jnp.zeros(v.shape, F32)
    for k, part in [(0, mine)] + [(k, swap(mine, k)) for k in (3, 2, 1)]:
        whole = lax.dynamic_update_slice_in_dim(whole, part.astype(F32), (z ^ k) * rows, 0)
    return whole


def total_sum(v, sizes):
    for name, size in sizes:
        if size & (size - 1):
            v = lax.psum(v, name)
            continue
        k = 1
        while k < size:
            v = v + lax.ppermute(v, name, xor_pairs(size, k))
            k *= 2
    return v


def on_device(
    layer_input,
    segment_ids,
    gain_in,
    in_weight,
    conv_weight,
    conv_bias,
    dt_bias,
    a_log,
    skip_gain,
    gain_out,
    out_weight,
    cotangent,
):
    shards, parts = lax.axis_size("fsdp"), lax.axis_size("seq")
    at_fsdp, at_seq = lax.axis_index("fsdp"), lax.axis_index("seq")
    _, batch, part_len, depth = layer_input.shape
    heads = dt_bias.shape[0]
    inner = heads * HEADDIM
    taps = conv_weight.shape[1]
    conv_chans = conv_weight.shape[0] * shards
    state = (conv_chans - inner) // 2
    assert part_len == SPAN and batch == 2 and state == LANES and taps == 4
    wide = conv_chans + LANES
    main = batch * SPAN
    chunk = depth // shards
    up = [(i, i + 1) for i in range(parts - 1)]
    down = [(i + 1, i) for i in range(parts - 1)]

    w_rest = jnp.pad(in_weight[:, inner:], ((0, 0), (0, wide - conv_chans - heads)))
    w_pair = jnp.concatenate([out_weight, in_weight[:, : inner // 2], in_weight[:, inner // 2 : inner]], axis=0)
    custom = gather_layout(chunk, shards)
    halo_in = lax.ppermute(layer_input[0, :, SPAN - HALO :, :], "seq", up).reshape(batch * HALO, depth)
    if custom:
        rest_pieces = gather_pieces(w_rest)
        w_pair, _ = lax.optimization_barrier((w_pair, rest_pieces[3][0]))
        pair_pieces = gather_pieces(w_pair)
        idx = at_fsdp.astype(jnp.int32).reshape(1)
    else:
        rest_pieces = [(lax.all_gather(w_rest, "fsdp", axis=0, tiled=True), 0, 0)]
        whole = lax.all_gather(w_pair, "fsdp", axis=0)
        rows_out = inner // shards
        whole = jnp.concatenate(
            [
                whole[:, :rows_out].reshape(inner, depth),
                whole[:, rows_out : rows_out + chunk].reshape(depth, depth),
                whole[:, rows_out + chunk :].reshape(depth, depth),
            ],
            axis=0,
        )
        pair_pieces = [(whole, 0, 0)]
        idx = jnp.zeros((1,), jnp.int32)
    small = jnp.concatenate([gain_in, conv_weight.T.reshape(-1), conv_bias, gain_out])
    small = lax.all_gather(small, "fsdp", axis=0).astype(F32)
    cut0, cut1 = chunk, chunk + taps * conv_chans // shards
    cut2 = cut1 + conv_chans // shards
    gain_front = small[:, :cut0].reshape(1, depth)
    taps_all = small[:, cut0:cut1].reshape(shards, taps, conv_chans // shards).transpose(1, 0, 2).reshape(taps, conv_chans)
    convw = jnp.concatenate([taps_all, small[:, cut1:cut2].reshape(1, conv_chans), jnp.zeros((7 - taps, conv_chans), F32)])
    gain_back = small[:, cut2:].reshape(1, inner)
    pad_heads = lambda v, fill: jnp.pad(v.astype(F32), (0, LANES - heads), constant_values=fill)
    head_rows = jnp.stack([pad_heads(dt_bias, OFF), pad_heads(a_log, 0.0), pad_heads(skip_gain, 0.0)])
    head_rows = jnp.pad(head_rows, ((0, 5), (0, 0)))
    segs = jnp.pad(segment_ids[0], ((0, 0), (HALO, 0)), constant_values=-1).astype(F32)
    segs = lax.dynamic_slice_in_dim(segs, at_seq * SPAN, HALO + SPAN, 1)
    seg_col = segs[:, :, None]
    seg_row = segs[:, None, HALO:]
    tokens = layer_input.reshape(main, depth)
    cot = cotangent.reshape(main, depth)

    rows = main + batch * HALO
    normed = vmem_call(norm_body, sds((rows, depth), BF16), 0, 3, moved=4 * rows * depth)(tokens, halo_in, gain_front)
    layout = tuple((k, off) for _, k, off in rest_pieces)
    proj = vmem_call(
        partial(proj_body, layout, batch, inner, state),
        (
            sds((depth, wide), BF16),
            sds((batch, HALO + SPAN, conv_chans), BF16),
            sds((batch, SPAN, LANES), F32),
            sds((batch, SPAN, inner), F32),
            sds((batch, SPAN, 2 * state), BF16),
            sds((batch, SPAN, inner), BF16),
            sds((batch, SPAN, LANES), F32),
            sds((batch, SPAN, LANES), F32),
            sds((batch, LANES, SPAN), F32),
            sds((batch, state, inner), F32),
            sds((batch, state, inner), BF16),
            sds((batch, 8, inner), F32),
        ),
        1,
        4 + len(layout),
        scratch=[pltpu.VMEM((HALO + SPAN, WIDE), F32), pltpu.VMEM((batch, SPAN, 2 * LANES), BF16)],
        flops=2 * rows * depth * wide,
        moved=8 * rows * wide,
    )(idx, normed, convw, head_rows, seg_col, *[v for v, _, _ in rest_pieces])
    (w_all, conv_in, dt_raw, x_all, bc_all, xdt_all, dt_all, s_all, st_all, fresh, send, decay) = proj

    carry = [jnp.zeros((state, inner), BF16) for _ in range(batch)]
    moving = [send[b] for b in range(batch)]
    for hop in range(parts - 1):
        for b in range(batch):
            got = lax.ppermute(moving[b], "seq", [up[hop]])
            carry[b] = carry[b] + got
            if hop < parts - 2:
                moving[b] = (fresh[b] + decay[b, 0:1] * carry[b].astype(F32)).astype(BF16)

    y_in = [
        vmem_call(partial(intra_body, state), sds((SPAN, inner), F32), 0, 6, flops=4 * heads * SPAN * SPAN * LANES, moved=4 * SPAN * inner)(
            bc_all[b], xdt_all[b], s_all[b], st_all[b], seg_col[b], seg_row[b]
        )
        for b in range(batch)
    ]
    layout2 = tuple((k, off) for _, k, off in pair_pieces)
    w_out, w_gate, gating, d_outn = vmem_call(
        partial(dense_body, layout2, inner),
        (sds((inner, depth), BF16), sds((depth, inner), BF16), sds((main, inner), F32), sds((main, inner), F32)),
        1,
        2 + len(layout2),
        flops=4 * main * depth * inner,
        moved=12 * main * inner,
    )(idx, normed, cot, *[v for v, _, _ in pair_pieces])

    gated = [
        vmem_call(
            partial(gate_body, state, b * SPAN),
            (
                sds((SPAN, inner), BF16),
                sds((SPAN, inner), BF16),
                sds((SPAN, inner), BF16),
                sds((SPAN, inner), BF16),
                sds((SPAN, LANES), F32),
                sds((state, inner), F32),
                sds((state, inner), BF16),
                sds((8, inner), F32),
            ),
            0,
            10,
            scratch=[pltpu.VMEM((SPAN, inner), F32), pltpu.VMEM((SPAN, inner), F32)],
            flops=8 * SPAN * LANES * inner,
            moved=16 * SPAN * inner,
        )(y_in[b], carry[b], bc_all[b], s_all[b], seg_col[b], x_all[b], gating, d_outn, gain_back, head_rows)
        for b in range(batch)
    ]

    d_carry = [jnp.zeros((state, inner), BF16) for _ in range(batch)]
    moving = [gated[b][6] for b in range(batch)]
    for hop in range(parts - 1):
        for b in range(batch):
            got = lax.ppermute(moving[b], "seq", [down[parts - 2 - hop]])
            d_carry[b] = d_carry[b] + got
            if hop < parts - 2:
                moving[b] = (gated[b][5] + decay[b, 0:1] * d_carry[b].astype(F32)).astype(BF16)

    inner_back = [
        vmem_call(
            partial(intra_back_body, state),
            (sds((SPAN, inner), F32), sds((SPAN, 2 * state), F32)),
            0,
            9,
            scratch=[pltpu.VMEM((SPAN, SPAN), F32)],
            flops=8 * heads * SPAN * SPAN * LANES,
            moved=8 * SPAN * inner,
        )(bc_all[b], xdt_all[b], gated[b][1], gated[b][2], carry[b], s_all[b], st_all[b], seg_col[b], seg_row[b])
        for b in range(batch)
    ]
    ways = shards if custom else 1
    pair_rows = (inner + 2 * depth) // ways
    halves = lambda r, c: tuple(sds((max(ways // 2, 1), r, c), BF16) for _ in range(min(ways, 2)))
    *pair_grads, out_rows, d_normed_gate = vmem_call(
        partial(out_body, ways),
        halves(pair_rows, depth) + (sds((main, depth), BF16), sds((main, depth), F32)),
        1,
        9,
        scratch=[pltpu.VMEM((inner, depth), F32), pltpu.VMEM((depth, inner), F32)],
        flops=8 * main * depth * inner,
        moved=16 * depth * inner,
    )(idx, gated[0][0], gated[1][0], cot, tokens, w_out, gated[0][3], gated[1][3], normed, w_gate)
    if custom:
        pair_sum = seq_sum(scatter_sum(*pair_grads), parts)
    else:
        whole = pair_grads[0][0]
        pair_sum = jnp.concatenate(
            [
                lax.psum_scatter(whole[lo:hi], "fsdp", scatter_dimension=0, tiled=True)
                for lo, hi in ((0, inner), (inner, inner + depth), (inner + depth, inner + 2 * depth))
            ],
            axis=0,
        )
        pair_sum = seq_sum(pair_sum.astype(F32), parts)

    back = [
        vmem_call(
            partial(mixer_back_body, state),
            (sds((SPAN, wide), BF16), sds((HALO, wide), BF16), sds((8, conv_chans), F32), sds((8, LANES), F32)),
            0,
            16,
            scratch=[
                pltpu.VMEM((HALO + SPAN, WIDE), F32),
                pltpu.VMEM((2 * HALO + SPAN, WIDE), F32),
                pltpu.VMEM((2 * HALO + SPAN, WIDE), F32),
            ],
            flops=8 * SPAN * LANES * inner,
            moved=16 * SPAN * inner,
        )(
            conv_in[b],
            dt_raw[b],
            x_all[b],
            bc_all[b],
            xdt_all[b],
            dt_all[b],
            s_all[b],
            seg_col[b],
            convw,
            head_rows,
            inner_back[b][0],
            inner_back[b][1],
            gated[b][1],
            gated[b][4],
            carry[b],
            d_carry[b],
        )
        for b in range(batch)
    ]
    d_rows = (back[0][0], back[1][0], back[0][1], back[1][1])
    rest_grads = vmem_call(
        partial(in_grad_body, ways),
        halves(depth // ways, wide),
        1,
        5,
        scratch=[pltpu.VMEM((rows, wide), BF16), pltpu.VMEM((depth, wide), F32)],
        flops=2 * rows * depth * wide,
        moved=8 * depth * wide,
    )(idx, *d_rows, normed)
    if custom:
        rest_sum = seq_sum(scatter_sum(*rest_grads), parts)
    else:
        rest_sum = lax.psum_scatter(rest_grads[0][0], "fsdp", scatter_dimension=0, tiled=True)
        rest_sum = seq_sum(rest_sum.astype(F32), parts)
    in_grad, halo_grad, gain_grad = vmem_call(
        in_back_body,
        (sds((main, depth), F32), sds((batch * HALO, depth), F32), sds((1, depth), F32)),
        0,
        10,
        scratch=[pltpu.VMEM((rows, wide), BF16)],
        flops=2 * rows * depth * wide,
        moved=16 * rows * depth,
    )(*d_rows, w_all, d_normed_gate, cot, tokens, halo_in, gain_front)
    halo_back = lax.ppermute(halo_grad, "seq", down).reshape(batch, HALO, depth)
    input_grad = in_grad.reshape(batch, SPAN, depth).at[:, SPAN - HALO :].add(halo_back)[None]

    gate_small = gated[0][7] + gated[1][7]
    conv_small = back[0][2] + back[1][2]
    head_small = back[0][3] + back[1][3]
    skip_small = gate_small[1].reshape(heads, HEADDIM).sum(axis=1)
    pieces = [
        conv_small[: taps + 1].reshape(-1),
        gate_small[0],
        gain_grad[0],
        head_small[0, :heads],
        head_small[1, :heads],
        skip_small,
    ]
    flat = jnp.concatenate(pieces)
    flat = jnp.pad(flat, (0, -flat.shape[0] % (8 * LANES))).reshape(-1, LANES)
    flat = total_sum(flat, (("seq", parts), ("fsdp", shards))).reshape(-1)
    at = 0
    sums = []
    for p in pieces:
        sums.append(flat[at : at + p.shape[0]])
        at += p.shape[0]
    conv_sum = sums[0].reshape(taps + 1, conv_chans)
    own = lambda v, axis: lax.dynamic_slice_in_dim(v, at_fsdp * (v.shape[axis] // shards), v.shape[axis] // shards, axis)
    grad_conv_weight = own(conv_sum[:taps], 1).T
    grad_conv_bias = own(conv_sum[taps], 0)
    rows_out = inner // shards
    grad_in_weight = jnp.concatenate(
        [pair_sum[rows_out : rows_out + chunk], pair_sum[rows_out + chunk :], rest_sum[:, : conv_chans + heads]], axis=1
    )
    return (
        out_rows.reshape(1, batch, SPAN, depth),
        input_grad,
        own(sums[2], 0),
        grad_in_weight,
        grad_conv_weight,
        grad_conv_bias,
        sums[3],
        sums[4],
        sums[5],
        own(sums[1], 0),
        pair_sum[:rows_out],
    )


def solution(mesh):
    tokens = P("fsdp", None, "seq", None)
    row, matrix = P("fsdp"), P("fsdp", None)
    return jax.shard_map(
        on_device,
        mesh=mesh,
        in_specs=(tokens, P("fsdp", None, None), row, matrix, matrix, row, P(), P(), P(), row, matrix, tokens),
        out_specs=(tokens, tokens, row, matrix, matrix, row, P(), P(), P(), row, matrix),
        check_vma=False,
    )
```

```python
from functools import partial

import jax
import jax.numpy as jnp
from jax import lax
from jax.experimental import pallas as pl
from jax.experimental.pallas import tpu as pltpu
from jax.sharding import PartitionSpec as P

SPAN = 256
HEADDIM = 64
LANES = 128
HALO = 16
WIDE = 256
EPS_NORM = 1e-05
COST = 1e9
OFF = -10000.0
F32 = jnp.float32
BF16 = jnp.bfloat16


def nn(a, b):
    return lax.dot_general(a, b, (((1,), (0,)), ((), ())), preferred_element_type=F32)


def nt(a, b):
    return lax.dot_general(a, b, (((1,), (1,)), ((), ())), preferred_element_type=F32)


def tn(a, b):
    return lax.dot_general(a, b, (((0,), (0,)), ((), ())), preferred_element_type=F32)


def iota(shape, dim):
    return lax.broadcasted_iota(jnp.int32, shape, dim)


def ones_where(cond):
    return jnp.where(cond, 1.0, 0.0)


def split2(v):
    high = v.astype(BF16)
    low = (v - high.astype(F32)).astype(BF16)
    return jnp.concatenate([high, low], axis=1)


def to_heads(v, picks):
    high = v.astype(BF16)
    mid = (v - high.astype(F32)).astype(BF16)
    return nt(high, picks) + nt(mid, picks)


def running_sum(tri, v):
    high = v.astype(BF16)
    rest = v - high.astype(F32)
    mid = rest.astype(BF16)
    low = (rest - mid.astype(F32)).astype(BF16)
    return nn(tri, high) + nn(tri, mid) + nn(tri, low)


def silu_slope(v, sig):
    return sig * (1.0 + v * (1.0 - sig))


def softplus(v):
    return jnp.maximum(v, 0.0) + jnp.log1p(jnp.exp(-jnp.abs(v)))


def row_masks(seg_ref, b, taps):
    here = segs_of(seg_ref, b)
    return [ones_where(seg_ref[pl.ds(HALO - j, SPAN), b : b + 1] == here) for j in range(1, taps)]


def segs_of(seg_ref, b):
    return seg_ref[pl.ds(HALO, SPAN), b : b + 1]


def seg_before(seg_ref, b):
    return seg_ref[HALO - 1 : HALO, b : b + 1]


def seg_last(seg_ref, b):
    return seg_ref[HALO + SPAN - 1 : HALO + SPAN, b : b + 1]


def conv_pre(ext_ref, cols, convw_ref, masks):
    taps = len(masks) + 1
    total = convw_ref[taps : taps + 1, cols] + convw_ref[taps - 1 : taps, cols] * ext_ref[pl.ds(HALO, SPAN), :]
    for j in range(1, taps):
        total = total + convw_ref[taps - 1 - j : taps - j, cols] * (
            ext_ref[pl.ds(HALO - j, SPAN), :] * masks[j - 1]
        )
    return total


def vmem_call(body, out_shape, operands, idx=None, scratch=(), mib=8, after=(), us=0.05, hbm=False):
    vm = pl.BlockSpec(memory_space=pltpu.VMEM)
    smem = [] if idx is None else [idx]
    head, tail = len(smem) + len(operands), len(after)

    def run(*refs):
        body(*refs[:head], *refs[head + tail :])

    return pl.pallas_call(
        run,
        out_shape=out_shape,
        in_specs=[pl.BlockSpec(memory_space=pltpu.SMEM)] * len(smem)
        + [pl.BlockSpec(memory_space=pltpu.HBM) if hbm else vm] * len(operands)
        + [pl.BlockSpec(memory_space=pl.ANY)] * tail,
        out_specs=jax.tree.map(lambda _: vm, out_shape),
        scratch_shapes=list(scratch),
        compiler_params=pltpu.CompilerParams(vmem_limit_bytes=mib * 1024 * 1024),
        cost_estimate=pl.CostEstimate(flops=int(us * COST), bytes_accessed=0, transcendentals=0),
        name=body.func.__name__ if isinstance(body, partial) else body.__name__,
    )(*smem, *operands, *after)


def sds(shape, dtype):
    return jax.ShapeDtypeStruct(shape, dtype)


def prep_body(heads, segs_ref, dtb_ref, alog_ref, skip_ref, spread_ref, seg_ref, heads_ref):
    for c0 in range(0, spread_ref.shape[1], WIDE):
        shape = (2 * LANES, WIDE)
        hit = (iota(shape, 0) & (LANES - 1)) == ((iota(shape, 1) + c0) >> 6)
        spread_ref[:, c0 : c0 + WIDE] = ones_where(hit).astype(BF16)
    seg_ref[...] = segs_ref[...].T[0 : HALO + SPAN, :]
    heads_ref[...] = jnp.zeros(heads_ref.shape, F32)
    heads_ref[0:1, :] = jnp.full((1, LANES), OFF, F32)
    for row, ref in enumerate((dtb_ref, alog_ref, skip_ref)):
        heads_ref[row : row + 1, 0:heads] = ref[...].astype(F32)


def small_rows(taps, width):
    third = -(-width // 3)
    return [
        (t, 3 * t + m, m * third, min(third, width - m * third)) for t in range(taps + 1) for m in range(3)
    ]


def pack_body(heads, inner, *refs):
    given, out_ref, end_ref, sems = refs[:5], refs[5], refs[6], refs[-1]
    copies = [pltpu.make_async_copy(a, b, sems.at[i]) for i, (a, b) in enumerate(zip(given, refs[7:12]))]
    for copy in copies:
        copy.start()
    for copy in copies:
        copy.wait()
    w_ref, gain_ref, conv_ref, bias_ref, back_ref = refs[7:12]
    full = w_ref.shape[1] - inner - heads
    taps, width = conv_ref.shape
    flat = lambda ref: ref[...].astype(F32).reshape(1, ref.shape[0])
    out_ref[:, 0:full] = w_ref[:, inner : inner + full]
    end_ref[...] = jnp.zeros(end_ref.shape, F32)
    end_ref[:, 0:heads] = w_ref[:, inner + full :].astype(F32)
    conv, bias, back = conv_ref[...].astype(F32), flat(bias_ref), flat(back_ref)
    for t, row, first, size in small_rows(taps, width):
        value = conv[t : t + 1] if t < taps else bias
        end_ref[row : row + 1, heads : heads + size] = value[:, first : first + size]
    row = 3 * (taps + 1)
    chunk, half = gain_ref.shape[0], back_ref.shape[0] // 2
    end_ref[row : row + 1, heads : heads + chunk] = flat(gain_ref)
    for m in range(2):
        end_ref[row + 1 + m : row + 2 + m, heads : heads + half] = back[:, m * half : (m + 1) * half]
    out_ref[:, full:] = end_ref[...].astype(BF16)


def unpack(heads, taps, shards, end_ref, gain_ref, conv_ref, back_ref):
    chunk = end_ref.shape[0] // shards
    width, half = conv_ref.shape[1] // shards, back_ref.shape[1] // shards // 2
    conv_ref[taps + 1 :, :] = jnp.zeros((7 - taps, conv_ref.shape[1]), F32)
    for i in range(shards):
        at = i * chunk
        for t, row, first, size in small_rows(taps, width):
            conv_ref[t : t + 1, i * width + first : i * width + first + size] = end_ref[
                at + row : at + row + 1, heads : heads + size
            ]
        row = at + 3 * (taps + 1)
        gain_ref[:, i * chunk : (i + 1) * chunk] = end_ref[row : row + 1, heads : heads + chunk]
        for m in range(2):
            first = (2 * i + m) * half
            back_ref[:, first : first + half] = end_ref[row + 1 + m : row + 2 + m, heads : heads + half]


def proj_body(layout, batch, heads, shards, state, *refs):
    idx_ref, tokens_ref, halo_ref, heads_ref, seg_ref, spread_ref = refs[:6]
    pieces = refs[6 : 6 + len(layout)]
    (w_ref, normed_ref, gain_ref, convw_ref, back_ref, convin_ref, dtraw_ref, x_ref, bc_ref, xdt_ref, dt_ref, s_ref, st_ref, fresh_ref, send_ref, decay_ref) = refs[
        6 + len(layout) : 22 + len(layout)
    ]
    ext_ref, tail_ref, end_ref = refs[22 + len(layout) :]
    inner = heads * HEADDIM
    chunk = w_ref.shape[0] // (1 if len(layout) == 1 else 8)

    def store(first, off, view):
        w_ref[pl.ds(pl.multiple_of(first, HALO), view.shape[0]), :] = view[...]

    put_pieces(layout, pieces, idx_ref[0], chunk, store)
    conv_chans = inner + 2 * state
    taps = 4
    end_ref[...] = w_ref[:, conv_chans:].astype(F32)
    unpack(heads, taps, shards, end_ref, gain_ref, convw_ref, back_ref)
    w_ref[:, conv_chans:] = jnp.where(iota(end_ref.shape, 1) < heads, end_ref[...], 0.0).astype(BF16)
    main = tokens_ref.shape[0]
    for ref, first in ((tokens_ref, 0), (halo_ref, main)):
        v = ref[...].astype(F32)
        scale = lax.rsqrt(jnp.mean(v * v, axis=1, keepdims=True) + EPS_NORM)
        normed_ref[pl.ds(first, ref.shape[0]), :] = (v * scale * gain_ref[...]).astype(BF16)
    normed = normed_ref[...]
    raw = nn(normed, w_ref[:, conv_chans : conv_chans + LANES])
    tri = ones_where(iota((SPAN, SPAN), 0) >= iota((SPAN, SPAN), 1)).astype(BF16)
    all_masks = []
    for b in range(batch):
        all_masks.append(row_masks(seg_ref, b, taps))
        dt_raw = raw[b * SPAN : (b + 1) * SPAN].astype(BF16).astype(F32)
        dtraw_ref[b][...] = dt_raw
        dt = softplus(dt_raw + heads_ref[0:1, :])
        dt_ref[b][...] = dt
        rate = -jnp.exp(heads_ref[1:2, :])
        logs = running_sum(tri, dt * rate)
        s_ref[b][...] = logs
        st_ref[b][...] = logs.T
        last = logs[SPAN - 1 : SPAN, :]
        same_last = ones_where(segs_of(seg_ref, b) == seg_last(seg_ref, b))
        tail_ref[b] = split2(jnp.exp(last - logs) * same_last)
        keep = ones_where(seg_last(seg_ref, b) == seg_before(seg_ref, b))
        factor = jnp.broadcast_to(jnp.exp(last) * keep, (8, LANES))
        for c0 in range(0, inner, WIDE):
            decay_ref[b][:, c0 : c0 + WIDE] = nn(split2(factor), spread_ref[:, c0 : c0 + WIDE])
    for c0 in [inner] + list(range(0, inner, WIDE)):
        cols = slice(c0, c0 + WIDE)
        projected = nn(normed, w_ref[:, cols]).astype(BF16)
        for b in range(batch):
            halo0 = batch * SPAN + b * HALO
            top = projected[halo0 : halo0 + HALO]
            rest = projected[b * SPAN : (b + 1) * SPAN]
            convin_ref[b][0:HALO, cols] = top
            convin_ref[b][HALO : HALO + SPAN, cols] = rest
            ext_ref[0:HALO, :] = top.astype(F32)
            ext_ref[HALO : HALO + SPAN, :] = rest.astype(F32)
            pre = conv_pre(ext_ref, cols, convw_ref, all_masks[b])
            act = pre * jax.nn.sigmoid(pre)
            if c0 == inner:
                bc_ref[b][...] = act.astype(BF16)
            else:
                spread = spread_ref[:, cols]
                x_ref[b][:, cols] = act
                xdt = (nn(split2(dt_ref[b][...]), spread) * act).astype(BF16)
                xdt_ref[b][:, cols] = xdt
                xt = (nn(tail_ref[b], spread) * xdt.astype(F32)).astype(BF16)
                fresh = tn(bc_ref[b][:, 0:state], xt)
                fresh_ref[b][:, cols] = fresh
                send_ref[b][:, cols] = fresh.astype(BF16)


def inside_mask(seg_ref, segr_ref, b, flipped):
    rows, cols = iota((SPAN, SPAN), 0), iota((SPAN, SPAN), 1)
    ordered = rows <= cols if flipped else rows >= cols
    return ordered & (segs_of(seg_ref, b) == segr_ref[b : b + 1, :])


def head_halves(block):
    low = iota(block.shape, 1) < HEADDIM
    zero = jnp.zeros_like(block)
    return jnp.where(low, block, zero), jnp.where(low, zero, block)


def intra_body(state, b, bc_ref, xdt_ref, s_ref, st_ref, seg_ref, segr_ref, y_ref):
    scores = nt(bc_ref[:, state : 2 * state], bc_ref[:, 0:state])
    scores = jnp.where(inside_mask(seg_ref, segr_ref, b, False), scores, 0.0)
    for pair in range(xdt_ref.shape[1] // LANES):
        cols = slice(pair * LANES, (pair + 1) * LANES)
        total = None
        for half, values in enumerate(head_halves(xdt_ref[:, cols])):
            h = 2 * pair + half
            decay = jnp.exp(jnp.minimum(s_ref[:, h : h + 1] - st_ref[h : h + 1, :], 0.0))
            part = nn((scores * decay).astype(BF16), values)
            total = part if total is None else total + part
        y_ref[:, cols] = total


def dense_body(layout, inner, *refs):
    idx_ref, normed_ref, cot_ref = refs[:3]
    pieces = refs[3 : 3 + len(layout)]
    wout_ref, wgate_ref, gating_ref, dout_ref = refs[3 + len(layout) :]
    depth = wgate_ref.shape[0]
    shards = 1 if len(layout) == 1 else 8
    ochunk, gchunk = inner // shards, depth // shards
    half_cols = inner // 2
    def store(owner, off, view):
        wout_ref[pl.ds(pl.multiple_of(owner * ochunk, HALO), ochunk), :] = view[0:ochunk, :]
        for side in range(2):
            wgate_ref[
                pl.ds(pl.multiple_of(owner * gchunk, HALO), gchunk), side * half_cols : (side + 1) * half_cols
            ] = view[ochunk + side * gchunk : ochunk + (side + 1) * gchunk, :]

    put_pieces(layout, pieces, idx_ref[0], 1, store)
    normed = normed_ref[0 : cot_ref.shape[0], :]
    cot = cot_ref[...]
    for c0 in range(0, inner, WIDE):
        gating_ref[:, c0 : c0 + WIDE] = nn(normed, wgate_ref[:, c0 : c0 + WIDE])
        dout_ref[:, c0 : c0 + WIDE] = nt(cot, wout_ref[c0 : c0 + WIDE, :])


def gate_body(state, b, *refs):
    (yin_ref, carry_ref, bc_ref, s_ref, seg_ref, x_ref, gating_ref, dout_ref, gain_ref, heads_ref, spread_ref) = refs[:11]
    (outn_ref, dy_ref, ey_ref, dgat_ref, rowterm_ref, grad_ref, send_ref, small_ref) = refs[11:19]
    y_ref, gated_ref = refs[19:]
    inner = x_ref.shape[1]
    rows = pl.ds(b * SPAN, SPAN)
    c_mat = bc_ref[:, state : 2 * state]
    carried = ones_where(segs_of(seg_ref, b) == seg_before(seg_ref, b))
    factor = split2(jnp.exp(s_ref[...]) * carried)
    skip = split2(jnp.broadcast_to(heads_ref[2:3, :], (8, LANES)))
    sumsq = jnp.zeros((SPAN, 1), F32)
    sumeg = jnp.zeros((SPAN, 1), F32)
    for c0 in range(0, inner, WIDE):
        cols = slice(c0, c0 + WIDE)
        spread = spread_ref[:, cols]
        y = yin_ref[:, cols] + nn(factor, spread) * nn(c_mat, carry_ref[:, cols])
        y_ref[:, cols] = y
        mixed = (y + nn(skip, spread)[0:1, :] * x_ref[:, cols]).astype(BF16).astype(F32)
        gate = gating_ref[rows, cols]
        gated = mixed * (gate * jax.nn.sigmoid(gate))
        gated_ref[:, cols] = gated
        sumsq = sumsq + jnp.sum(gated * gated, axis=1, keepdims=True)
        sumeg = sumeg + jnp.sum(dout_ref[rows, cols] * gain_ref[:, cols] * gated, axis=1, keepdims=True)
    r = lax.rsqrt(sumsq / inner + EPS_NORM)
    coef = r * r * r * (sumeg / inner)
    terms = jnp.zeros((SPAN, LANES), F32)
    skips = jnp.zeros((8, LANES), F32)
    for c0 in range(0, inner, WIDE):
        cols = slice(c0, c0 + WIDE)
        spread = spread_ref[:, cols]
        gated = gated_ref[:, cols]
        gain = gain_ref[:, cols]
        dout = dout_ref[rows, cols]
        normal = gated * r
        outn_ref[:, cols] = (normal * gain).astype(BF16)
        y = y_ref[:, cols]
        x = x_ref[:, cols]
        d_gated = r * (dout * gain) - gated * coef
        gate = gating_ref[rows, cols]
        sig = jax.nn.sigmoid(gate)
        mixed = (y + nn(skip, spread)[0:1, :] * x).astype(BF16).astype(F32)
        dgat_ref[:, cols] = (d_gated * mixed * silu_slope(gate, sig)).astype(BF16)
        dy = (d_gated * (gate * sig)).astype(BF16)
        dy_ref[:, cols] = dy
        dyf = dy.astype(F32)
        ey = (nn(factor, spread) * dyf).astype(BF16)
        ey_ref[:, cols] = ey
        terms = terms + to_heads(dyf * y, spread_ref[0:LANES, cols])
        grad = tn(c_mat, ey)
        grad_ref[:, cols] = grad
        send_ref[:, cols] = grad.astype(BF16)
        skips = skips + to_heads(jnp.broadcast_to(jnp.sum(dyf * x, axis=0, keepdims=True), (8, WIDE)), spread_ref[0:LANES, cols])
    rowterm_ref[...] = terms
    small_ref[...] = jnp.where(iota(skips.shape, 0) == 2, skips, 0.0)


def intra_back_body(state, b, *refs):
    (bc_ref, xdt_ref, dy_ref, ey_ref, carry_ref, s_ref, st_ref, seg_ref, segr_ref) = refs[:9]
    dxdt_ref, dbc_ref = refs[9:11]
    acc_ref = refs[11]
    b_mat = bc_ref[:, 0:state]
    c_mat = bc_ref[:, state : 2 * state]
    mask = inside_mask(seg_ref, segr_ref, b, True)
    scores = jnp.where(mask, nt(b_mat, c_mat), 0.0)
    for pair in range(xdt_ref.shape[1] // LANES):
        cols = slice(pair * LANES, (pair + 1) * LANES)
        total = None
        dy_block = dy_ref[:, cols]
        for half, (values, grads) in enumerate(zip(head_halves(xdt_ref[:, cols]), head_halves(dy_block))):
            h = 2 * pair + half
            decay = jnp.exp(jnp.minimum(st_ref[h : h + 1, :] - s_ref[:, h : h + 1], 0.0))
            part = nn((scores * decay).astype(BF16), grads)
            total = part if total is None else total + part
            d_weight = nt(values, dy_block) * decay
            if h == 0:
                acc_ref[...] = d_weight
            else:
                acc_ref[...] += d_weight
        dxdt_ref[:, cols] = total
    d_scores = jnp.where(mask, acc_ref[...], 0.0).astype(BF16)
    dbc_ref[:, 0:state] = nn(d_scores, c_mat)
    dbc_ref[:, state : 2 * state] = tn(d_scores, b_mat) + nt(ey_ref[...], carry_ref[...])


def mixer_back_body(state, b, *refs):
    (convin_ref, dtraw_ref, x_ref, bc_ref, xdt_ref, dt_ref, s_ref, seg_ref, convw_ref, heads_ref) = refs[:10]
    (dxdt_ref, dbc_ref, dy_ref, rowterm_ref, carry_ref, dcarry_ref, spread_ref) = refs[10:17]
    (dmain_ref, dhalo_ref, small_ref, hsmall_ref) = refs[17:21]
    ext_ref, dpre_ref, dconv_ref = refs[21:]
    inner = x_ref.shape[1]
    taps = 4
    conv_chans = inner + 2 * state
    masks = row_masks(seg_ref, b, taps)
    b_mat = bc_ref[:, 0:state]
    logs = s_ref[...]
    dt = dt_ref[...]
    rate = -jnp.exp(heads_ref[1:2, :])
    last = logs[SPAN - 1 : SPAN, :]
    same_last = ones_where(segs_of(seg_ref, b) == seg_last(seg_ref, b))
    keep = ones_where(seg_last(seg_ref, b) == seg_before(seg_ref, b))
    tail = split2(jnp.exp(last - logs) * same_last)
    dt2 = split2(dt)
    skip = split2(jnp.broadcast_to(heads_ref[2:3, :], (8, LANES)))
    col_term = jnp.zeros((SPAN, LANES), F32)
    direct = jnp.zeros((SPAN, LANES), F32)
    last_term = jnp.zeros((8, LANES), F32)
    d_b = dbc_ref[:, 0:state]
    dconv_ref[HALO + SPAN : HALO + SPAN + HALO, :] = jnp.zeros((HALO, WIDE), F32)
    dpre_ref[0:HALO, :] = jnp.zeros((HALO, WIDE), F32)
    dpre_ref[HALO + SPAN : HALO + SPAN + HALO, :] = jnp.zeros((HALO, WIDE), F32)
    small_ref[taps + 1 : 8, :] = jnp.zeros((7 - taps, conv_chans), F32)

    def conv_back(cols, d_act):
        ext_ref[...] = convin_ref[:, cols].astype(F32)
        pre = conv_pre(ext_ref, cols, convw_ref, masks)
        d_pre = d_act * silu_slope(pre, jax.nn.sigmoid(pre))
        small_ref[taps : taps + 1, cols] = jnp.sum(d_pre, axis=0, keepdims=True)
        small_ref[taps - 1 : taps, cols] = jnp.sum(d_pre * ext_ref[pl.ds(HALO, SPAN), :], axis=0, keepdims=True)
        dpre_ref[pl.ds(HALO, SPAN), :] = d_pre
        total = convw_ref[taps - 1 : taps, cols] * dpre_ref[pl.ds(0, HALO + SPAN), :]
        for j in range(1, taps):
            masked = d_pre * masks[j - 1]
            small_ref[taps - 1 - j : taps - j, cols] = jnp.sum(
                masked * ext_ref[pl.ds(HALO - j, SPAN), :], axis=0, keepdims=True
            )
            dconv_ref[pl.ds(0, HALO), :] = jnp.zeros((HALO, WIDE), F32)
            dconv_ref[pl.ds(HALO, SPAN), :] = masked
            total = total + convw_ref[taps - 1 - j : taps - j, cols] * dconv_ref[pl.ds(j, HALO + SPAN), :]
        total = total.astype(BF16)
        dhalo_ref[:, cols] = total[0:HALO]
        dmain_ref[:, cols] = total[HALO : HALO + SPAN]

    for c0 in range(0, inner, WIDE):
        cols = slice(c0, c0 + WIDE)
        spread = spread_ref[:, cols]
        picks = spread_ref[0:LANES, cols]
        d_carry = dcarry_ref[:, cols]
        tails = nn(tail, spread)
        xdt = xdt_ref[:, cols].astype(F32)
        d_tail = tails * nn(b_mat, d_carry)
        d_xdt = dxdt_ref[:, cols] + d_tail
        x = x_ref[:, cols]
        col_term = col_term + to_heads(xdt * d_xdt, picks)
        direct = direct + to_heads(x * d_xdt, picks)
        from_tail = jnp.sum(xdt * d_tail, axis=0, keepdims=True)
        through = jnp.sum(d_carry.astype(F32) * carry_ref[:, cols].astype(F32), axis=0, keepdims=True)
        both = to_heads(jnp.concatenate([from_tail, through, jnp.zeros((6, WIDE), F32)], axis=0), picks)
        last_term = last_term + both
        d_b = d_b + nt((tails * xdt).astype(BF16), d_carry)
        d_x = nn(dt2, spread) * d_xdt + nn(skip, spread)[0:1, :] * dy_ref[:, cols].astype(F32)
        conv_back(cols, d_x)
    conv_back(slice(inner, conv_chans), jnp.concatenate([d_b, dbc_ref[:, state : 2 * state]], axis=1))
    at_end = last_term[0:1, :] + last_term[1:2, :] * (jnp.exp(last) * keep)
    upper = ones_where(iota((SPAN, SPAN), 0) <= iota((SPAN, SPAN), 1)).astype(BF16)
    d_logs = running_sum(upper, rowterm_ref[...] - col_term) + at_end
    d_dt = direct + rate * d_logs
    d_raw = d_dt * jax.nn.sigmoid(dtraw_ref[...] + heads_ref[0:1, :])
    dmain_ref[:, conv_chans : conv_chans + LANES] = d_raw.astype(BF16)
    dhalo_ref[:, conv_chans : conv_chans + LANES] = jnp.zeros((HALO, LANES), BF16)
    hsmall_ref[0:1, :] = jnp.sum(d_raw, axis=0, keepdims=True)
    hsmall_ref[1:2, :] = jnp.sum(dt * d_logs, axis=0, keepdims=True) * rate
    hsmall_ref[2:8, :] = jnp.zeros((6, LANES), F32)


def out_grad_body(shards, *refs):
    (idx_ref, on0_ref, on1_ref, cot_ref, dg0_ref, dg1_ref, normed_ref) = refs[:7]
    outs = refs[7:-2]
    gout_ref, ggate_ref = refs[-2:]
    main = cot_ref.shape[0]
    inner, width = gout_ref.shape
    outn = jnp.concatenate([on0_ref[...], on1_ref[...]], axis=0)
    dgat = jnp.concatenate([dg0_ref[...], dg1_ref[...]], axis=0)
    normed = normed_ref[0:main, :]
    gout_ref[...] = tn(outn, cot_ref[...])
    for c0 in range(0, inner, width):
        ggate_ref[:, c0 : c0 + width] = tn(normed, dgat[:, c0 : c0 + width])
    ochunk, gchunk = inner // shards, width // shards
    for k in range(shards):
        owner = idx_ref[0] ^ k
        ref = outs[0].at[k // 2] if k % 2 == 0 else outs[1 + k // 2]
        ref[0:ochunk, :] = gout_ref[pl.ds(pl.multiple_of(owner * ochunk, HALO), ochunk), :].astype(BF16)
        for side in range(2):
            ref[ochunk + side * gchunk : ochunk + (side + 1) * gchunk, :] = ggate_ref[
                pl.ds(pl.multiple_of(owner * gchunk, HALO), gchunk), side * width : (side + 1) * width
            ].astype(BF16)


def out_body(on0_ref, on1_ref, dg0_ref, dg1_ref, xin_ref, wout_ref, wgate_ref, lout_ref, dng_ref):
    for b, (outn_ref, dgat_ref) in enumerate(((on0_ref, dg0_ref), (on1_ref, dg1_ref))):
        rows = slice(b * SPAN, (b + 1) * SPAN)
        lout_ref[rows, :] = (xin_ref[rows, :].astype(F32) + nn(outn_ref[...], wout_ref[...])).astype(BF16)
        dng_ref[rows, :] = nt(dgat_ref[...], wgate_ref[...])


def join_rows(m0_ref, m1_ref, h0_ref, h1_ref, all_ref):
    all_ref[0:SPAN, :] = m0_ref[...]
    all_ref[SPAN : 2 * SPAN, :] = m1_ref[...]
    all_ref[2 * SPAN : 2 * SPAN + HALO, :] = h0_ref[...]
    all_ref[2 * SPAN + HALO : 2 * SPAN + 2 * HALO, :] = h1_ref[...]


def in_grad_body(shards, heads, taps, exact, *refs):
    idx_ref, m0_ref, m1_ref, h0_ref, h1_ref, normed_ref = refs[:6]
    conv0_ref, conv1_ref, head0_ref, head1_ref, skip0_ref, skip1_ref = refs[6:12]
    outs = refs[12:-3]
    all_ref, grad_ref, line_ref = refs[-3:]
    join_rows(m0_ref, m1_ref, h0_ref, h1_ref, all_ref)
    depth, wide = grad_ref.shape
    for c0 in range(0, wide, 384):
        grad_ref[:, c0 : c0 + 384] = tn(normed_ref[...], all_ref[:, c0 : c0 + 384])
    conv = conv0_ref[...] + conv1_ref[...]
    three = head0_ref[...] + head1_ref[...] + skip0_ref[...] + skip1_ref[...]
    chunk, width = depth // shards, conv.shape[1] // shards
    lane0 = wide - LANES + heads
    for i in range(shards):
        for t, row, first, size in small_rows(taps, width):
            at = i * chunk + row
            grad_ref[at : at + 1, lane0 : lane0 + size] = conv[t : t + 1, i * width + first : i * width + first + size]
    if exact:
        line_ref[...] = jnp.zeros(line_ref.shape, F32)
        for m in range(3):
            line_ref[0:1, (m + 1) * heads : (m + 2) * heads] = three[m : m + 1, 0:heads]
        value = line_ref[0:1, :]
        high = value.astype(BF16).astype(F32)
        last = slice(wide - LANES, wide)
        rows = iota((2 * exact, LANES), 0)
        mine = jnp.where(rows == 2 * idx_ref[1], high, 0.0) + jnp.where(rows == 2 * idx_ref[1] + 1, value - high, 0.0)
        for i in range(shards):
            at = slice(i * chunk + 3 * (taps + 1) + 1, i * chunk + 3 * (taps + 1) + 1 + 2 * exact)
            grad_ref[at, last] = grad_ref[at, last] + mine
    ways = 1 if len(outs) == 1 else shards
    part = depth // ways
    for k in range(ways):
        first = pl.multiple_of((idx_ref[0] ^ k) * part, HALO)
        outs[k % 2][k // 2] = grad_ref[pl.ds(first, part), :].astype(BF16)


def in_back_body(m0_ref, m1_ref, h0_ref, h1_ref, w_ref, dng_ref, cot_ref, xin_ref, halo_ref, gain_ref, *outs):
    igrad_ref, hgrad_ref, all_ref = outs
    main = cot_ref.shape[0]
    join_rows(m0_ref, m1_ref, h0_ref, h1_ref, all_ref)
    d_normed = nt(all_ref[...], w_ref[...])
    gain = gain_ref[...]

    def back(dn, v):
        q = lax.rsqrt(jnp.mean(v * v, axis=1, keepdims=True) + EPS_NORM)
        e = dn * gain
        return q * e - v * (q * q * q * jnp.mean(e * v, axis=1, keepdims=True))

    grad = back(d_normed[0:main] + dng_ref[...], xin_ref[...].astype(F32))
    igrad_ref[...] = cot_ref[...].astype(F32) + grad
    hgrad_ref[...] = back(d_normed[main:], halo_ref[...].astype(F32))


def xor_pairs(size, k):
    return [(i, i ^ k) for i in range(size)]


def stack_body(*refs):
    out_ref = refs[-1]
    for i, ref in enumerate(refs[:-1]):
        out_ref[i] = ref[...]


def rows_body(top_ref, low_ref, out_ref):
    half = top_ref.shape[0]
    out_ref[0:half, :] = top_ref[...]
    out_ref[half:, :] = low_ref[...]


def stack(parts, after=()):
    return vmem_call(stack_body, sds((len(parts),) + parts[0].shape, BF16), parts, after=after)


def layout_of(pieces):
    return [v for v, _ in pieces], tuple(places for _, places in pieces)


def put_pieces(layout, refs, idx, chunk, store):
    for ref, places in zip(refs, layout):
        for sub, k, off in places:
            view = ref if sub is None else ref.at[sub]
            store((idx ^ k) * chunk + off, off, view)


def combine_body(last, *refs):
    if last:
        got_ref, carry_ref, out_ref = refs
        out_ref[...] = got_ref[...] + carry_ref[...]
        return
    first = len(refs) == 5
    got_ref, fresh_ref, decay_ref = refs[:3]
    out_ref, send_ref = refs[-2:]
    state = got_ref[...] if first else got_ref[...] + refs[3][...]
    out_ref[...] = state
    send_ref[...] = (fresh_ref[...] + decay_ref[0:1, :] * state.astype(F32)).astype(BF16)


class Chain:
    def __init__(self, fresh, send, decay, pairs):
        self.fresh, self.send, self.decay, self.pairs = fresh, send, decay, pairs
        self.state = None
        self.hop = 0
        self.start()

    def start(self):
        self.got = lax.ppermute(self.send, "seq", [self.pairs[self.hop]])

    def step(self, after=(), us=0.05):
        shape = sds(self.got.shape, BF16)
        prior = [] if self.state is None else [self.state]
        if self.hop == len(self.pairs) - 1:
            if prior:
                self.state = vmem_call(partial(combine_body, True), shape, [self.got] + prior, after=after)
            else:
                self.state = self.got
            return self.state
        self.state, self.send = vmem_call(
            partial(combine_body, False),
            (shape, shape),
            [self.got, self.fresh, self.decay] + prior,
            after=after,
            us=us,
        )
        self.hop += 1
        self.start()
        return self.state


def swap(v, k):
    return lax.ppermute(v, "fsdp", xor_pairs(8, k))


def pair_body(even_ref, *refs):
    own_ref, side_ref, down_ref, top_ref, low_ref = refs[-5:]
    got = refs[:-5] if len(refs) > 6 else [refs[0].at[i] for i in range(4)]
    half = top_ref.shape[0]
    add = lambda s: even_ref[s].astype(F32) + got[s][...].astype(F32)
    far = add(3).astype(BF16)
    top_ref[...] = far[0:half]
    low_ref[...] = far[half:]
    own_ref[...] = add(0)
    side_ref[...] = add(1)
    down_ref[...] = add(2)


def relay_body(side_ref, down_ref, top_ref, low_ref, side_out, down_out):
    half = top_ref.shape[0]
    side_out[0:half, :] = side_ref[0:half, :].astype(BF16)
    side_out[half:, :] = (side_ref[half:, :] + low_ref[...].astype(F32)).astype(BF16)
    down_out[0:half, :] = (down_ref[0:half, :] + top_ref[...].astype(F32)).astype(BF16)
    down_out[half:, :] = down_ref[half:, :].astype(BF16)


class Reduce:
    def __init__(self, even, *odd):
        self.even = even
        self.got = [swap(v, 1) for v in odd]

    def pair(self, after=()):
        _, rows, cols = self.even.shape
        full, half = sds((rows, cols), F32), sds((rows // 2, cols), BF16)
        self.own, self.side, self.down, top, low = vmem_call(
            pair_body, (full, full, full, half, half), [self.even] + self.got, after=after
        )
        self.top, self.low = swap(top, 2), swap(low, 4)
        return self.own

    def relay(self, after=()):
        shape = sds(self.own.shape, BF16)
        side, down = vmem_call(relay_body, (shape, shape), [self.side, self.down, self.top, self.low], after=after)
        self.side, self.down = swap(side, 2), swap(down, 4)
        return side

    def spread(self, z, parts, after=()):
        rows, cols = self.own.shape
        self.parts, self.z = parts, z
        if parts != 4:
            total = self.own + self.side.astype(F32) + self.down.astype(F32)
            self.total = lax.psum(total, "seq")
            return self.total
        cut = sds((rows // 4, cols), BF16)
        mine, *others = vmem_call(
            spread_body,
            (sds((rows // 4, cols), F32), cut, cut, cut),
            [self.own, self.side, self.down],
            idx=z,
            scratch=[pltpu.VMEM((rows, cols), F32)],
            after=after,
        )
        self.mine = mine
        self.others = [lax.ppermute(v, "seq", xor_pairs(4, k + 1)) for k, v in enumerate(others)]
        return mine

    def collect(self, after=()):
        if self.parts != 4:
            return self.total
        part = vmem_call(collect_body, sds(self.mine.shape, BF16), [self.mine] + self.others, after=after, us=30)
        self.quarters = [part] + [lax.ppermute(part, "seq", xor_pairs(4, k)) for k in (1, 2, 3)]
        return part


def spread_body(z_ref, own_ref, side_ref, down_ref, mine_ref, one_ref, two_ref, three_ref, all_ref):
    all_ref[...] = own_ref[...] + side_ref[...].astype(F32) + down_ref[...].astype(F32)
    rows = mine_ref.shape[0]
    for k, ref in enumerate((mine_ref, one_ref, two_ref, three_ref)):
        first = pl.multiple_of((z_ref[0] ^ k) * rows, 8)
        ref[...] = all_ref[pl.ds(first, rows), :].astype(ref.dtype)


def collect_body(mine_ref, one_ref, two_ref, three_ref, out_ref):
    total = mine_ref[...] + one_ref[...].astype(F32) + two_ref[...].astype(F32) + three_ref[...].astype(F32)
    out_ref[...] = total.astype(BF16)


def final_body(heads, taps, sources, idx_ref, *refs):
    w_ref, gain_ref, wout_ref, back_ref, pair_ref = refs[:5]
    quarters = refs[5:-9]
    grad_ref, gout_ref, ggain_ref, gback_ref, conv_ref, bias_ref, heads_ref = refs[-9:-2]
    rest_ref, sums_ref = refs[-2:]
    rows = quarters[0].shape[0]
    for k, ref in enumerate(quarters):
        first = pl.multiple_of((idx_ref[0] ^ k) * rows, 8) if len(quarters) > 1 else 0
        rest_ref[pl.ds(first, rows), :] = ref[...].astype(F32)
    chunk, half = grad_ref.shape[0], pair_ref.shape[1]
    rows_out = gout_ref.shape[0]
    grad_ref[:, 0:half] = pair_ref[rows_out : rows_out + chunk, :]
    grad_ref[:, half : 2 * half] = pair_ref[rows_out + chunk : rows_out + 2 * chunk, :]
    grad_ref[:, 2 * half :] = rest_ref[:, 0 : grad_ref.shape[1] - 2 * half]
    gout_ref[...] = pair_ref[0:rows_out, :]
    total = jnp.sum(w_ref[...].astype(F32) * grad_ref[...], axis=1, keepdims=True)
    sums_ref[0:chunk, :] = jnp.broadcast_to(total, (chunk, LANES))
    ggain_ref[...] = sums_ref[...].T[0:1, 0:chunk] / gain_ref[...].astype(F32)
    total = jnp.sum(wout_ref[...].astype(F32) * gout_ref[...], axis=1, keepdims=True)
    sums_ref[0:rows_out, :] = jnp.broadcast_to(total, (rows_out, LANES))
    gback_ref[...] = sums_ref[...].T[0:1, 0:rows_out] / back_ref[...].astype(F32)
    width = conv_ref.shape[1]
    lane0 = rest_ref.shape[1] - LANES + heads
    for t, row, first, size in small_rows(taps, width):
        value = rest_ref[row : row + 1, lane0 : lane0 + size]
        if t < taps:
            conv_ref[t : t + 1, first : first + size] = value
        else:
            bias_ref[:, first : first + size] = value
    if sources:
        row = 3 * (taps + 1) + 1
        total = jnp.sum(rest_ref[row : row + 2 * sources, rest_ref.shape[1] - LANES :], axis=0, keepdims=True)
        for m in range(3):
            heads_ref[m : m + 1, :] = total[:, (m + 1) * heads : (m + 2) * heads]
    else:
        heads_ref[...] = jnp.zeros(heads_ref.shape, F32)


def halo_add_body(grad_ref, halo_ref, out_ref):
    out_ref[...] = grad_ref[...]
    for b in range(out_ref.shape[0] // SPAN):
        rows = slice((b + 1) * SPAN - HALO, (b + 1) * SPAN)
        out_ref[rows, :] = grad_ref[rows, :] + halo_ref[b * HALO : (b + 1) * HALO, :]


def join_body(z_ref, q0_ref, q1_ref, q2_ref, q3_ref, out_ref):
    rows = q0_ref.shape[0]
    for k, ref in enumerate((q0_ref, q1_ref, q2_ref, q3_ref)):
        out_ref[pl.ds(pl.multiple_of((z_ref[0] ^ k) * rows, 8), rows), :] = ref[...].astype(F32)


def on_device(
    layer_input,
    segment_ids,
    gain_in,
    in_weight,
    conv_weight,
    conv_bias,
    dt_bias,
    a_log,
    skip_gain,
    gain_out,
    out_weight,
    cotangent,
):
    shards, parts = lax.axis_size("fsdp"), lax.axis_size("seq")
    at_fsdp, at_seq = lax.axis_index("fsdp"), lax.axis_index("seq")
    _, batch, part_len, depth = layer_input.shape
    heads = dt_bias.shape[0]
    inner = heads * HEADDIM
    taps = conv_weight.shape[1]
    conv_chans = conv_weight.shape[0] * shards
    state = (conv_chans - inner) // 2
    assert part_len == SPAN and batch == 2 and state == LANES and taps == 4
    wide = conv_chans + LANES
    main = batch * SPAN
    chunk = depth // shards
    up = [(i, i + 1) for i in range(parts - 1)]
    down = [(i + 1, i) for i in range(parts - 1)]

    custom = shards == 8 and chunk % (2 * HALO) == 0
    rows_out = inner // shards
    line = lambda v: v.reshape(1, -1)
    w_rest = vmem_call(
        partial(pack_body, heads, inner),
        sds((chunk, wide), BF16),
        [in_weight, gain_in, conv_weight.T, conv_bias, gain_out],
        scratch=[
            pltpu.VMEM((chunk, LANES), F32),
            *[pltpu.VMEM(v.shape, BF16) for v in (in_weight, gain_in, conv_weight.T, conv_bias, gain_out)],
            pltpu.SemaphoreType.DMA((5,)),
        ],
        hbm=True,
        mib=60,
    )
    segs = jnp.pad(segment_ids[0], ((0, 0), (HALO, 0)), constant_values=-1).astype(F32)
    segs = lax.dynamic_slice_in_dim(segs, at_seq * SPAN, HALO + SPAN, 1)
    seg_row = jnp.pad(segs[:, HALO:], ((0, 8 - batch), (0, 0)))
    segs = jnp.pad(segs, ((0, LANES - batch), (0, -(HALO + SPAN) % LANES)))
    spread, seg_col, head_rows = vmem_call(
        partial(prep_body, heads),
        (sds((2 * LANES, inner), BF16), sds((HALO + SPAN, LANES), F32), sds((8, LANES), F32)),
        [segs, line(dt_bias), line(a_log), line(skip_gain)],
        after=[w_rest],
    )
    w_pair = jnp.concatenate([out_weight, in_weight[:, : inner // 2], in_weight[:, inner // 2 : inner]], axis=0)
    exact = shards * parts if custom and 3 * (taps + 1) + 1 + 2 * shards * parts <= chunk else 0
    me = (at_seq * shards + at_fsdp).astype(jnp.int32)
    idx = jnp.stack([at_fsdp.astype(jnp.int32) if custom else jnp.int32(0), me])
    z_idx = at_seq.astype(jnp.int32).reshape(1)
    halo_in = lax.ppermute(layer_input[0, :, SPAN - HALO :, :], "seq", up).reshape(batch * HALO, depth)
    if custom:
        side, down_w = swap(w_rest, 2), swap(w_rest, 4)
        early = (side, down_w, seg_col, seg_row, head_rows, idx, z_idx, w_pair, halo_in)
        side, down_w, seg_col, seg_row, head_rows, idx, z_idx, w_pair, halo_in = lax.optimization_barrier(early)
        top, low = swap(down_w[: chunk // 2], 2), swap(side[chunk // 2 :], 4)
        near = stack([w_rest, side, down_w])
        near_other = swap(near, 1)
        far = vmem_call(rows_body, sds((chunk, wide), BF16), [top, low], after=[near])
        far_other = swap(far, 1)
        rest_pieces = [
            (w_rest, [(None, 0, 0)]),
            (side, [(None, 2, 0)]),
            (down_w, [(None, 4, 0)]),
            (far, [(None, 6, 0)]),
            (near_other, [(0, 1, 0), (1, 3, 0), (2, 5, 0)]),
            (far_other, [(None, 7, 0)]),
        ]
        w_pair, _ = lax.optimization_barrier((w_pair, far))
        side, down_w = swap(w_pair, 2), swap(w_pair, 4)
        pair_own = [w_pair, side, down_w]
    else:
        rest_pieces = [(lax.all_gather(w_rest, "fsdp", axis=0, tiled=True), [(None, 0, 0)])]
        whole = lax.all_gather(w_pair, "fsdp", axis=0)
        pair_own = [
            jnp.concatenate(
                [
                    whole[:, :rows_out].reshape(inner, depth),
                    whole[:, rows_out : rows_out + chunk].reshape(depth, depth),
                    whole[:, rows_out + chunk :].reshape(depth, depth),
                ],
                axis=0,
            )
        ]
    tokens = layer_input.reshape(main, depth)
    cot = cotangent.reshape(main, depth)
    both = range(batch)

    rows = main + batch * HALO
    rest_values, layout = layout_of(rest_pieces)
    each = lambda shape, dtype: tuple(sds(shape, dtype) for _ in both)
    proj = vmem_call(
        partial(proj_body, layout, batch, heads, shards, state),
        (
            sds((depth, wide), BF16),
            sds((rows, depth), BF16),
            sds((1, depth), F32),
            sds((8, conv_chans), F32),
            sds((1, inner), F32),
            each((HALO + SPAN, conv_chans), BF16),
            each((SPAN, LANES), F32),
            each((SPAN, inner), F32),
            each((SPAN, 2 * state), BF16),
            each((SPAN, inner), BF16),
            each((SPAN, LANES), F32),
            each((SPAN, LANES), F32),
            each((LANES, SPAN), F32),
            each((state, inner), F32),
            each((state, inner), BF16),
            each((8, inner), F32),
        ),
        [tokens, halo_in, head_rows, seg_col, spread] + rest_values,
        idx=idx,
        scratch=[
            pltpu.VMEM((HALO + SPAN, WIDE), F32),
            pltpu.VMEM((batch, SPAN, 2 * LANES), BF16),
            pltpu.VMEM((depth, LANES), F32),
        ],
        us=10,
    )
    (w_all, normed, gain_front, convw, gain_back, conv_in, dt_raw, x_all, bc_all) = proj[:9]
    (xdt_all, dt_all, s_all, st_all, fresh, send, decay) = proj[9:]

    if custom:
        far_w, pair_own[1], _ = lax.optimization_barrier((pair_own[2], pair_own[1], w_all))
        pair_own.append(swap(far_w, 2))

    hops = len(up)
    forth = [Chain(fresh[b], send[b], decay[b], up) for b in both]
    forth[0].step()
    y_in = []
    for b in both:
        y_in.append(
            vmem_call(
                partial(intra_body, state, b),
                sds((SPAN, inner), F32),
                [bc_all[b], xdt_all[b], s_all[b], st_all[b], seg_col, seg_row],
                after=[forth[0].state, pair_own[2]] if custom else [forth[0].state],
                us=2,
            )
        )
    forth[1].step(after=[forth[0].step(after=y_in)])
    if custom:
        *pair_own, _ = lax.optimization_barrier((*pair_own, forth[1].state))
        pair_pieces = [(v, [(None, 2 * m, 0)]) for m, v in enumerate(pair_own)]
        pair_pieces += [(swap(v, 1), [(None, 2 * m + 1, 0)]) for m, v in enumerate(pair_own)]
    else:
        pair_pieces = [(pair_own[0], [(None, 0, 0)])]
    pair_values, layout2 = layout_of(pair_pieces)
    w_out, w_gate, gating, d_outn = vmem_call(
        partial(dense_body, layout2, inner),
        (sds((inner, depth), BF16), sds((depth, inner), BF16), sds((main, inner), F32), sds((main, inner), F32)),
        [normed, cot] + pair_values,
        idx=idx,
        after=[forth[1].state],
        us=3,
    )
    forth[1].step(after=[gating])
    for hop in range(2, hops):
        forth[1].step(after=[forth[0].step(after=[forth[1].state])])
    carry = [forth[b].state for b in both]

    gated, ebb = [], []
    for b in both:
        gated.append(
            vmem_call(
                partial(gate_body, state, b),
                (
                    sds((SPAN, inner), BF16),
                    sds((SPAN, inner), BF16),
                    sds((SPAN, inner), BF16),
                    sds((SPAN, inner), BF16),
                    sds((SPAN, LANES), F32),
                    sds((state, inner), F32),
                    sds((state, inner), BF16),
                    sds((8, LANES), F32),
                ),
                [y_in[b], carry[b], bc_all[b], s_all[b], seg_col, x_all[b], gating, d_outn, gain_back, head_rows, spread],
                scratch=[pltpu.VMEM((SPAN, inner), F32), pltpu.VMEM((SPAN, inner), F32)],
                after=[ebb[0].state] if ebb else [],
                us=4,
            )
        )
        ebb.append(Chain(gated[b][5], gated[b][6], decay[b], down[::-1]))
        if b == 0:
            ebb[0].step(after=[carry[1]])
    ways = shards if custom else 1
    pair_rows = (inner + 2 * depth) // ways
    halves = lambda r, c: tuple(sds((max(ways // 2, 1), r, c), BF16) for _ in range(min(ways, 2)))
    pair_grads = vmem_call(
        partial(out_grad_body, ways),
        halves(pair_rows, depth)[:1] + tuple(sds((pair_rows, depth), BF16) for _ in range(ways // 2)),
        [gated[0][0], gated[1][0], cot, gated[0][3], gated[1][3], normed],
        idx=idx,
        scratch=[pltpu.VMEM((inner, depth), F32), pltpu.VMEM((depth, inner), F32)],
        mib=20,
        us=4,
    )
    ebb[1].step(after=[ebb[0].step(after=[pair_grads[0]])], us=20)
    inner_back = []
    for b in both:
        inner_back.append(
            vmem_call(
                partial(intra_back_body, state, b),
                (sds((SPAN, inner), F32), sds((SPAN, 2 * state), F32)),
                [bc_all[b], xdt_all[b], gated[b][1], gated[b][2], carry[b], s_all[b], st_all[b], seg_col, seg_row],
                scratch=[pltpu.VMEM((SPAN, SPAN), F32)],
                after=[ebb[1].state],
                us=0.05,
            )
        )
    waits = [inner_back[0][1], inner_back[1][1]]
    if custom:
        first = Reduce(*pair_grads)
        waits.append(first.relay(after=[first.pair(after=[ebb[1].state])] + waits))
    for hop in range(2, hops - 1):
        ebb[1].step(after=[ebb[0].step(after=waits)])

    back = []
    ebb[1].step(after=[ebb[0].step(after=waits)])
    for b in both:
        if b == 1:
            ebb[1].step(after=[back[0][0]])
        back.append(
            vmem_call(
                partial(mixer_back_body, state, b),
                (sds((SPAN, wide), BF16), sds((HALO, wide), BF16), sds((8, conv_chans), F32), sds((8, LANES), F32)),
                [
                    conv_in[b],
                    dt_raw[b],
                    x_all[b],
                    bc_all[b],
                    xdt_all[b],
                    dt_all[b],
                    s_all[b],
                    seg_col,
                    convw,
                    head_rows,
                    inner_back[b][0],
                    inner_back[b][1],
                    gated[b][1],
                    gated[b][4],
                    carry[b],
                    ebb[b].state,
                    spread,
                ],
                scratch=[
                    pltpu.VMEM((HALO + SPAN, WIDE), F32),
                    pltpu.VMEM((2 * HALO + SPAN, WIDE), F32),
                    pltpu.VMEM((2 * HALO + SPAN, WIDE), F32),
                ],
                after=[ebb[1].state] if b == 0 else [],
                us=6,
            )
        )
    d_rows = [back[0][0], back[1][0], back[0][1], back[1][1]]
    waits = [first.spread(z_idx, parts, after=[back[1][0]])] if custom else []
    rest_grads = vmem_call(
        partial(in_grad_body, shards, heads, taps, exact),
        halves(depth // ways, wide),
        d_rows + [normed, back[0][2], back[1][2], back[0][3], back[1][3], gated[0][7], gated[1][7]],
        idx=idx,
        scratch=[pltpu.VMEM((rows, wide), BF16), pltpu.VMEM((depth, wide), F32), pltpu.VMEM((8, LANES), F32)],
        after=waits,
        mib=14,
        us=4,
    )
    out_rows, d_normed_gate = vmem_call(
        out_body,
        (sds((main, depth), BF16), sds((main, depth), F32)),
        [gated[0][0], gated[1][0], gated[0][3], gated[1][3], tokens, w_out, w_gate],
        after=[rest_grads[0]],
        us=0.05,
    )
    if custom:
        rest = Reduce(*rest_grads)
        sent = rest.pair(after=[out_rows])
    in_grad, halo_grad = vmem_call(
        in_back_body,
        (sds((main, depth), F32), sds((batch * HALO, depth), F32)),
        d_rows + [w_all, d_normed_gate, cot, tokens, halo_in, gain_front],
        scratch=[pltpu.VMEM((rows, wide), BF16)],
        after=[sent] if custom else [rest_grads[0]],
        mib=12,
        us=20,
    )
    halo_back = lax.ppermute(halo_grad, "seq", down)
    if custom:
        sent = rest.relay(after=[in_grad])
        sent = first.collect(after=[sent])
        sent = rest.spread(z_idx, parts, after=[sent])
        sent = rest.collect(after=[sent])
        if parts == 4:
            pair_sum = vmem_call(join_body, sds((pair_rows, depth), F32), first.quarters, idx=z_idx, after=[sent])
        else:
            pair_sum = first.total
        rest_parts = rest.quarters if parts == 4 else [rest.total]
    else:
        whole = pair_grads[0][0]
        cuts = ((0, inner), (inner, inner + depth), (inner + depth, inner + 2 * depth))
        shard_sum = lambda v: lax.psum_scatter(v, "fsdp", scatter_dimension=0, tiled=True)
        pair_sum = lax.psum(jnp.concatenate([shard_sum(whole[lo:hi]) for lo, hi in cuts], axis=0).astype(F32), "seq")
        rest_parts = [lax.psum(shard_sum(rest_grads[0][0]).astype(F32), "seq")]
    input_grad = vmem_call(
        halo_add_body, sds(in_grad.shape, F32), [in_grad, halo_back], after=[sent] if custom else []
    ).reshape(1, batch, SPAN, depth)
    width = conv_chans // shards
    grad_in_weight, grad_out_weight, grad_gain, grad_back, grad_conv, grad_bias, head_sums = vmem_call(
        partial(final_body, heads, taps, exact),
        (
            sds((chunk, in_weight.shape[1]), F32),
            sds((rows_out, depth), F32),
            sds((1, chunk), F32),
            sds((1, rows_out), F32),
            sds((taps, width), F32),
            sds((1, width), F32),
            sds((3, heads), F32),
        ),
        [in_weight, line(gain_in), out_weight, line(gain_out), pair_sum] + rest_parts,
        idx=z_idx,
        scratch=[pltpu.VMEM((chunk, wide), F32), pltpu.VMEM((-(-rows_out // LANES) * LANES, LANES), F32)],
    )
    if not exact:
        three = back[0][3] + back[1][3] + gated[0][7] + gated[1][7]
        head_sums = lax.psum(three[:3, :heads], ("fsdp", "seq"))
    return (
        out_rows.reshape(1, batch, SPAN, depth),
        input_grad,
        grad_gain[0],
        grad_in_weight,
        grad_conv.T,
        grad_bias[0],
        head_sums[0],
        head_sums[1],
        head_sums[2],
        grad_back[0],
        grad_out_weight,
    )


def solution(mesh):
    tokens = P("fsdp", None, "seq", None)
    row, matrix = P("fsdp"), P("fsdp", None)
    return jax.shard_map(
        on_device,
        mesh=mesh,
        in_specs=(tokens, P("fsdp", None, None), row, matrix, matrix, row, P(), P(), P(), row, matrix, tokens),
        out_specs=(tokens, tokens, row, matrix, matrix, row, P(), P(), P(), row, matrix),
        check_vma=False,
    )
```

```python
from functools import partial

import jax
import jax.numpy as jnp
from jax import lax
from jax.experimental import pallas as pl
from jax.experimental.pallas import tpu as pltpu
from jax.sharding import PartitionSpec as P

SPAN = 256
HEADDIM = 64
LANES = 128
HALO = 16
WIDE = 256
EPS_NORM = 1e-05
COST = 1e9
OFF = -10000.0
F32 = jnp.float32
BF16 = jnp.bfloat16


def nn(a, b):
    return lax.dot_general(a, b, (((1,), (0,)), ((), ())), preferred_element_type=F32)


def nt(a, b):
    return lax.dot_general(a, b, (((1,), (1,)), ((), ())), preferred_element_type=F32)


def tn(a, b):
    return lax.dot_general(a, b, (((0,), (0,)), ((), ())), preferred_element_type=F32)


def iota(shape, dim):
    return lax.broadcasted_iota(jnp.int32, shape, dim)


def ones_where(cond):
    return jnp.where(cond, 1.0, 0.0)


def split2(v):
    high = v.astype(BF16)
    low = (v - high.astype(F32)).astype(BF16)
    return jnp.concatenate([high, low], axis=1)


def to_heads(v, picks):
    high = v.astype(BF16)
    mid = (v - high.astype(F32)).astype(BF16)
    return nt(high, picks) + nt(mid, picks)


def running_sum(tri, v):
    high = v.astype(BF16)
    rest = v - high.astype(F32)
    mid = rest.astype(BF16)
    low = (rest - mid.astype(F32)).astype(BF16)
    return nn(tri, high) + nn(tri, mid) + nn(tri, low)


def silu_slope(v, sig):
    return sig * (1.0 + v * (1.0 - sig))


def softplus(v):
    return jnp.maximum(v, 0.0) + jnp.log1p(jnp.exp(-jnp.abs(v)))


def row_masks(seg_ref, b, taps):
    here = segs_of(seg_ref, b)
    return [ones_where(seg_ref[pl.ds(HALO - j, SPAN), b : b + 1] == here) for j in range(1, taps)]


def segs_of(seg_ref, b):
    return seg_ref[pl.ds(HALO, SPAN), b : b + 1]


def seg_before(seg_ref, b):
    return seg_ref[HALO - 1 : HALO, b : b + 1]


def seg_last(seg_ref, b):
    return seg_ref[HALO + SPAN - 1 : HALO + SPAN, b : b + 1]


def conv_pre(ext_ref, cols, convw_ref, masks):
    taps = len(masks) + 1
    total = convw_ref[taps : taps + 1, cols] + convw_ref[taps - 1 : taps, cols] * ext_ref[pl.ds(HALO, SPAN), :]
    for j in range(1, taps):
        total = total + convw_ref[taps - 1 - j : taps - j, cols] * (
            ext_ref[pl.ds(HALO - j, SPAN), :] * masks[j - 1]
        )
    return total


def vmem_call(body, out_shape, operands, idx=None, scratch=(), mib=8, after=(), us=0.05, hbm=False):
    vm = pl.BlockSpec(memory_space=pltpu.VMEM)
    smem = [] if idx is None else [idx]
    head, tail = len(smem) + len(operands), len(after)

    def run(*refs):
        body(*refs[:head], *refs[head + tail :])

    return pl.pallas_call(
        run,
        out_shape=out_shape,
        in_specs=[pl.BlockSpec(memory_space=pltpu.SMEM)] * len(smem)
        + [pl.BlockSpec(memory_space=pltpu.HBM) if hbm else vm] * len(operands)
        + [pl.BlockSpec(memory_space=pl.ANY)] * tail,
        out_specs=jax.tree.map(lambda _: vm, out_shape),
        scratch_shapes=list(scratch),
        compiler_params=pltpu.CompilerParams(vmem_limit_bytes=mib * 1024 * 1024),
        cost_estimate=pl.CostEstimate(flops=int(us * COST), bytes_accessed=0, transcendentals=0),
        name=body.func.__name__ if isinstance(body, partial) else body.__name__,
    )(*smem, *operands, *after)


def sds(shape, dtype):
    return jax.ShapeDtypeStruct(shape, dtype)


def prep_body(heads, segs_ref, dtb_ref, alog_ref, skip_ref, spread_ref, seg_ref, heads_ref):
    for c0 in range(0, spread_ref.shape[1], WIDE):
        shape = (2 * LANES, WIDE)
        hit = (iota(shape, 0) & (LANES - 1)) == ((iota(shape, 1) + c0) >> 6)
        spread_ref[:, c0 : c0 + WIDE] = ones_where(hit).astype(BF16)
    seg_ref[...] = segs_ref[...].T[0 : HALO + SPAN, :]
    heads_ref[...] = jnp.zeros(heads_ref.shape, F32)
    heads_ref[0:1, :] = jnp.full((1, LANES), OFF, F32)
    for row, ref in enumerate((dtb_ref, alog_ref, skip_ref)):
        heads_ref[row : row + 1, 0:heads] = ref[...].astype(F32)


def small_rows(taps, width):
    third = -(-width // 3)
    return [
        (t, 3 * t + m, m * third, min(third, width - m * third)) for t in range(taps + 1) for m in range(3)
    ]


def pack_body(heads, inner, *refs):
    given, out_ref, end_ref, sems = refs[:5], refs[5], refs[6], refs[-1]
    copies = [pltpu.make_async_copy(a, b, sems.at[i]) for i, (a, b) in enumerate(zip(given, refs[7:12]))]
    for copy in copies:
        copy.start()
    for copy in copies:
        copy.wait()
    w_ref, gain_ref, conv_ref, bias_ref, back_ref = refs[7:12]
    full = w_ref.shape[1] - inner - heads
    taps, width = conv_ref.shape
    flat = lambda ref: ref[...].astype(F32).reshape(1, ref.shape[0])
    out_ref[:, 0:full] = w_ref[:, inner : inner + full]
    end_ref[...] = jnp.zeros(end_ref.shape, F32)
    end_ref[:, 0:heads] = w_ref[:, inner + full :].astype(F32)
    conv, bias, back = conv_ref[...].astype(F32), flat(bias_ref), flat(back_ref)
    for t, row, first, size in small_rows(taps, width):
        value = conv[t : t + 1] if t < taps else bias
        end_ref[row : row + 1, heads : heads + size] = value[:, first : first + size]
    row = 3 * (taps + 1)
    chunk, half = gain_ref.shape[0], back_ref.shape[0] // 2
    end_ref[row : row + 1, heads : heads + chunk] = flat(gain_ref)
    for m in range(2):
        end_ref[row + 1 + m : row + 2 + m, heads : heads + half] = back[:, m * half : (m + 1) * half]
    out_ref[:, full:] = end_ref[...].astype(BF16)


def unpack(heads, taps, shards, end_ref, gain_ref, conv_ref, back_ref):
    chunk = end_ref.shape[0] // shards
    width, half = conv_ref.shape[1] // shards, back_ref.shape[1] // shards // 2
    conv_ref[taps + 1 :, :] = jnp.zeros((7 - taps, conv_ref.shape[1]), F32)
    for i in range(shards):
        at = i * chunk
        for t, row, first, size in small_rows(taps, width):
            conv_ref[t : t + 1, i * width + first : i * width + first + size] = end_ref[
                at + row : at + row + 1, heads : heads + size
            ]
        row = at + 3 * (taps + 1)
        gain_ref[:, i * chunk : (i + 1) * chunk] = end_ref[row : row + 1, heads : heads + chunk]
        for m in range(2):
            first = (2 * i + m) * half
            back_ref[:, first : first + half] = end_ref[row + 1 + m : row + 2 + m, heads : heads + half]


def proj_body(layout, batch, heads, shards, state, *refs):
    idx_ref, tokens_ref, halo_ref, heads_ref, seg_ref, spread_ref = refs[:6]
    pieces = refs[6 : 6 + len(layout)]
    (w_ref, normed_ref, gain_ref, convw_ref, back_ref, convin_ref, dtraw_ref, x_ref, bc_ref, xdt_ref, dt_ref, s_ref, st_ref, fresh_ref, send_ref, decay_ref) = refs[
        6 + len(layout) : 22 + len(layout)
    ]
    ext_ref, tail_ref, end_ref = refs[22 + len(layout) :]
    inner = heads * HEADDIM
    chunk = w_ref.shape[0] // (1 if len(layout) == 1 else 8)

    def store(first, off, view):
        w_ref[pl.ds(pl.multiple_of(first, HALO), view.shape[0]), :] = view[...]

    put_pieces(layout, pieces, idx_ref[0], chunk, store)
    conv_chans = inner + 2 * state
    taps = 4
    end_ref[...] = w_ref[:, conv_chans:].astype(F32)
    unpack(heads, taps, shards, end_ref, gain_ref, convw_ref, back_ref)
    w_ref[:, conv_chans:] = jnp.where(iota(end_ref.shape, 1) < heads, end_ref[...], 0.0).astype(BF16)
    main = tokens_ref.shape[0]
    for ref, first in ((tokens_ref, 0), (halo_ref, main)):
        v = ref[...].astype(F32)
        scale = lax.rsqrt(jnp.mean(v * v, axis=1, keepdims=True) + EPS_NORM)
        normed_ref[pl.ds(first, ref.shape[0]), :] = (v * scale * gain_ref[...]).astype(BF16)
    normed = normed_ref[...]
    raw = nn(normed, w_ref[:, conv_chans : conv_chans + LANES])
    tri = ones_where(iota((SPAN, SPAN), 0) >= iota((SPAN, SPAN), 1)).astype(BF16)
    all_masks = []
    for b in range(batch):
        all_masks.append(row_masks(seg_ref, b, taps))
        dt_raw = raw[b * SPAN : (b + 1) * SPAN].astype(BF16).astype(F32)
        dtraw_ref[b][...] = dt_raw
        dt = softplus(dt_raw + heads_ref[0:1, :])
        dt_ref[b][...] = dt
        rate = -jnp.exp(heads_ref[1:2, :])
        logs = running_sum(tri, dt * rate)
        s_ref[b][...] = logs
        st_ref[b][...] = logs.T
        last = logs[SPAN - 1 : SPAN, :]
        same_last = ones_where(segs_of(seg_ref, b) == seg_last(seg_ref, b))
        tail_ref[b] = split2(jnp.exp(last - logs) * same_last)
        keep = ones_where(seg_last(seg_ref, b) == seg_before(seg_ref, b))
        factor = jnp.broadcast_to(jnp.exp(last) * keep, (8, LANES))
        for c0 in range(0, inner, WIDE):
            decay_ref[b][:, c0 : c0 + WIDE] = nn(split2(factor), spread_ref[:, c0 : c0 + WIDE])
    for c0 in [inner] + list(range(0, inner, WIDE)):
        cols = slice(c0, c0 + WIDE)
        projected = nn(normed, w_ref[:, cols]).astype(BF16)
        for b in range(batch):
            halo0 = batch * SPAN + b * HALO
            top = projected[halo0 : halo0 + HALO]
            rest = projected[b * SPAN : (b + 1) * SPAN]
            convin_ref[b][0:HALO, cols] = top
            convin_ref[b][HALO : HALO + SPAN, cols] = rest
            ext_ref[0:HALO, :] = top.astype(F32)
            ext_ref[HALO : HALO + SPAN, :] = rest.astype(F32)
            pre = conv_pre(ext_ref, cols, convw_ref, all_masks[b])
            act = pre * jax.nn.sigmoid(pre)
            if c0 == inner:
                bc_ref[b][...] = act.astype(BF16)
            else:
                spread = spread_ref[:, cols]
                x_ref[b][:, cols] = act
                xdt = (nn(split2(dt_ref[b][...]), spread) * act).astype(BF16)
                xdt_ref[b][:, cols] = xdt
                xt = (nn(tail_ref[b], spread) * xdt.astype(F32)).astype(BF16)
                fresh = tn(bc_ref[b][:, 0:state], xt)
                fresh_ref[b][:, cols] = fresh
                send_ref[b][:, cols] = fresh.astype(BF16)


def inside_mask(seg_ref, segr_ref, b, flipped):
    rows, cols = iota((SPAN, SPAN), 0), iota((SPAN, SPAN), 1)
    ordered = rows <= cols if flipped else rows >= cols
    return ordered & (segs_of(seg_ref, b) == segr_ref[b : b + 1, :])


def head_halves(block):
    low = iota(block.shape, 1) < HEADDIM
    zero = jnp.zeros_like(block)
    return jnp.where(low, block, zero), jnp.where(low, zero, block)


def intra_body(state, b, bc_ref, xdt_ref, s_ref, st_ref, seg_ref, segr_ref, y_ref):
    scores = nt(bc_ref[:, state : 2 * state], bc_ref[:, 0:state])
    scores = jnp.where(inside_mask(seg_ref, segr_ref, b, False), scores, 0.0)
    for pair in range(xdt_ref.shape[1] // LANES):
        cols = slice(pair * LANES, (pair + 1) * LANES)
        total = None
        for half, values in enumerate(head_halves(xdt_ref[:, cols])):
            h = 2 * pair + half
            decay = jnp.exp(jnp.minimum(s_ref[:, h : h + 1] - st_ref[h : h + 1, :], 0.0))
            part = nn((scores * decay).astype(BF16), values)
            total = part if total is None else total + part
        y_ref[:, cols] = total


def dense_body(layout, inner, *refs):
    idx_ref, normed_ref, cot_ref = refs[:3]
    pieces = refs[3 : 3 + len(layout)]
    wout_ref, wgate_ref, gating_ref, dout_ref, turned_ref = refs[3 + len(layout) :]
    depth = wgate_ref.shape[0]
    shards = 1 if len(layout) == 1 else 8
    ochunk, gchunk = inner // shards, depth // shards
    half_cols = inner // 2
    def store(owner, off, view):
        wout_ref[pl.ds(pl.multiple_of(owner * ochunk, HALO), ochunk), :] = view[0:ochunk, :]
        for side in range(2):
            wgate_ref[
                pl.ds(pl.multiple_of(owner * gchunk, HALO), gchunk), side * half_cols : (side + 1) * half_cols
            ] = view[ochunk + side * gchunk : ochunk + (side + 1) * gchunk, :]

    put_pieces(layout, pieces, idx_ref[0], 1, store)
    for r0 in range(0, depth, WIDE):
        turned_ref[r0 : r0 + WIDE, :] = normed_ref[:, r0 : r0 + WIDE].T
    normed = normed_ref[0 : cot_ref.shape[0], :]
    cot = cot_ref[...]
    for c0 in range(0, inner, WIDE):
        gating_ref[:, c0 : c0 + WIDE] = nn(normed, wgate_ref[:, c0 : c0 + WIDE])
        dout_ref[:, c0 : c0 + WIDE] = nt(cot, wout_ref[c0 : c0 + WIDE, :])


def gate_body(state, b, *refs):
    (yin_ref, carry_ref, bc_ref, s_ref, seg_ref, x_ref, gating_ref, dout_ref, gain_ref, heads_ref, spread_ref) = refs[:11]
    (outn_ref, dy_ref, ey_ref, dgat_ref, rowterm_ref, grad_ref, send_ref, small_ref) = refs[11:19]
    y_ref, gated_ref = refs[19:]
    inner = x_ref.shape[1]
    rows = pl.ds(b * SPAN, SPAN)
    c_mat = bc_ref[:, state : 2 * state]
    carried = ones_where(segs_of(seg_ref, b) == seg_before(seg_ref, b))
    factor = split2(jnp.exp(s_ref[...]) * carried)
    skip = split2(jnp.broadcast_to(heads_ref[2:3, :], (8, LANES)))
    sumsq = jnp.zeros((SPAN, 1), F32)
    sumeg = jnp.zeros((SPAN, 1), F32)
    for c0 in range(0, inner, WIDE):
        cols = slice(c0, c0 + WIDE)
        spread = spread_ref[:, cols]
        y = yin_ref[:, cols] + nn(factor, spread) * nn(c_mat, carry_ref[:, cols])
        y_ref[:, cols] = y
        mixed = (y + nn(skip, spread)[0:1, :] * x_ref[:, cols]).astype(BF16).astype(F32)
        gate = gating_ref[rows, cols]
        gated = mixed * (gate * jax.nn.sigmoid(gate))
        gated_ref[:, cols] = gated
        sumsq = sumsq + jnp.sum(gated * gated, axis=1, keepdims=True)
        sumeg = sumeg + jnp.sum(dout_ref[rows, cols] * gain_ref[:, cols] * gated, axis=1, keepdims=True)
    r = lax.rsqrt(sumsq / inner + EPS_NORM)
    coef = r * r * r * (sumeg / inner)
    terms = jnp.zeros((SPAN, LANES), F32)
    skips = jnp.zeros((8, LANES), F32)
    for c0 in range(0, inner, WIDE):
        cols = slice(c0, c0 + WIDE)
        spread = spread_ref[:, cols]
        gated = gated_ref[:, cols]
        gain = gain_ref[:, cols]
        dout = dout_ref[rows, cols]
        normal = gated * r
        outn_ref[:, cols] = (normal * gain).astype(BF16)
        y = y_ref[:, cols]
        x = x_ref[:, cols]
        d_gated = r * (dout * gain) - gated * coef
        gate = gating_ref[rows, cols]
        sig = jax.nn.sigmoid(gate)
        mixed = (y + nn(skip, spread)[0:1, :] * x).astype(BF16).astype(F32)
        dgat_ref[:, cols] = (d_gated * mixed * silu_slope(gate, sig)).astype(BF16)
        dy = (d_gated * (gate * sig)).astype(BF16)
        dy_ref[:, cols] = dy
        dyf = dy.astype(F32)
        ey = (nn(factor, spread) * dyf).astype(BF16)
        ey_ref[:, cols] = ey
        terms = terms + to_heads(dyf * y, spread_ref[0:LANES, cols])
        grad = tn(c_mat, ey)
        grad_ref[:, cols] = grad
        send_ref[:, cols] = grad.astype(BF16)
        skips = skips + to_heads(jnp.broadcast_to(jnp.sum(dyf * x, axis=0, keepdims=True), (8, WIDE)), spread_ref[0:LANES, cols])
    rowterm_ref[...] = terms
    small_ref[...] = jnp.where(iota(skips.shape, 0) == 2, skips, 0.0)


def intra_back_body(state, b, *refs):
    (bc_ref, xdt_ref, dy_ref, ey_ref, carry_ref, s_ref, st_ref, seg_ref, segr_ref) = refs[:9]
    dxdt_ref, dbc_ref = refs[9:11]
    acc_ref = refs[11]
    b_mat = bc_ref[:, 0:state]
    c_mat = bc_ref[:, state : 2 * state]
    mask = inside_mask(seg_ref, segr_ref, b, True)
    scores = jnp.where(mask, nt(b_mat, c_mat), 0.0)
    for pair in range(xdt_ref.shape[1] // LANES):
        cols = slice(pair * LANES, (pair + 1) * LANES)
        total = None
        dy_block = dy_ref[:, cols]
        for half, (values, grads) in enumerate(zip(head_halves(xdt_ref[:, cols]), head_halves(dy_block))):
            h = 2 * pair + half
            decay = jnp.exp(jnp.minimum(st_ref[h : h + 1, :] - s_ref[:, h : h + 1], 0.0))
            part = nn((scores * decay).astype(BF16), grads)
            total = part if total is None else total + part
            d_weight = nt(values, dy_block) * decay
            if h == 0:
                acc_ref[...] = d_weight
            else:
                acc_ref[...] += d_weight
        dxdt_ref[:, cols] = total
    d_scores = jnp.where(mask, acc_ref[...], 0.0).astype(BF16)
    dbc_ref[:, 0:state] = nn(d_scores, c_mat)
    dbc_ref[:, state : 2 * state] = tn(d_scores, b_mat) + nt(ey_ref[...], carry_ref[...])


def mixer_back_body(state, b, *refs):
    (convin_ref, dtraw_ref, x_ref, bc_ref, xdt_ref, dt_ref, s_ref, seg_ref, convw_ref, heads_ref) = refs[:10]
    (dxdt_ref, dbc_ref, dy_ref, rowterm_ref, carry_ref, dcarry_ref, spread_ref) = refs[10:17]
    (dmain_ref, dhalo_ref, small_ref, hsmall_ref) = refs[17:21]
    ext_ref, dpre_ref, dconv_ref = refs[21:]
    inner = x_ref.shape[1]
    taps = 4
    conv_chans = inner + 2 * state
    masks = row_masks(seg_ref, b, taps)
    b_mat = bc_ref[:, 0:state]
    logs = s_ref[...]
    dt = dt_ref[...]
    rate = -jnp.exp(heads_ref[1:2, :])
    last = logs[SPAN - 1 : SPAN, :]
    same_last = ones_where(segs_of(seg_ref, b) == seg_last(seg_ref, b))
    keep = ones_where(seg_last(seg_ref, b) == seg_before(seg_ref, b))
    tail = split2(jnp.exp(last - logs) * same_last)
    dt2 = split2(dt)
    skip = split2(jnp.broadcast_to(heads_ref[2:3, :], (8, LANES)))
    col_term = jnp.zeros((SPAN, LANES), F32)
    direct = jnp.zeros((SPAN, LANES), F32)
    last_term = jnp.zeros((8, LANES), F32)
    d_b = dbc_ref[:, 0:state]
    dconv_ref[HALO + SPAN : HALO + SPAN + HALO, :] = jnp.zeros((HALO, WIDE), F32)
    dpre_ref[0:HALO, :] = jnp.zeros((HALO, WIDE), F32)
    dpre_ref[HALO + SPAN : HALO + SPAN + HALO, :] = jnp.zeros((HALO, WIDE), F32)
    small_ref[taps + 1 : 8, :] = jnp.zeros((7 - taps, conv_chans), F32)

    def conv_back(cols, d_act):
        ext_ref[...] = convin_ref[:, cols].astype(F32)
        pre = conv_pre(ext_ref, cols, convw_ref, masks)
        d_pre = d_act * silu_slope(pre, jax.nn.sigmoid(pre))
        small_ref[taps : taps + 1, cols] = jnp.sum(d_pre, axis=0, keepdims=True)
        small_ref[taps - 1 : taps, cols] = jnp.sum(d_pre * ext_ref[pl.ds(HALO, SPAN), :], axis=0, keepdims=True)
        dpre_ref[pl.ds(HALO, SPAN), :] = d_pre
        total = convw_ref[taps - 1 : taps, cols] * dpre_ref[pl.ds(0, HALO + SPAN), :]
        for j in range(1, taps):
            masked = d_pre * masks[j - 1]
            small_ref[taps - 1 - j : taps - j, cols] = jnp.sum(
                masked * ext_ref[pl.ds(HALO - j, SPAN), :], axis=0, keepdims=True
            )
            dconv_ref[pl.ds(0, HALO), :] = jnp.zeros((HALO, WIDE), F32)
            dconv_ref[pl.ds(HALO, SPAN), :] = masked
            total = total + convw_ref[taps - 1 - j : taps - j, cols] * dconv_ref[pl.ds(j, HALO + SPAN), :]
        total = total.astype(BF16)
        dhalo_ref[:, cols] = total[0:HALO]
        dmain_ref[:, cols] = total[HALO : HALO + SPAN]

    for c0 in range(0, inner, WIDE):
        cols = slice(c0, c0 + WIDE)
        spread = spread_ref[:, cols]
        picks = spread_ref[0:LANES, cols]
        d_carry = dcarry_ref[:, cols]
        tails = nn(tail, spread)
        xdt = xdt_ref[:, cols].astype(F32)
        d_tail = tails * nn(b_mat, d_carry)
        d_xdt = dxdt_ref[:, cols] + d_tail
        x = x_ref[:, cols]
        col_term = col_term + to_heads(xdt * d_xdt, picks)
        direct = direct + to_heads(x * d_xdt, picks)
        from_tail = jnp.sum(xdt * d_tail, axis=0, keepdims=True)
        through = jnp.sum(d_carry.astype(F32) * carry_ref[:, cols].astype(F32), axis=0, keepdims=True)
        both = to_heads(jnp.concatenate([from_tail, through, jnp.zeros((6, WIDE), F32)], axis=0), picks)
        last_term = last_term + both
        d_b = d_b + nt((tails * xdt).astype(BF16), d_carry)
        d_x = nn(dt2, spread) * d_xdt + nn(skip, spread)[0:1, :] * dy_ref[:, cols].astype(F32)
        conv_back(cols, d_x)
    conv_back(slice(inner, conv_chans), jnp.concatenate([d_b, dbc_ref[:, state : 2 * state]], axis=1))
    at_end = last_term[0:1, :] + last_term[1:2, :] * (jnp.exp(last) * keep)
    upper = ones_where(iota((SPAN, SPAN), 0) <= iota((SPAN, SPAN), 1)).astype(BF16)
    d_logs = running_sum(upper, rowterm_ref[...] - col_term) + at_end
    d_dt = direct + rate * d_logs
    d_raw = d_dt * jax.nn.sigmoid(dtraw_ref[...] + heads_ref[0:1, :])
    dmain_ref[:, conv_chans : conv_chans + LANES] = d_raw.astype(BF16)
    dhalo_ref[:, conv_chans : conv_chans + LANES] = jnp.zeros((HALO, LANES), BF16)
    hsmall_ref[0:1, :] = jnp.sum(d_raw, axis=0, keepdims=True)
    hsmall_ref[1:2, :] = jnp.sum(dt * d_logs, axis=0, keepdims=True) * rate
    hsmall_ref[2:8, :] = jnp.zeros((6, LANES), F32)


def out_grad_body(shards, *refs):
    (idx_ref, on0_ref, on1_ref, cot_ref, dg0_ref, dg1_ref, normed_ref) = refs[:7]
    outs = refs[7:-2]
    gout_ref, ggate_ref = refs[-2:]
    main = cot_ref.shape[0]
    inner, width = gout_ref.shape
    outn = jnp.concatenate([on0_ref[...], on1_ref[...]], axis=0)
    dgat = jnp.concatenate([dg0_ref[...], dg1_ref[...]], axis=0)
    normed = normed_ref[0:main, :]
    gout_ref[...] = tn(outn, cot_ref[...])
    for c0 in range(0, inner, width):
        ggate_ref[:, c0 : c0 + width] = tn(normed, dgat[:, c0 : c0 + width])
    ochunk, gchunk = inner // shards, width // shards
    for k in range(shards):
        owner = idx_ref[0] ^ k
        ref = outs[0].at[k // 2] if k % 2 == 0 else outs[1 + k // 2]
        ref[0:ochunk, :] = gout_ref[pl.ds(pl.multiple_of(owner * ochunk, HALO), ochunk), :].astype(BF16)
        for side in range(2):
            ref[ochunk + side * gchunk : ochunk + (side + 1) * gchunk, :] = ggate_ref[
                pl.ds(pl.multiple_of(owner * gchunk, HALO), gchunk), side * width : (side + 1) * width
            ].astype(BF16)


def out_body(on0_ref, on1_ref, xin_ref, wout_ref, lout_ref):
    for b, outn_ref in enumerate((on0_ref, on1_ref)):
        rows = slice(b * SPAN, (b + 1) * SPAN)
        lout_ref[rows, :] = (xin_ref[rows, :].astype(F32) + nn(outn_ref[...], wout_ref[...])).astype(BF16)


def join_rows(m0_ref, m1_ref, h0_ref, h1_ref, all_ref):
    all_ref[0:SPAN, :] = m0_ref[...]
    all_ref[SPAN : 2 * SPAN, :] = m1_ref[...]
    all_ref[2 * SPAN : 2 * SPAN + HALO, :] = h0_ref[...]
    all_ref[2 * SPAN + HALO : 2 * SPAN + 2 * HALO, :] = h1_ref[...]


def in_grad_body(shards, heads, taps, exact, *refs):
    idx_ref, m0_ref, m1_ref, h0_ref, h1_ref, normed_ref = refs[:6]
    conv0_ref, conv1_ref, head0_ref, head1_ref, skip0_ref, skip1_ref = refs[6:12]
    outs = refs[12:-3]
    all_ref, grad_ref, line_ref = refs[-3:]
    join_rows(m0_ref, m1_ref, h0_ref, h1_ref, all_ref)
    depth, wide = grad_ref.shape
    for c0 in range(0, wide, 384):
        grad_ref[:, c0 : c0 + 384] = nn(normed_ref[...], all_ref[:, c0 : c0 + 384])
    conv = conv0_ref[...] + conv1_ref[...]
    three = head0_ref[...] + head1_ref[...] + skip0_ref[...] + skip1_ref[...]
    chunk, width = depth // shards, conv.shape[1] // shards
    lane0 = wide - LANES + heads
    for i in range(shards):
        for t, row, first, size in small_rows(taps, width):
            at = i * chunk + row
            grad_ref[at : at + 1, lane0 : lane0 + size] = conv[t : t + 1, i * width + first : i * width + first + size]
    if exact:
        line_ref[...] = jnp.zeros(line_ref.shape, F32)
        for m in range(3):
            line_ref[0:1, (m + 1) * heads : (m + 2) * heads] = three[m : m + 1, 0:heads]
        value = line_ref[0:1, :]
        high = value.astype(BF16).astype(F32)
        last = slice(wide - LANES, wide)
        rows = iota((2 * exact, LANES), 0)
        mine = jnp.where(rows == 2 * idx_ref[1], high, 0.0) + jnp.where(rows == 2 * idx_ref[1] + 1, value - high, 0.0)
        for i in range(shards):
            at = slice(i * chunk + 3 * (taps + 1) + 1, i * chunk + 3 * (taps + 1) + 1 + 2 * exact)
            grad_ref[at, last] = grad_ref[at, last] + mine
    ways = 1 if len(outs) == 1 else shards
    part = depth // ways
    for k in range(ways):
        first = pl.multiple_of((idx_ref[0] ^ k) * part, HALO)
        outs[k % 2][k // 2] = grad_ref[pl.ds(first, part), :].astype(BF16)


def in_back_body(*refs):
    m0_ref, m1_ref, h0_ref, h1_ref, w_ref, dg0_ref, dg1_ref, wgate_ref, cot_ref, xin_ref, halo_ref, gain_ref = refs[:12]
    igrad_ref, hgrad_ref, all_ref = refs[12:]
    main = cot_ref.shape[0]
    join_rows(m0_ref, m1_ref, h0_ref, h1_ref, all_ref)
    d_normed = nt(all_ref[...], w_ref[...])
    gain = gain_ref[...]

    def back(dn, v):
        q = lax.rsqrt(jnp.mean(v * v, axis=1, keepdims=True) + EPS_NORM)
        e = dn * gain
        return q * e - v * (q * q * q * jnp.mean(e * v, axis=1, keepdims=True))

    for b, dgat_ref in enumerate((dg0_ref, dg1_ref)):
        rows = slice(b * SPAN, (b + 1) * SPAN)
        d_both = d_normed[rows] + nt(dgat_ref[...], wgate_ref[...])
        igrad_ref[rows, :] = cot_ref[rows, :].astype(F32) + back(d_both, xin_ref[rows, :].astype(F32))
    hgrad_ref[...] = back(d_normed[main:], halo_ref[...].astype(F32))


def xor_pairs(size, k):
    return [(i, i ^ k) for i in range(size)]


def stack_body(*refs):
    out_ref = refs[-1]
    for i, ref in enumerate(refs[:-1]):
        out_ref[i] = ref[...]


def rows_body(top_ref, low_ref, out_ref):
    half = top_ref.shape[0]
    out_ref[0:half, :] = top_ref[...]
    out_ref[half:, :] = low_ref[...]


def stack(parts, after=()):
    return vmem_call(stack_body, sds((len(parts),) + parts[0].shape, BF16), parts, after=after)


def layout_of(pieces):
    return [v for v, _ in pieces], tuple(places for _, places in pieces)


def put_pieces(layout, refs, idx, chunk, store):
    for ref, places in zip(refs, layout):
        for sub, k, off in places:
            view = ref if sub is None else ref.at[sub]
            store((idx ^ k) * chunk + off, off, view)


def combine_body(last, *refs):
    if last:
        got_ref, carry_ref, out_ref = refs
        out_ref[...] = got_ref[...] + carry_ref[...]
        return
    first = len(refs) == 5
    got_ref, fresh_ref, decay_ref = refs[:3]
    out_ref, send_ref = refs[-2:]
    state = got_ref[...] if first else got_ref[...] + refs[3][...]
    out_ref[...] = state
    send_ref[...] = (fresh_ref[...] + decay_ref[0:1, :] * state.astype(F32)).astype(BF16)


class Chain:
    def __init__(self, fresh, send, decay, pairs):
        self.fresh, self.send, self.decay, self.pairs = fresh, send, decay, pairs
        self.state = None
        self.hop = 0
        self.start()

    def start(self):
        self.got = lax.ppermute(self.send, "seq", [self.pairs[self.hop]])

    def step(self, after=(), us=0.05):
        shape = sds(self.got.shape, BF16)
        prior = [] if self.state is None else [self.state]
        if self.hop == len(self.pairs) - 1:
            if prior:
                self.state = vmem_call(partial(combine_body, True), shape, [self.got] + prior, after=after)
            else:
                self.state = self.got
            return self.state
        self.state, self.send = vmem_call(
            partial(combine_body, False),
            (shape, shape),
            [self.got, self.fresh, self.decay] + prior,
            after=after,
            us=us,
        )
        self.hop += 1
        self.start()
        return self.state


def swap(v, k):
    return lax.ppermute(v, "fsdp", xor_pairs(8, k))


def pair_body(even_ref, *refs):
    own_ref, side_ref, down_ref, top_ref, low_ref = refs[-5:]
    got = refs[:-5] if len(refs) > 6 else [refs[0].at[i] for i in range(4)]
    half = top_ref.shape[0]
    add = lambda s: even_ref[s].astype(F32) + got[s][...].astype(F32)
    far = add(3).astype(BF16)
    top_ref[...] = far[0:half]
    low_ref[...] = far[half:]
    own_ref[...] = add(0)
    side_ref[...] = add(1)
    down_ref[...] = add(2)


def relay_body(side_ref, down_ref, top_ref, low_ref, side_out, down_out):
    half = top_ref.shape[0]
    side_out[0:half, :] = side_ref[0:half, :].astype(BF16)
    side_out[half:, :] = (side_ref[half:, :] + low_ref[...].astype(F32)).astype(BF16)
    down_out[0:half, :] = (down_ref[0:half, :] + top_ref[...].astype(F32)).astype(BF16)
    down_out[half:, :] = down_ref[half:, :].astype(BF16)


class Reduce:
    def __init__(self, even, *odd):
        self.even, self.stage = even, 0
        self.got = [swap(v, 1) for v in odd]

    def pair(self, after=()):
        _, rows, cols = self.even.shape
        full, half = sds((rows, cols), F32), sds((rows // 2, cols), BF16)
        self.own, self.side, self.down, top, low = vmem_call(
            pair_body, (full, full, full, half, half), [self.even] + self.got, after=after
        )
        self.top, self.low = swap(top, 2), swap(low, 4)
        return self.own

    def relay(self, after=()):
        shape = sds(self.own.shape, BF16)
        side, down = vmem_call(relay_body, (shape, shape), [self.side, self.down, self.top, self.low], after=after)
        self.side, self.down = swap(side, 2), swap(down, 4)
        return side

    def step(self, z, parts, after=()):
        rows, cols = self.own.shape
        along = lambda v, k: lax.ppermute(v, "seq", xor_pairs(parts, k))
        stage, self.stage = self.stage, self.stage + 1
        if parts != 4:
            if stage == 0:
                total = self.own + self.side.astype(F32) + self.down.astype(F32)
                self.total = lax.psum(total, "seq")
            return self.total
        f32, bf16 = lambda n: sds((n, cols), F32), lambda n: sds((n, cols), BF16)
        whole, half = pltpu.VMEM((rows, cols), F32), pltpu.VMEM((rows // 2, cols), F32)
        if stage == 0:
            given = [self.own, self.side, self.down]
            self.keep, send = vmem_call(
                halve_body, (f32(rows // 2), bf16(rows // 2)), given, idx=z, scratch=[whole], after=after
            )
            self.got = along(send, 1)
            return self.keep
        if stage == 1:
            given = [self.keep, self.got]
            self.keep, send = vmem_call(
                fold_body, (f32(rows // 4), bf16(rows // 4)), given, idx=z, scratch=[half], after=after
            )
            self.got = along(send, 2)
            return self.keep
        if stage == 2:
            self.keep = vmem_call(total_body, bf16(rows // 4), [self.keep, self.got], after=after)
            self.got = along(self.keep, 2)
            return self.keep
        if stage == 3:
            given = [self.keep, self.got]
            self.keep = vmem_call(partial(unfold_body, 1), bf16(rows // 2), given, idx=z, scratch=[half], after=after)
            self.got = along(self.keep, 1)
            return self.keep
        given = [self.keep, self.got]
        return vmem_call(partial(unfold_body, 0), f32(rows), given, idx=z, scratch=[whole], after=after)

    def spread(self, z, parts, after=()):
        rows, cols = self.own.shape
        self.parts, self.z = parts, z
        if parts != 4:
            total = self.own + self.side.astype(F32) + self.down.astype(F32)
            self.total = lax.psum(total, "seq")
            return self.total
        cut = sds((rows // 4, cols), BF16)
        mine, *others = vmem_call(
            spread_body,
            (sds((rows // 4, cols), F32), cut, cut, cut),
            [self.own, self.side, self.down],
            idx=z,
            scratch=[pltpu.VMEM((rows, cols), F32)],
            after=after,
        )
        self.mine = mine
        self.others = [lax.ppermute(v, "seq", xor_pairs(4, k + 1)) for k, v in enumerate(others)]
        return mine

    def collect(self, after=()):
        if self.parts != 4:
            return self.total
        part = vmem_call(collect_body, sds(self.mine.shape, BF16), [self.mine] + self.others, after=after, us=30)
        self.quarters = [part] + [lax.ppermute(part, "seq", xor_pairs(4, k)) for k in (1, 2, 3)]
        return part


def halve_body(z_ref, own_ref, side_ref, down_ref, keep_ref, send_ref, all_ref):
    all_ref[...] = own_ref[...] + side_ref[...].astype(F32) + down_ref[...].astype(F32)
    rows = keep_ref.shape[0]
    bit = z_ref[0] & 1
    keep_ref[...] = all_ref[pl.ds(pl.multiple_of(bit * rows, 8), rows), :]
    send_ref[...] = all_ref[pl.ds(pl.multiple_of((1 - bit) * rows, 8), rows), :].astype(BF16)


def fold_body(z_ref, half_ref, got_ref, keep_ref, send_ref, all_ref):
    all_ref[...] = half_ref[...] + got_ref[...].astype(F32)
    rows = keep_ref.shape[0]
    bit = (z_ref[0] >> 1) & 1
    keep_ref[...] = all_ref[pl.ds(pl.multiple_of(bit * rows, 8), rows), :]
    send_ref[...] = all_ref[pl.ds(pl.multiple_of((1 - bit) * rows, 8), rows), :].astype(BF16)


def total_body(keep_ref, got_ref, out_ref):
    out_ref[...] = (keep_ref[...] + got_ref[...].astype(F32)).astype(BF16)


def unfold_body(shift, z_ref, mine_ref, got_ref, out_ref, all_ref):
    rows = mine_ref.shape[0]
    bit = (z_ref[0] >> shift) & 1
    all_ref[pl.ds(pl.multiple_of(bit * rows, 8), rows), :] = mine_ref[...].astype(F32)
    all_ref[pl.ds(pl.multiple_of((1 - bit) * rows, 8), rows), :] = got_ref[...].astype(F32)
    out_ref[...] = all_ref[...].astype(out_ref.dtype)


def spread_body(z_ref, own_ref, side_ref, down_ref, mine_ref, one_ref, two_ref, three_ref, all_ref):
    all_ref[...] = own_ref[...] + side_ref[...].astype(F32) + down_ref[...].astype(F32)
    rows = mine_ref.shape[0]
    for k, ref in enumerate((mine_ref, one_ref, two_ref, three_ref)):
        first = pl.multiple_of((z_ref[0] ^ k) * rows, 8)
        ref[...] = all_ref[pl.ds(first, rows), :].astype(ref.dtype)


def collect_body(mine_ref, one_ref, two_ref, three_ref, out_ref):
    total = mine_ref[...] + one_ref[...].astype(F32) + two_ref[...].astype(F32) + three_ref[...].astype(F32)
    out_ref[...] = total.astype(BF16)


def final_body(heads, taps, sources, idx_ref, *refs):
    w_ref, gain_ref, wout_ref, back_ref, pair_ref = refs[:5]
    quarters = refs[5:-9]
    grad_ref, gout_ref, ggain_ref, gback_ref, conv_ref, bias_ref, heads_ref = refs[-9:-2]
    rest_ref, sums_ref = refs[-2:]
    rows = quarters[0].shape[0]
    for k, ref in enumerate(quarters):
        first = pl.multiple_of((idx_ref[0] ^ k) * rows, 8) if len(quarters) > 1 else 0
        rest_ref[pl.ds(first, rows), :] = ref[...].astype(F32)
    chunk, half = grad_ref.shape[0], pair_ref.shape[1]
    rows_out = gout_ref.shape[0]
    grad_ref[:, 0:half] = pair_ref[rows_out : rows_out + chunk, :]
    grad_ref[:, half : 2 * half] = pair_ref[rows_out + chunk : rows_out + 2 * chunk, :]
    grad_ref[:, 2 * half :] = rest_ref[:, 0 : grad_ref.shape[1] - 2 * half]
    gout_ref[...] = pair_ref[0:rows_out, :]
    total = jnp.sum(w_ref[...].astype(F32) * grad_ref[...], axis=1, keepdims=True)
    sums_ref[0:chunk, :] = jnp.broadcast_to(total, (chunk, LANES))
    ggain_ref[...] = sums_ref[...].T[0:1, 0:chunk] / gain_ref[...].astype(F32)
    total = jnp.sum(wout_ref[...].astype(F32) * gout_ref[...], axis=1, keepdims=True)
    sums_ref[0:rows_out, :] = jnp.broadcast_to(total, (rows_out, LANES))
    gback_ref[...] = sums_ref[...].T[0:1, 0:rows_out] / back_ref[...].astype(F32)
    width = conv_ref.shape[1]
    lane0 = rest_ref.shape[1] - LANES + heads
    for t, row, first, size in small_rows(taps, width):
        value = rest_ref[row : row + 1, lane0 : lane0 + size]
        if t < taps:
            conv_ref[t : t + 1, first : first + size] = value
        else:
            bias_ref[:, first : first + size] = value
    if sources:
        row = 3 * (taps + 1) + 1
        total = jnp.sum(rest_ref[row : row + 2 * sources, rest_ref.shape[1] - LANES :], axis=0, keepdims=True)
        for m in range(3):
            heads_ref[m : m + 1, :] = total[:, (m + 1) * heads : (m + 2) * heads]
    else:
        heads_ref[...] = jnp.zeros(heads_ref.shape, F32)


def halo_add_body(grad_ref, halo_ref, out_ref):
    out_ref[...] = grad_ref[...]
    for b in range(out_ref.shape[0] // SPAN):
        rows = slice((b + 1) * SPAN - HALO, (b + 1) * SPAN)
        out_ref[rows, :] = grad_ref[rows, :] + halo_ref[b * HALO : (b + 1) * HALO, :]


def on_device(
    layer_input,
    segment_ids,
    gain_in,
    in_weight,
    conv_weight,
    conv_bias,
    dt_bias,
    a_log,
    skip_gain,
    gain_out,
    out_weight,
    cotangent,
):
    shards, parts = lax.axis_size("fsdp"), lax.axis_size("seq")
    at_fsdp, at_seq = lax.axis_index("fsdp"), lax.axis_index("seq")
    _, batch, part_len, depth = layer_input.shape
    heads = dt_bias.shape[0]
    inner = heads * HEADDIM
    taps = conv_weight.shape[1]
    conv_chans = conv_weight.shape[0] * shards
    state = (conv_chans - inner) // 2
    assert part_len == SPAN and batch == 2 and state == LANES and taps == 4
    wide = conv_chans + LANES
    main = batch * SPAN
    chunk = depth // shards
    up = [(i, i + 1) for i in range(parts - 1)]
    down = [(i + 1, i) for i in range(parts - 1)]

    custom = shards == 8 and chunk % (2 * HALO) == 0
    rows_out = inner // shards
    line = lambda v: v.reshape(1, -1)
    w_rest = vmem_call(
        partial(pack_body, heads, inner),
        sds((chunk, wide), BF16),
        [in_weight, gain_in, conv_weight.T, conv_bias, gain_out],
        scratch=[
            pltpu.VMEM((chunk, LANES), F32),
            *[pltpu.VMEM(v.shape, BF16) for v in (in_weight, gain_in, conv_weight.T, conv_bias, gain_out)],
            pltpu.SemaphoreType.DMA((5,)),
        ],
        hbm=True,
        mib=60,
    )
    segs = jnp.pad(segment_ids[0], ((0, 0), (HALO, 0)), constant_values=-1).astype(F32)
    segs = lax.dynamic_slice_in_dim(segs, at_seq * SPAN, HALO + SPAN, 1)
    seg_row = jnp.pad(segs[:, HALO:], ((0, 8 - batch), (0, 0)))
    segs = jnp.pad(segs, ((0, LANES - batch), (0, -(HALO + SPAN) % LANES)))
    spread, seg_col, head_rows = vmem_call(
        partial(prep_body, heads),
        (sds((2 * LANES, inner), BF16), sds((HALO + SPAN, LANES), F32), sds((8, LANES), F32)),
        [segs, line(dt_bias), line(a_log), line(skip_gain)],
        after=[w_rest],
    )
    w_pair = jnp.concatenate([out_weight, in_weight[:, : inner // 2], in_weight[:, inner // 2 : inner]], axis=0)
    exact = shards * parts if custom and 3 * (taps + 1) + 1 + 2 * shards * parts <= chunk else 0
    me = (at_seq * shards + at_fsdp).astype(jnp.int32)
    idx = jnp.stack([at_fsdp.astype(jnp.int32) if custom else jnp.int32(0), me])
    z_idx = at_seq.astype(jnp.int32).reshape(1)
    halo_in = lax.ppermute(layer_input[0, :, SPAN - HALO :, :], "seq", up).reshape(batch * HALO, depth)
    if custom:
        side, down_w = swap(w_rest, 2), swap(w_rest, 4)
        early = (side, down_w, seg_col, seg_row, head_rows, idx, z_idx, w_pair, halo_in)
        side, down_w, seg_col, seg_row, head_rows, idx, z_idx, w_pair, halo_in = lax.optimization_barrier(early)
        top, low = swap(down_w[: chunk // 2], 2), swap(side[chunk // 2 :], 4)
        near = stack([w_rest, side, down_w])
        near_other = swap(near, 1)
        far = vmem_call(rows_body, sds((chunk, wide), BF16), [top, low], after=[near])
        far_other = swap(far, 1)
        rest_pieces = [
            (w_rest, [(None, 0, 0)]),
            (side, [(None, 2, 0)]),
            (down_w, [(None, 4, 0)]),
            (far, [(None, 6, 0)]),
            (near_other, [(0, 1, 0), (1, 3, 0), (2, 5, 0)]),
            (far_other, [(None, 7, 0)]),
        ]
        w_pair, _ = lax.optimization_barrier((w_pair, far))
        side, down_w = swap(w_pair, 2), swap(w_pair, 4)
        pair_own = [w_pair, side, down_w]
    else:
        rest_pieces = [(lax.all_gather(w_rest, "fsdp", axis=0, tiled=True), [(None, 0, 0)])]
        whole = lax.all_gather(w_pair, "fsdp", axis=0)
        pair_own = [
            jnp.concatenate(
                [
                    whole[:, :rows_out].reshape(inner, depth),
                    whole[:, rows_out : rows_out + chunk].reshape(depth, depth),
                    whole[:, rows_out + chunk :].reshape(depth, depth),
                ],
                axis=0,
            )
        ]
    tokens = layer_input.reshape(main, depth)
    cot = cotangent.reshape(main, depth)
    both = range(batch)

    rows = main + batch * HALO
    rest_values, layout = layout_of(rest_pieces)
    each = lambda shape, dtype: tuple(sds(shape, dtype) for _ in both)
    proj = vmem_call(
        partial(proj_body, layout, batch, heads, shards, state),
        (
            sds((depth, wide), BF16),
            sds((rows, depth), BF16),
            sds((1, depth), F32),
            sds((8, conv_chans), F32),
            sds((1, inner), F32),
            each((HALO + SPAN, conv_chans), BF16),
            each((SPAN, LANES), F32),
            each((SPAN, inner), F32),
            each((SPAN, 2 * state), BF16),
            each((SPAN, inner), BF16),
            each((SPAN, LANES), F32),
            each((SPAN, LANES), F32),
            each((LANES, SPAN), F32),
            each((state, inner), F32),
            each((state, inner), BF16),
            each((8, inner), F32),
        ),
        [tokens, halo_in, head_rows, seg_col, spread] + rest_values,
        idx=idx,
        scratch=[
            pltpu.VMEM((HALO + SPAN, WIDE), F32),
            pltpu.VMEM((batch, SPAN, 2 * LANES), BF16),
            pltpu.VMEM((depth, LANES), F32),
        ],
        us=10,
    )
    (w_all, normed, gain_front, convw, gain_back, conv_in, dt_raw, x_all, bc_all) = proj[:9]
    (xdt_all, dt_all, s_all, st_all, fresh, send, decay) = proj[9:]

    if custom:
        far_w, pair_own[1], _ = lax.optimization_barrier((pair_own[2], pair_own[1], w_all))
        pair_own.append(swap(far_w, 2))

    hops = len(up)
    forth = [Chain(fresh[0], send[0], decay[0], up)]
    second, forth[0].got = lax.optimization_barrier((send[1], forth[0].got))
    forth.append(Chain(fresh[1], second, decay[1], up))
    forth[0].step(us=0.05)
    y_in = []
    for b in both:
        y_in.append(
            vmem_call(
                partial(intra_body, state, b),
                sds((SPAN, inner), F32),
                [bc_all[b], xdt_all[b], s_all[b], st_all[b], seg_col, seg_row],
                after=[forth[0].state, pair_own[2]] if custom else [forth[0].state],
                us=2,
            )
        )
    forth[0].step(after=[forth[1].step(after=y_in, us=0.05)], us=0.05)
    if custom:
        *pair_own, _ = lax.optimization_barrier((*pair_own, forth[0].state))
        pair_pieces = [(v, [(None, 2 * m, 0)]) for m, v in enumerate(pair_own)]
        pair_pieces += [(swap(v, 1), [(None, 2 * m + 1, 0)]) for m, v in enumerate(pair_own)]
    else:
        pair_pieces = [(pair_own[0], [(None, 0, 0)])]
    pair_values, layout2 = layout_of(pair_pieces)
    w_out, w_gate, gating, d_outn, turned = vmem_call(
        partial(dense_body, layout2, inner),
        (sds((inner, depth), BF16), sds((depth, inner), BF16), sds((main, inner), F32), sds((main, inner), F32), sds((depth, rows), BF16)),
        [normed, cot] + pair_values,
        idx=idx,
        after=[forth[0].state],
        us=3,
    )
    forth[1].step(after=[gating])
    for hop in range(2, hops - 1):
        forth[1].step(after=[forth[0].step(after=[forth[1].state])])
    forth[0].step(after=[forth[1].state])

    gated, ebb = [], []
    for b in both:
        gated.append(
            vmem_call(
                partial(gate_body, state, b),
                (
                    sds((SPAN, inner), BF16),
                    sds((SPAN, inner), BF16),
                    sds((SPAN, inner), BF16),
                    sds((SPAN, inner), BF16),
                    sds((SPAN, LANES), F32),
                    sds((state, inner), F32),
                    sds((state, inner), BF16),
                    sds((8, LANES), F32),
                ),
                [y_in[b], forth[b].state, bc_all[b], s_all[b], seg_col, x_all[b], gating, d_outn, gain_back, head_rows, spread],
                scratch=[pltpu.VMEM((SPAN, inner), F32), pltpu.VMEM((SPAN, inner), F32)],
                us=4,
            )
        )
        ebb.append(Chain(gated[b][5], gated[b][6], decay[b], down[::-1]))
        if b == 0:
            forth[1].step(after=[gated[0][4]])
    carry = [forth[b].state for b in both]
    def inner_back_of(b, after):
        return vmem_call(
            partial(intra_back_body, state, b),
            (sds((SPAN, inner), F32), sds((SPAN, 2 * state), F32)),
            [bc_all[b], xdt_all[b], gated[b][1], gated[b][2], carry[b], s_all[b], st_all[b], seg_col, seg_row],
            scratch=[pltpu.VMEM((SPAN, SPAN), F32)],
            after=after,
            us=0.05,
        )

    inner_back = [inner_back_of(0, [gated[1][4]])]
    ebb[0].step(after=[inner_back[0][1]])
    ways = shards if custom else 1
    pair_rows = (inner + 2 * depth) // ways
    halves = lambda r, c: tuple(sds((max(ways // 2, 1), r, c), BF16) for _ in range(min(ways, 2)))
    pair_grads = vmem_call(
        partial(out_grad_body, ways),
        halves(pair_rows, depth)[:1] + tuple(sds((pair_rows, depth), BF16) for _ in range(ways // 2)),
        [gated[0][0], gated[1][0], cot, gated[0][3], gated[1][3], normed],
        idx=idx,
        scratch=[pltpu.VMEM((inner, depth), F32), pltpu.VMEM((depth, inner), F32)],
        mib=20,
        us=4,
    )
    ebb[0].step(after=[ebb[1].step(after=[pair_grads[0]], us=0.05)], us=20)
    inner_back.append(inner_back_of(1, [ebb[0].state]))
    waits = [inner_back[1][1]]
    if custom:
        first = Reduce(*pair_grads)
        waits.append(first.pair(after=[ebb[0].state]))
    ebb[1].step(after=waits)
    waits = [ebb[1].state]
    if custom:
        waits = [first.relay(after=waits)]
    for hop in range(2, hops - 1):
        ebb[1].step(after=[ebb[0].step(after=waits)])

    back = []
    ebb[0].step(after=waits)
    for b in both:
        if b == 1:
            ebb[1].step(after=[back[0][0]])
        back.append(
            vmem_call(
                partial(mixer_back_body, state, b),
                (sds((SPAN, wide), BF16), sds((HALO, wide), BF16), sds((8, conv_chans), F32), sds((8, LANES), F32)),
                [
                    conv_in[b],
                    dt_raw[b],
                    x_all[b],
                    bc_all[b],
                    xdt_all[b],
                    dt_all[b],
                    s_all[b],
                    seg_col,
                    convw,
                    head_rows,
                    inner_back[b][0],
                    inner_back[b][1],
                    gated[b][1],
                    gated[b][4],
                    carry[b],
                    ebb[b].state,
                    spread,
                ],
                scratch=[
                    pltpu.VMEM((HALO + SPAN, WIDE), F32),
                    pltpu.VMEM((2 * HALO + SPAN, WIDE), F32),
                    pltpu.VMEM((2 * HALO + SPAN, WIDE), F32),
                ],
                us=6,
            )
        )
    d_rows = [back[0][0], back[1][0], back[0][1], back[1][1]]
    waits = [first.step(z_idx, parts, after=[back[1][0]])] if custom else []
    rest_grads = vmem_call(
        partial(in_grad_body, shards, heads, taps, exact),
        halves(depth // ways, wide),
        d_rows + [turned, back[0][2], back[1][2], back[0][3], back[1][3], gated[0][7], gated[1][7]],
        idx=idx,
        scratch=[pltpu.VMEM((rows, wide), BF16), pltpu.VMEM((depth, wide), F32), pltpu.VMEM((8, LANES), F32)],
        after=waits,
        mib=14,
        us=4,
    )
    if custom:
        rest = Reduce(*rest_grads)
        sent = rest.pair()
    out_rows = vmem_call(
        out_body,
        sds((main, depth), BF16),
        [gated[0][0], gated[1][0], tokens, w_out],
        after=[sent] if custom else [rest_grads[0]],
        us=3,
    )
    if custom:
        sent = rest.relay(after=[out_rows])
        sent = first.step(z_idx, parts, after=[sent])
    in_grad, halo_grad = vmem_call(
        in_back_body,
        (sds((main, depth), F32), sds((batch * HALO, depth), F32)),
        d_rows + [w_all, gated[0][3], gated[1][3], w_gate, cot, tokens, halo_in, gain_front],
        scratch=[pltpu.VMEM((rows, wide), BF16)],
        after=[sent] if custom else [],
        mib=12,
        us=0.05,
    )
    halo_back = lax.ppermute(halo_grad, "seq", down)
    if custom:
        sent = first.step(z_idx, parts, after=[in_grad])
        sent = rest.spread(z_idx, parts, after=[sent])
        sent = first.step(z_idx, parts, after=[sent])
        sent = rest.collect(after=[sent])
        pair_sum = first.step(z_idx, parts, after=[sent])
        rest_parts = rest.quarters if parts == 4 else [rest.total]
    else:
        whole = pair_grads[0][0]
        cuts = ((0, inner), (inner, inner + depth), (inner + depth, inner + 2 * depth))
        shard_sum = lambda v: lax.psum_scatter(v, "fsdp", scatter_dimension=0, tiled=True)
        pair_sum = lax.psum(jnp.concatenate([shard_sum(whole[lo:hi]) for lo, hi in cuts], axis=0).astype(F32), "seq")
        rest_parts = [lax.psum(shard_sum(rest_grads[0][0]).astype(F32), "seq")]
    input_grad = vmem_call(
        halo_add_body, sds(in_grad.shape, F32), [in_grad, halo_back], after=[sent] if custom else []
    ).reshape(1, batch, SPAN, depth)
    width = conv_chans // shards
    grad_in_weight, grad_out_weight, grad_gain, grad_back, grad_conv, grad_bias, head_sums = vmem_call(
        partial(final_body, heads, taps, exact),
        (
            sds((chunk, in_weight.shape[1]), F32),
            sds((rows_out, depth), F32),
            sds((1, chunk), F32),
            sds((1, rows_out), F32),
            sds((taps, width), F32),
            sds((1, width), F32),
            sds((3, heads), F32),
        ),
        [in_weight, line(gain_in), out_weight, line(gain_out), pair_sum] + rest_parts,
        idx=z_idx,
        scratch=[pltpu.VMEM((chunk, wide), F32), pltpu.VMEM((-(-rows_out // LANES) * LANES, LANES), F32)],
    )
    if not exact:
        three = back[0][3] + back[1][3] + gated[0][7] + gated[1][7]
        head_sums = lax.psum(three[:3, :heads], ("fsdp", "seq"))
    return (
        out_rows.reshape(1, batch, SPAN, depth),
        input_grad,
        grad_gain[0],
        grad_in_weight,
        grad_conv.T,
        grad_bias[0],
        head_sums[0],
        head_sums[1],
        head_sums[2],
        grad_back[0],
        grad_out_weight,
    )


def solution(mesh):
    tokens = P("fsdp", None, "seq", None)
    row, matrix = P("fsdp"), P("fsdp", None)
    return jax.shard_map(
        on_device,
        mesh=mesh,
        in_specs=(tokens, P("fsdp", None, None), row, matrix, matrix, row, P(), P(), P(), row, matrix, tokens),
        out_specs=(tokens, tokens, row, matrix, matrix, row, P(), P(), P(), row, matrix),
        check_vma=False,
    )
```

```python
from functools import partial

import jax
import jax.numpy as jnp
from jax import lax
from jax.experimental import pallas as pl
from jax.experimental.pallas import tpu as pltpu
from jax.sharding import PartitionSpec as P

SPAN = 256
HEADDIM = 64
LANES = 128
HALO = 16
WIDE = 256
EPS_NORM = 1e-05
COST = 1e9
OFF = -10000.0
F32 = jnp.float32
BF16 = jnp.bfloat16


def nn(a, b):
    return lax.dot_general(a, b, (((1,), (0,)), ((), ())), preferred_element_type=F32)


def nt(a, b):
    return lax.dot_general(a, b, (((1,), (1,)), ((), ())), preferred_element_type=F32)


def tn(a, b):
    return lax.dot_general(a, b, (((0,), (0,)), ((), ())), preferred_element_type=F32)


def iota(shape, dim):
    return lax.broadcasted_iota(jnp.int32, shape, dim)


def ones_where(cond):
    return jnp.where(cond, 1.0, 0.0)


def split2(v):
    high = v.astype(BF16)
    low = (v - high.astype(F32)).astype(BF16)
    return jnp.concatenate([high, low], axis=1)


def to_heads(values, picks):
    parts = []
    for v in values:
        high = v.astype(BF16)
        parts += [high, (v - high.astype(F32)).astype(BF16)]
    sums = nt(jnp.concatenate(parts, axis=0), picks)
    out, at = [], 0
    for v in values:
        rows = v.shape[0]
        out.append(sums[at : at + rows] + sums[at + rows : at + 2 * rows])
        at += 2 * rows
    return out


def running_sum(tri, v):
    high = v.astype(BF16)
    rest = v - high.astype(F32)
    mid = rest.astype(BF16)
    low = (rest - mid.astype(F32)).astype(BF16)
    return nn(tri, high) + nn(tri, mid) + nn(tri, low)


def sigmoid(v):
    return 0.5 * jnp.tanh(0.5 * v) + 0.5


def silu_slope(v, sig):
    return sig * (1.0 + v * (1.0 - sig))


def softplus(v):
    return jnp.maximum(v, 0.0) + jnp.log1p(jnp.exp(-jnp.abs(v)))


def row_masks(seg_ref, b, taps):
    here = segs_of(seg_ref, b)
    return [ones_where(seg_ref[pl.ds(HALO - j, SPAN), b : b + 1] == here) for j in range(1, taps)]


def segs_of(seg_ref, b):
    return seg_ref[pl.ds(HALO, SPAN), b : b + 1]


def seg_before(seg_ref, b):
    return seg_ref[HALO - 1 : HALO, b : b + 1]


def seg_last(seg_ref, b):
    return seg_ref[HALO + SPAN - 1 : HALO + SPAN, b : b + 1]


def conv_pre(ext_ref, cols, convw_ref, masks):
    taps = len(masks) + 1
    total = convw_ref[taps : taps + 1, cols] + convw_ref[taps - 1 : taps, cols] * ext_ref[pl.ds(HALO, SPAN), :]
    for j in range(1, taps):
        total = total + convw_ref[taps - 1 - j : taps - j, cols] * (
            ext_ref[pl.ds(HALO - j, SPAN), :] * masks[j - 1]
        )
    return total


def vmem_call(body, out_shape, operands, idx=None, scratch=(), mib=8, after=(), us=0.05, hbm=False):
    vm = pl.BlockSpec(memory_space=pltpu.VMEM)
    smem = [] if idx is None else [idx]
    head, tail = len(smem) + len(operands), len(after)

    def run(*refs):
        body(*refs[:head], *refs[head + tail :])

    return pl.pallas_call(
        run,
        out_shape=out_shape,
        in_specs=[pl.BlockSpec(memory_space=pltpu.SMEM)] * len(smem)
        + [pl.BlockSpec(memory_space=pltpu.HBM) if hbm else vm] * len(operands)
        + [pl.BlockSpec(memory_space=pl.ANY)] * tail,
        out_specs=jax.tree.map(lambda _: vm, out_shape),
        scratch_shapes=list(scratch),
        compiler_params=pltpu.CompilerParams(vmem_limit_bytes=mib * 1024 * 1024),
        cost_estimate=pl.CostEstimate(flops=int(us * COST), bytes_accessed=0, transcendentals=0),
        name=body.func.__name__ if isinstance(body, partial) else body.__name__,
    )(*smem, *operands, *after)


def sds(shape, dtype):
    return jax.ShapeDtypeStruct(shape, dtype)


def prep_body(heads, segs_ref, dtb_ref, alog_ref, skip_ref, spread_ref, seg_ref, heads_ref):
    for c0 in range(0, spread_ref.shape[1], WIDE):
        shape = (2 * LANES, WIDE)
        hit = (iota(shape, 0) & (LANES - 1)) == ((iota(shape, 1) + c0) >> 6)
        spread_ref[:, c0 : c0 + WIDE] = ones_where(hit).astype(BF16)
    seg_ref[...] = segs_ref[...].T[0 : HALO + SPAN, :]
    heads_ref[...] = jnp.zeros(heads_ref.shape, F32)
    heads_ref[0:1, :] = jnp.full((1, LANES), OFF, F32)
    for row, ref in enumerate((dtb_ref, alog_ref, skip_ref)):
        heads_ref[row : row + 1, 0:heads] = ref[...].astype(F32)


def small_rows(taps, width):
    third = -(-width // 3)
    return [
        (t, 3 * t + m, m * third, min(third, width - m * third)) for t in range(taps + 1) for m in range(3)
    ]


def pack_body(heads, inner, *refs):
    given, out_ref, end_ref, sems = refs[:5], refs[5], refs[6], refs[-1]
    copies = [pltpu.make_async_copy(a, b, sems.at[i]) for i, (a, b) in enumerate(zip(given, refs[7:12]))]
    for copy in copies:
        copy.start()
    for copy in copies:
        copy.wait()
    w_ref, gain_ref, conv_ref, bias_ref, back_ref = refs[7:12]
    full = w_ref.shape[1] - inner - heads
    taps, width = conv_ref.shape
    flat = lambda ref: ref[...].astype(F32).reshape(1, ref.shape[0])
    out_ref[:, 0:full] = w_ref[:, inner : inner + full]
    end_ref[...] = jnp.zeros(end_ref.shape, F32)
    end_ref[:, 0:heads] = w_ref[:, inner + full :].astype(F32)
    conv, bias, back = conv_ref[...].astype(F32), flat(bias_ref), flat(back_ref)
    for t, row, first, size in small_rows(taps, width):
        value = conv[t : t + 1] if t < taps else bias
        end_ref[row : row + 1, heads : heads + size] = value[:, first : first + size]
    row = 3 * (taps + 1)
    chunk, half = gain_ref.shape[0], back_ref.shape[0] // 2
    end_ref[row : row + 1, heads : heads + chunk] = flat(gain_ref)
    for m in range(2):
        end_ref[row + 1 + m : row + 2 + m, heads : heads + half] = back[:, m * half : (m + 1) * half]
    out_ref[:, full:] = end_ref[...].astype(BF16)


def unpack(heads, taps, shards, end_ref, gain_ref, conv_ref, back_ref):
    chunk = end_ref.shape[0] // shards
    width, half = conv_ref.shape[1] // shards, back_ref.shape[1] // shards // 2
    conv_ref[taps + 1 :, :] = jnp.zeros((7 - taps, conv_ref.shape[1]), F32)
    for i in range(shards):
        at = i * chunk
        for t, row, first, size in small_rows(taps, width):
            conv_ref[t : t + 1, i * width + first : i * width + first + size] = end_ref[
                at + row : at + row + 1, heads : heads + size
            ]
        row = at + 3 * (taps + 1)
        gain_ref[:, i * chunk : (i + 1) * chunk] = end_ref[row : row + 1, heads : heads + chunk]
        for m in range(2):
            first = (2 * i + m) * half
            back_ref[:, first : first + half] = end_ref[row + 1 + m : row + 2 + m, heads : heads + half]


def proj_body(layout, batch, heads, shards, state, *refs):
    idx_ref, tokens_ref, halo_ref, heads_ref, seg_ref, spread_ref = refs[:6]
    pieces = refs[6 : 6 + len(layout)]
    (w_ref, normed_ref, gain_ref, convw_ref, back_ref, convin_ref, dtraw_ref, x_ref, bc_ref, xdt_ref, dt_ref, s_ref, st_ref, fresh_ref, send_ref, decay_ref, slope_ref) = refs[
        6 + len(layout) : 23 + len(layout)
    ]
    ext_ref, heads_all_ref, end_ref, turned_ref = refs[23 + len(layout) :]
    group = 2 * SPAN + HALO
    inner = heads * HEADDIM
    chunk = w_ref.shape[0] // (1 if len(layout) == 1 else 8)

    def store(first, off, view):
        w_ref[pl.ds(pl.multiple_of(first, HALO), view.shape[0]), :] = view[...]

    put_pieces(layout, pieces, idx_ref[0], chunk, store)
    conv_chans = inner + 2 * state
    taps = 4
    end_ref[...] = w_ref[:, conv_chans:].astype(F32)
    unpack(heads, taps, shards, end_ref, gain_ref, convw_ref, back_ref)
    w_ref[:, conv_chans:] = jnp.where(iota(end_ref.shape, 1) < heads, end_ref[...], 0.0).astype(BF16)
    main = tokens_ref.shape[0]
    for ref, first in ((tokens_ref, 0), (halo_ref, main)):
        v = ref[...].astype(F32)
        scale = lax.rsqrt(jnp.mean(v * v, axis=1, keepdims=True) + EPS_NORM)
        normed_ref[pl.ds(first, ref.shape[0]), :] = (v * scale * gain_ref[...]).astype(BF16)
    normed = normed_ref[...]
    raw = nn(normed, w_ref[:, conv_chans : conv_chans + LANES])
    tri = ones_where(iota((SPAN, SPAN), 0) >= iota((SPAN, SPAN), 1)).astype(BF16)
    all_masks = []
    for b in range(batch):
        all_masks.append(row_masks(seg_ref, b, taps))
        dt_raw = raw[b * SPAN : (b + 1) * SPAN].astype(BF16).astype(F32)
        dtraw_ref[b][...] = dt_raw
        dt = softplus(dt_raw + heads_ref[0:1, :])
        dt_ref[b][...] = dt
        rate = -jnp.exp(heads_ref[1:2, :])
        logs = running_sum(tri, dt * rate)
        s_ref[b][...] = logs
        st_ref[b][...] = logs.T
        last = logs[SPAN - 1 : SPAN, :]
        same_last = ones_where(segs_of(seg_ref, b) == seg_last(seg_ref, b))
        at = b * group
        heads_all_ref[at : at + SPAN, :] = split2(dt)
        heads_all_ref[at + SPAN : at + 2 * SPAN, :] = split2(jnp.exp(last - logs) * same_last)
        keep = ones_where(seg_last(seg_ref, b) == seg_before(seg_ref, b))
        heads_all_ref[at + 2 * SPAN : at + group, :] = split2(jnp.broadcast_to(jnp.exp(last) * keep, (HALO, LANES)))
    for c0 in [inner] + list(range(0, inner, WIDE)):
        cols = slice(c0, c0 + WIDE)
        projected = nn(normed, w_ref[:, cols]).astype(BF16)
        if c0 < inner:
            wide = nn(heads_all_ref[...], spread_ref[:, cols])
        for b in range(batch):
            halo0 = batch * SPAN + b * HALO
            top = projected[halo0 : halo0 + HALO]
            rest = projected[b * SPAN : (b + 1) * SPAN]
            convin_ref[b][0:HALO, cols] = top
            convin_ref[b][HALO : HALO + SPAN, cols] = rest
            ext_ref[0:HALO, :] = top.astype(F32)
            ext_ref[HALO : HALO + SPAN, :] = rest.astype(F32)
            pre = conv_pre(ext_ref, cols, convw_ref, all_masks[b])
            sig = sigmoid(pre)
            act = pre * sig
            slope_ref[b][:, cols] = silu_slope(pre, sig).astype(BF16)
            if c0 == inner:
                bc_ref[b][...] = act.astype(BF16)
                turned_ref[b] = bc_ref[b][:, 0:state].T
            else:
                at = b * group
                x_ref[b][:, cols] = act
                xdt = (wide[at : at + SPAN] * act).astype(BF16)
                xdt_ref[b][:, cols] = xdt
                xt = (wide[at + SPAN : at + 2 * SPAN] * xdt.astype(F32)).astype(BF16)
                decay_ref[b][:, cols] = wide[at + 2 * SPAN : at + 2 * SPAN + 8]
                fresh = nn(turned_ref[b], xt)
                fresh_ref[b][:, cols] = fresh
                send_ref[b][:, cols] = fresh.astype(BF16)


def inside_mask(seg_ref, segr_ref, b, flipped):
    rows, cols = iota((SPAN, SPAN), 0), iota((SPAN, SPAN), 1)
    ordered = rows <= cols if flipped else rows >= cols
    return ordered & (segs_of(seg_ref, b) == segr_ref[b : b + 1, :])


def head_halves(block):
    low = iota(block.shape, 1) < HEADDIM
    zero = jnp.zeros_like(block)
    return jnp.where(low, block, zero), jnp.where(low, zero, block)


def intra_body(state, b, bc_ref, xdt_ref, s_ref, st_ref, seg_ref, segr_ref, y_ref):
    scores = nt(bc_ref[:, state : 2 * state], bc_ref[:, 0:state])
    scores = jnp.where(inside_mask(seg_ref, segr_ref, b, False), scores, 0.0)
    for pair in range(xdt_ref.shape[1] // LANES):
        cols = slice(pair * LANES, (pair + 1) * LANES)
        total = None
        for half, values in enumerate(head_halves(xdt_ref[:, cols])):
            h = 2 * pair + half
            decay = jnp.exp(jnp.minimum(s_ref[:, h : h + 1] - st_ref[h : h + 1, :], 0.0))
            part = nn((scores * decay).astype(BF16), values)
            total = part if total is None else total + part
        y_ref[:, cols] = total


def dense_body(layout, inner, *refs):
    idx_ref, normed_ref, cot_ref = refs[:3]
    pieces = refs[3 : 3 + len(layout)]
    wout_ref, wgate_ref, gating_ref, dout_ref, turned_ref, turn_ref = refs[3 + len(layout) :]
    depth = wgate_ref.shape[0]
    shards = 1 if len(layout) == 1 else 8
    ochunk, gchunk = inner // shards, depth // shards
    half_cols = inner // 2
    def store(owner, off, view):
        wout_ref[pl.ds(pl.multiple_of(owner * ochunk, HALO), ochunk), :] = view[0:ochunk, :]
        for side in range(2):
            wgate_ref[
                pl.ds(pl.multiple_of(owner * gchunk, HALO), gchunk), side * half_cols : (side + 1) * half_cols
            ] = view[ochunk + side * gchunk : ochunk + (side + 1) * gchunk, :]

    put_pieces(layout, pieces, idx_ref[0], 1, store)
    for r0 in range(0, depth, WIDE):
        turn_ref[r0 : r0 + WIDE, :] = normed_ref[:, r0 : r0 + WIDE].T
    for k in range(shards):
        turned_ref[k * gchunk : (k + 1) * gchunk, :] = turn_ref[
            pl.ds(pl.multiple_of((idx_ref[0] ^ k) * gchunk, HALO), gchunk), :
        ]
    normed = normed_ref[0 : cot_ref.shape[0], :]
    cot = cot_ref[...]
    for c0 in range(0, inner, WIDE):
        gating_ref[:, c0 : c0 + WIDE] = nn(normed, wgate_ref[:, c0 : c0 + WIDE])
        dout_ref[:, c0 : c0 + WIDE] = nt(cot, wout_ref[c0 : c0 + WIDE, :])


def gate_body(state, b, *refs):
    (yin_ref, carry_ref, bc_ref, s_ref, seg_ref, x_ref, gating_ref, dout_ref, gain_ref, heads_ref, spread_ref) = refs[:11]
    (outn_ref, dy_ref, ey_ref, dgat_ref, rowterm_ref, grad_ref, send_ref, small_ref) = refs[11:19]
    y_ref, gated_ref, sig_ref, wide_ref, mixed_ref = refs[19:]
    inner = x_ref.shape[1]
    rows = pl.ds(b * SPAN, SPAN)
    c_mat = bc_ref[:, state : 2 * state]
    c_turned = c_mat.T
    carried = ones_where(segs_of(seg_ref, b) == seg_before(seg_ref, b))
    factor = split2(jnp.exp(s_ref[...]) * carried)
    factor = jnp.concatenate([factor, split2(jnp.broadcast_to(heads_ref[2:3, :], (HALO, LANES)))], axis=0)
    sumsq = jnp.zeros((SPAN, 1), F32)
    sumeg = jnp.zeros((SPAN, 1), F32)
    for c0 in range(0, inner, WIDE):
        cols = slice(c0, c0 + WIDE)
        spread = spread_ref[:, cols]
        both = nn(factor, spread)
        wide = both[0:SPAN]
        wide_ref[:, cols] = wide
        y = yin_ref[:, cols] + wide * nn(c_mat, carry_ref[:, cols])
        y_ref[:, cols] = y
        low = (y + both[SPAN : SPAN + 1] * x_ref[:, cols]).astype(BF16)
        mixed_ref[:, cols] = low
        mixed = low.astype(F32)
        gate = gating_ref[rows, cols]
        sig = sigmoid(gate)
        sig_ref[:, cols] = sig
        gated = mixed * (gate * sig)
        gated_ref[:, cols] = gated
        sumsq = sumsq + jnp.sum(gated * gated, axis=1, keepdims=True)
        sumeg = sumeg + jnp.sum(dout_ref[rows, cols] * gain_ref[:, cols] * gated, axis=1, keepdims=True)
    r = lax.rsqrt(sumsq / inner + EPS_NORM)
    coef = r * r * r * (sumeg / inner)
    terms = jnp.zeros((SPAN, LANES), F32)
    skips = jnp.zeros((8, LANES), F32)
    for c0 in range(0, inner, WIDE):
        cols = slice(c0, c0 + WIDE)
        gated = gated_ref[:, cols]
        gain = gain_ref[:, cols]
        dout = dout_ref[rows, cols]
        normal = gated * r
        outn_ref[:, cols] = (normal * gain).astype(BF16)
        y = y_ref[:, cols]
        x = x_ref[:, cols]
        d_gated = r * (dout * gain) - gated * coef
        gate = gating_ref[rows, cols]
        sig = sig_ref[:, cols]
        mixed = mixed_ref[:, cols].astype(F32)
        dgat_ref[:, cols] = (d_gated * mixed * silu_slope(gate, sig)).astype(BF16)
        dy = (d_gated * (gate * sig)).astype(BF16)
        dy_ref[:, cols] = dy
        dyf = dy.astype(F32)
        ey = (wide_ref[:, cols] * dyf).astype(BF16)
        ey_ref[:, cols] = ey
        skip_sum = jnp.broadcast_to(jnp.sum(dyf * x, axis=0, keepdims=True), (HALO, WIDE))
        term, skip = to_heads([dyf * y, skip_sum], spread_ref[0:LANES, cols])
        terms = terms + term
        skips = skips + skip[0:8]
        grad = nn(c_turned, ey)
        grad_ref[:, cols] = grad
        send_ref[:, cols] = grad.astype(BF16)
    rowterm_ref[...] = terms
    small_ref[...] = jnp.where(iota(skips.shape, 0) == 2, skips, 0.0)


def intra_back_body(state, b, *refs):
    (bc_ref, xdt_ref, dy_ref, ey_ref, carry_ref, s_ref, st_ref, seg_ref, segr_ref) = refs[:9]
    dxdt_ref, dbc_ref = refs[9:11]
    acc_ref = refs[11]
    b_mat = bc_ref[:, 0:state]
    c_mat = bc_ref[:, state : 2 * state]
    mask = inside_mask(seg_ref, segr_ref, b, True)
    scores = jnp.where(mask, nt(b_mat, c_mat), 0.0)
    for pair in range(xdt_ref.shape[1] // LANES):
        cols = slice(pair * LANES, (pair + 1) * LANES)
        total = None
        dy_block = dy_ref[:, cols]
        for half, (values, grads) in enumerate(zip(head_halves(xdt_ref[:, cols]), head_halves(dy_block))):
            h = 2 * pair + half
            decay = jnp.exp(jnp.minimum(st_ref[h : h + 1, :] - s_ref[:, h : h + 1], 0.0))
            part = nn((scores * decay).astype(BF16), grads)
            total = part if total is None else total + part
            d_weight = nt(values, dy_block) * decay
            if h == 0:
                acc_ref[...] = d_weight
            else:
                acc_ref[...] += d_weight
        dxdt_ref[:, cols] = total
    d_scores = jnp.where(mask, acc_ref[...], 0.0).astype(BF16)
    dbc_ref[:, 0:state] = nn(d_scores, c_mat)
    dbc_ref[:, state : 2 * state] = tn(d_scores, b_mat) + nt(ey_ref[...], carry_ref[...])


def mixer_back_body(state, b, *refs):
    (convin_ref, dtraw_ref, x_ref, bc_ref, xdt_ref, dt_ref, s_ref, seg_ref, convw_ref, heads_ref) = refs[:10]
    (dxdt_ref, dbc_ref, dy_ref, rowterm_ref, carry_ref, dcarry_ref, spread_ref, slope_ref) = refs[10:18]
    (dmain_ref, dhalo_ref, small_ref, hsmall_ref) = refs[18:22]
    dpre_ref, segs_ref = refs[22:]
    inner = x_ref.shape[1]
    taps = 4
    conv_chans = inner + 2 * state
    rows = HALO + SPAN
    segs_ref[0:rows, :] = seg_ref[...]
    segs_ref[rows:, :] = jnp.zeros((HALO, LANES), F32)
    here = segs_ref[0:rows, b : b + 1]
    masks = [ones_where(segs_ref[pl.ds(j, rows), b : b + 1] == here) for j in range(1, taps)]
    b_mat = bc_ref[:, 0:state]
    logs = s_ref[...]
    dt = dt_ref[...]
    rate = -jnp.exp(heads_ref[1:2, :])
    last = logs[SPAN - 1 : SPAN, :]
    same_last = ones_where(segs_of(seg_ref, b) == seg_last(seg_ref, b))
    keep = ones_where(seg_last(seg_ref, b) == seg_before(seg_ref, b))
    heads_all = jnp.concatenate(
        [
            split2(jnp.exp(last - logs) * same_last),
            split2(dt),
            split2(jnp.broadcast_to(heads_ref[2:3, :], (HALO, LANES))),
        ],
        axis=0,
    )
    col_term = jnp.zeros((SPAN, LANES), F32)
    direct = jnp.zeros((SPAN, LANES), F32)
    last_term = jnp.zeros((HALO, LANES), F32)
    d_b = dbc_ref[:, 0:state]
    dpre_ref[0:HALO, :] = jnp.zeros((HALO, WIDE), F32)
    dpre_ref[HALO + SPAN : HALO + SPAN + HALO, :] = jnp.zeros((HALO, WIDE), F32)
    small_ref[taps + 1 : 8, :] = jnp.zeros((7 - taps, conv_chans), F32)

    def conv_back(cols, d_act):
        ext = convin_ref[:, cols].astype(F32)
        d_pre = d_act * slope_ref[:, cols].astype(F32)
        dpre_ref[pl.ds(HALO, SPAN), :] = d_pre
        small_ref[taps : taps + 1, cols] = jnp.sum(d_pre, axis=0, keepdims=True)
        small_ref[taps - 1 : taps, cols] = jnp.sum(d_pre * ext[HALO:], axis=0, keepdims=True)
        total = convw_ref[taps - 1 : taps, cols] * dpre_ref[pl.ds(0, rows), :]
        for j in range(1, taps):
            moved = masks[j - 1] * dpre_ref[pl.ds(j, rows), :]
            small_ref[taps - 1 - j : taps - j, cols] = jnp.sum(moved * ext, axis=0, keepdims=True)
            total = total + convw_ref[taps - 1 - j : taps - j, cols] * moved
        total = total.astype(BF16)
        dhalo_ref[:, cols] = total[0:HALO]
        dmain_ref[:, cols] = total[HALO : HALO + SPAN]

    for c0 in range(0, inner, WIDE):
        cols = slice(c0, c0 + WIDE)
        spread = spread_ref[:, cols]
        picks = spread_ref[0:LANES, cols]
        d_carry = dcarry_ref[:, cols]
        wide = nn(heads_all, spread)
        tails = wide[0:SPAN]
        xdt = xdt_ref[:, cols].astype(F32)
        d_tail = tails * nn(b_mat, d_carry)
        d_xdt = dxdt_ref[:, cols] + d_tail
        x = x_ref[:, cols]
        from_tail = jnp.sum(xdt * d_tail, axis=0, keepdims=True)
        through = jnp.sum(d_carry.astype(F32) * carry_ref[:, cols].astype(F32), axis=0, keepdims=True)
        both = jnp.concatenate([from_tail, through, jnp.zeros((HALO - 2, WIDE), F32)], axis=0)
        cols_sum, direct_sum, both = to_heads([xdt * d_xdt, x * d_xdt, both], picks)
        col_term = col_term + cols_sum
        direct = direct + direct_sum
        last_term = last_term + both
        d_b = d_b + nt((tails * xdt).astype(BF16), d_carry)
        d_x = wide[SPAN : 2 * SPAN] * d_xdt + wide[2 * SPAN : 2 * SPAN + 1] * dy_ref[:, cols].astype(F32)
        conv_back(cols, d_x)
    conv_back(slice(inner, conv_chans), jnp.concatenate([d_b, dbc_ref[:, state : 2 * state]], axis=1))
    at_end = last_term[0:1, :] + last_term[1:2, :] * (jnp.exp(last) * keep)
    upper = ones_where(iota((SPAN, SPAN), 0) <= iota((SPAN, SPAN), 1)).astype(BF16)
    d_logs = running_sum(upper, rowterm_ref[...] - col_term) + at_end
    d_dt = direct + rate * d_logs
    d_raw = d_dt * sigmoid(dtraw_ref[...] + heads_ref[0:1, :])
    dmain_ref[:, conv_chans : conv_chans + LANES] = d_raw.astype(BF16)
    dhalo_ref[:, conv_chans : conv_chans + LANES] = jnp.zeros((HALO, LANES), BF16)
    hsmall_ref[0:1, :] = jnp.sum(d_raw, axis=0, keepdims=True)
    hsmall_ref[1:2, :] = jnp.sum(dt * d_logs, axis=0, keepdims=True) * rate
    hsmall_ref[2:8, :] = jnp.zeros((6, LANES), F32)


def out_grad_body(shards, *refs):
    (idx_ref, on0_ref, on1_ref, cot_ref, dg0_ref, dg1_ref, normed_ref) = refs[:7]
    outs = refs[7:-2]
    gout_ref, ggate_ref = refs[-2:]
    main = cot_ref.shape[0]
    inner, width = gout_ref.shape
    outn = jnp.concatenate([on0_ref[...], on1_ref[...]], axis=0)
    dgat = jnp.concatenate([dg0_ref[...], dg1_ref[...]], axis=0)
    normed = normed_ref[0:main, :]
    gout_ref[...] = tn(outn, cot_ref[...])
    for c0 in range(0, inner, width):
        ggate_ref[:, c0 : c0 + width] = tn(normed, dgat[:, c0 : c0 + width])
    ochunk, gchunk = inner // shards, width // shards
    for k in range(shards):
        owner = idx_ref[0] ^ k
        ref = outs[0].at[k // 2] if k % 2 == 0 else outs[1 + k // 2]
        ref[0:ochunk, :] = gout_ref[pl.ds(pl.multiple_of(owner * ochunk, HALO), ochunk), :].astype(BF16)
        for side in range(2):
            ref[ochunk + side * gchunk : ochunk + (side + 1) * gchunk, :] = ggate_ref[
                pl.ds(pl.multiple_of(owner * gchunk, HALO), gchunk), side * width : (side + 1) * width
            ].astype(BF16)


def out_body(on0_ref, on1_ref, xin_ref, wout_ref, lout_ref):
    for b, outn_ref in enumerate((on0_ref, on1_ref)):
        rows = slice(b * SPAN, (b + 1) * SPAN)
        lout_ref[rows, :] = (xin_ref[rows, :].astype(F32) + nn(outn_ref[...], wout_ref[...])).astype(BF16)


def join_rows(m0_ref, m1_ref, h0_ref, h1_ref, all_ref):
    all_ref[0:SPAN, :] = m0_ref[...]
    all_ref[SPAN : 2 * SPAN, :] = m1_ref[...]
    all_ref[2 * SPAN : 2 * SPAN + HALO, :] = h0_ref[...]
    all_ref[2 * SPAN + HALO : 2 * SPAN + 2 * HALO, :] = h1_ref[...]


def in_grad_body(shards, heads, taps, exact, *refs):
    idx_ref, m0_ref, m1_ref, h0_ref, h1_ref, normed_ref = refs[:6]
    conv0_ref, conv1_ref, head0_ref, head1_ref, skip0_ref, skip1_ref = refs[6:12]
    outs = refs[12:-3]
    all_ref, ends_ref, line_ref = refs[-3:]
    join_rows(m0_ref, m1_ref, h0_ref, h1_ref, all_ref)
    depth, wide = normed_ref.shape[0], all_ref.shape[1]
    conv = conv0_ref[...] + conv1_ref[...]
    three = head0_ref[...] + head1_ref[...] + skip0_ref[...] + skip1_ref[...]
    chunk, width = depth // shards, conv.shape[1] // shards
    ends_ref[...] = jnp.zeros(ends_ref.shape, F32)
    for i in range(shards):
        for t, row, first, size in small_rows(taps, width):
            at = i * chunk + row
            ends_ref[at : at + 1, heads : heads + size] = conv[t : t + 1, i * width + first : i * width + first + size]
    if exact:
        line_ref[...] = jnp.zeros(line_ref.shape, F32)
        for m in range(3):
            line_ref[0:1, (m + 1) * heads : (m + 2) * heads] = three[m : m + 1, 0:heads]
        value = line_ref[0:1, :]
        high = value.astype(BF16).astype(F32)
        rows = iota((2 * exact, LANES), 0)
        mine = jnp.where(rows == 2 * idx_ref[1], high, 0.0) + jnp.where(rows == 2 * idx_ref[1] + 1, value - high, 0.0)
        for i in range(shards):
            at = i * chunk + 3 * (taps + 1) + 1
            ends_ref[at : at + 2 * exact, :] = mine
    ways = 1 if len(outs) == 1 else shards
    part = depth // ways
    for c0 in range(0, wide, 384):
        cols = slice(c0, c0 + 384)
        grad = nn(normed_ref[...], all_ref[:, cols])
        for k in range(ways):
            share = grad[k * part : (k + 1) * part]
            out_ref = outs[k % 2].at[k // 2]
            if c0 + 384 < wide:
                out_ref[:, cols] = share.astype(BF16)
                continue
            out_ref[:, c0 : wide - LANES] = share[:, : 384 - LANES].astype(BF16)
            first = pl.multiple_of((idx_ref[0] ^ k) * part, 8)
            out_ref[:, wide - LANES :] = (share[:, 384 - LANES :] + ends_ref[pl.ds(first, part), :]).astype(BF16)


def in_back_body(*refs):
    m0_ref, m1_ref, h0_ref, h1_ref, w_ref, dg0_ref, dg1_ref, wgate_ref, cot_ref, xin_ref, halo_ref, gain_ref = refs[:12]
    igrad_ref, hgrad_ref, all_ref = refs[12:]
    main = cot_ref.shape[0]
    join_rows(m0_ref, m1_ref, h0_ref, h1_ref, all_ref)
    d_normed = nt(all_ref[...], w_ref[...])
    gain = gain_ref[...]

    def back(dn, v):
        q = lax.rsqrt(jnp.mean(v * v, axis=1, keepdims=True) + EPS_NORM)
        e = dn * gain
        return q * e - v * (q * q * q * jnp.mean(e * v, axis=1, keepdims=True))

    for b, dgat_ref in enumerate((dg0_ref, dg1_ref)):
        rows = slice(b * SPAN, (b + 1) * SPAN)
        d_both = d_normed[rows] + nt(dgat_ref[...], wgate_ref[...])
        igrad_ref[rows, :] = cot_ref[rows, :].astype(F32) + back(d_both, xin_ref[rows, :].astype(F32))
    hgrad_ref[...] = back(d_normed[main:], halo_ref[...].astype(F32))


def xor_pairs(size, k):
    return [(i, i ^ k) for i in range(size)]


def stack_body(*refs):
    out_ref = refs[-1]
    for i, ref in enumerate(refs[:-1]):
        out_ref[i] = ref[...]


def rows_body(top_ref, low_ref, out_ref):
    half = top_ref.shape[0]
    out_ref[0:half, :] = top_ref[...]
    out_ref[half:, :] = low_ref[...]


def stack(parts, after=()):
    return vmem_call(stack_body, sds((len(parts),) + parts[0].shape, BF16), parts, after=after)


def layout_of(pieces):
    return [v for v, _ in pieces], tuple(places for _, places in pieces)


def put_pieces(layout, refs, idx, chunk, store):
    for ref, places in zip(refs, layout):
        for sub, k, off in places:
            view = ref if sub is None else ref.at[sub]
            store((idx ^ k) * chunk + off, off, view)


def combine_body(last, *refs):
    if last:
        got_ref, carry_ref, out_ref = refs
        out_ref[...] = got_ref[...] + carry_ref[...]
        return
    first = len(refs) == 5
    got_ref, fresh_ref, decay_ref = refs[:3]
    out_ref, send_ref = refs[-2:]
    state = got_ref[...] if first else got_ref[...] + refs[3][...]
    out_ref[...] = state
    send_ref[...] = (fresh_ref[...] + decay_ref[0:1, :] * state.astype(F32)).astype(BF16)


class Chain:
    def __init__(self, fresh, send, decay, pairs):
        self.fresh, self.send, self.decay, self.pairs = fresh, send, decay, pairs
        self.state = None
        self.hop = 0
        self.start()

    def start(self):
        self.got = lax.ppermute(self.send, "seq", [self.pairs[self.hop]])

    def step(self, after=(), us=0.05):
        shape = sds(self.got.shape, BF16)
        prior = [] if self.state is None else [self.state]
        if self.hop == len(self.pairs) - 1:
            if prior:
                self.state = vmem_call(partial(combine_body, True), shape, [self.got] + prior, after=after)
            else:
                self.state = self.got
            return self.state
        self.state, self.send = vmem_call(
            partial(combine_body, False),
            (shape, shape),
            [self.got, self.fresh, self.decay] + prior,
            after=after,
            us=us,
        )
        self.hop += 1
        self.start()
        return self.state


def swap(v, k):
    return lax.ppermute(v, "fsdp", xor_pairs(8, k))


def pair_body(even_ref, *refs):
    own_ref, side_ref, down_ref, top_ref, low_ref = refs[-5:]
    got = refs[:-5] if len(refs) > 6 else [refs[0].at[i] for i in range(4)]
    half = top_ref.shape[0]
    add = lambda s: even_ref[s].astype(F32) + got[s][...].astype(F32)
    far = add(3).astype(BF16)
    top_ref[...] = far[0:half]
    low_ref[...] = far[half:]
    own_ref[...] = add(0)
    side_ref[...] = add(1)
    down_ref[...] = add(2)


def relay_body(side_ref, down_ref, top_ref, low_ref, side_out, down_out):
    half = top_ref.shape[0]
    side_out[0:half, :] = side_ref[0:half, :].astype(BF16)
    side_out[half:, :] = (side_ref[half:, :] + low_ref[...].astype(F32)).astype(BF16)
    down_out[0:half, :] = (down_ref[0:half, :] + top_ref[...].astype(F32)).astype(BF16)
    down_out[half:, :] = down_ref[half:, :].astype(BF16)


class Reduce:
    def __init__(self, even, *odd):
        self.even, self.stage = even, 0
        self.got = [swap(v, 1) for v in odd]

    def pair(self, after=()):
        _, rows, cols = self.even.shape
        full, half = sds((rows, cols), F32), sds((rows // 2, cols), BF16)
        self.own, self.side, self.down, top, low = vmem_call(
            pair_body, (full, full, full, half, half), [self.even] + self.got, after=after
        )
        self.top, self.low = swap(top, 2), swap(low, 4)
        return self.own

    def relay(self, after=()):
        shape = sds(self.own.shape, BF16)
        side, down = vmem_call(relay_body, (shape, shape), [self.side, self.down, self.top, self.low], after=after)
        self.side, self.down = swap(side, 2), swap(down, 4)
        return side

    def step(self, z, parts, after=()):
        rows, cols = self.own.shape
        along = lambda v, k: lax.ppermute(v, "seq", xor_pairs(parts, k))
        stage, self.stage = self.stage, self.stage + 1
        if parts != 4:
            if stage == 0:
                total = self.own + self.side.astype(F32) + self.down.astype(F32)
                self.total = lax.psum(total, "seq")
            return self.total
        f32, bf16 = lambda n: sds((n, cols), F32), lambda n: sds((n, cols), BF16)
        whole, half = pltpu.VMEM((rows, cols), F32), pltpu.VMEM((rows // 2, cols), F32)
        if stage == 0:
            given = [self.own, self.side, self.down]
            self.keep, send = vmem_call(
                halve_body, (f32(rows // 2), bf16(rows // 2)), given, idx=z, scratch=[whole], after=after
            )
            self.got = along(send, 1)
            return self.keep
        if stage == 1:
            given = [self.keep, self.got]
            self.keep, send = vmem_call(
                fold_body, (f32(rows // 4), bf16(rows // 4)), given, idx=z, scratch=[half], after=after
            )
            self.got = along(send, 2)
            return self.keep
        if stage == 2:
            self.keep = vmem_call(total_body, bf16(rows // 4), [self.keep, self.got], after=after)
            self.got = along(self.keep, 2)
            return self.keep
        if stage == 3:
            given = [self.keep, self.got]
            self.keep = vmem_call(partial(unfold_body, 1), bf16(rows // 2), given, idx=z, scratch=[half], after=after)
            self.got = along(self.keep, 1)
            return self.keep
        given = [self.keep, self.got]
        return vmem_call(partial(unfold_body, 0), f32(rows), given, idx=z, scratch=[whole], after=after)

    def spread(self, z, parts, after=()):
        rows, cols = self.own.shape
        self.parts, self.z = parts, z
        if parts != 4:
            total = self.own + self.side.astype(F32) + self.down.astype(F32)
            self.total = lax.psum(total, "seq")
            return self.total
        cut = sds((rows // 4, cols), BF16)
        mine, *others = vmem_call(
            spread_body,
            (sds((rows // 4, cols), F32), cut, cut, cut),
            [self.own, self.side, self.down],
            idx=z,
            scratch=[pltpu.VMEM((rows, cols), F32)],
            after=after,
        )
        self.mine = mine
        self.others = [lax.ppermute(v, "seq", xor_pairs(4, k + 1)) for k, v in enumerate(others)]
        return mine

    def collect(self, after=()):
        if self.parts != 4:
            return self.total
        part = vmem_call(collect_body, sds(self.mine.shape, BF16), [self.mine] + self.others, after=after, us=30)
        self.quarters = [part] + [lax.ppermute(part, "seq", xor_pairs(4, k)) for k in (1, 2, 3)]
        return part


def halve_body(z_ref, own_ref, side_ref, down_ref, keep_ref, send_ref, all_ref):
    all_ref[...] = own_ref[...] + side_ref[...].astype(F32) + down_ref[...].astype(F32)
    rows = keep_ref.shape[0]
    bit = z_ref[0] & 1
    keep_ref[...] = all_ref[pl.ds(pl.multiple_of(bit * rows, 8), rows), :]
    send_ref[...] = all_ref[pl.ds(pl.multiple_of((1 - bit) * rows, 8), rows), :].astype(BF16)


def fold_body(z_ref, half_ref, got_ref, keep_ref, send_ref, all_ref):
    all_ref[...] = half_ref[...] + got_ref[...].astype(F32)
    rows = keep_ref.shape[0]
    bit = (z_ref[0] >> 1) & 1
    keep_ref[...] = all_ref[pl.ds(pl.multiple_of(bit * rows, 8), rows), :]
    send_ref[...] = all_ref[pl.ds(pl.multiple_of((1 - bit) * rows, 8), rows), :].astype(BF16)


def total_body(keep_ref, got_ref, out_ref):
    out_ref[...] = (keep_ref[...] + got_ref[...].astype(F32)).astype(BF16)


def unfold_body(shift, z_ref, mine_ref, got_ref, out_ref, all_ref):
    rows = mine_ref.shape[0]
    bit = (z_ref[0] >> shift) & 1
    all_ref[pl.ds(pl.multiple_of(bit * rows, 8), rows), :] = mine_ref[...].astype(F32)
    all_ref[pl.ds(pl.multiple_of((1 - bit) * rows, 8), rows), :] = got_ref[...].astype(F32)
    out_ref[...] = all_ref[...].astype(out_ref.dtype)


def spread_body(z_ref, own_ref, side_ref, down_ref, mine_ref, one_ref, two_ref, three_ref, all_ref):
    all_ref[...] = own_ref[...] + side_ref[...].astype(F32) + down_ref[...].astype(F32)
    rows = mine_ref.shape[0]
    for k, ref in enumerate((mine_ref, one_ref, two_ref, three_ref)):
        first = pl.multiple_of((z_ref[0] ^ k) * rows, 8)
        ref[...] = all_ref[pl.ds(first, rows), :].astype(ref.dtype)


def collect_body(mine_ref, one_ref, two_ref, three_ref, out_ref):
    total = mine_ref[...] + one_ref[...].astype(F32) + two_ref[...].astype(F32) + three_ref[...].astype(F32)
    out_ref[...] = total.astype(BF16)


def final_body(heads, taps, sources, idx_ref, *refs):
    w_ref, gain_ref, wout_ref, back_ref, pair_ref = refs[:5]
    quarters = refs[5:-9]
    grad_ref, gout_ref, ggain_ref, gback_ref, conv_ref, bias_ref, heads_ref = refs[-9:-2]
    rest_ref, sums_ref = refs[-2:]
    rows = quarters[0].shape[0]
    for k, ref in enumerate(quarters):
        first = pl.multiple_of((idx_ref[0] ^ k) * rows, 8) if len(quarters) > 1 else 0
        rest_ref[pl.ds(first, rows), :] = ref[...].astype(F32)
    chunk, half = grad_ref.shape[0], pair_ref.shape[1]
    rows_out = gout_ref.shape[0]
    grad_ref[:, 0:half] = pair_ref[rows_out : rows_out + chunk, :]
    grad_ref[:, half : 2 * half] = pair_ref[rows_out + chunk : rows_out + 2 * chunk, :]
    grad_ref[:, 2 * half :] = rest_ref[:, 0 : grad_ref.shape[1] - 2 * half]
    gout_ref[...] = pair_ref[0:rows_out, :]
    total = jnp.sum(w_ref[...].astype(F32) * grad_ref[...], axis=1, keepdims=True)
    sums_ref[0:chunk, :] = jnp.broadcast_to(total, (chunk, LANES))
    ggain_ref[...] = sums_ref[...].T[0:1, 0:chunk] / gain_ref[...].astype(F32)
    total = jnp.sum(wout_ref[...].astype(F32) * gout_ref[...], axis=1, keepdims=True)
    sums_ref[0:rows_out, :] = jnp.broadcast_to(total, (rows_out, LANES))
    gback_ref[...] = sums_ref[...].T[0:1, 0:rows_out] / back_ref[...].astype(F32)
    width = conv_ref.shape[1]
    lane0 = rest_ref.shape[1] - LANES + heads
    for t, row, first, size in small_rows(taps, width):
        value = rest_ref[row : row + 1, lane0 : lane0 + size]
        if t < taps:
            conv_ref[t : t + 1, first : first + size] = value
        else:
            bias_ref[:, first : first + size] = value
    if sources:
        row = 3 * (taps + 1) + 1
        total = jnp.sum(rest_ref[row : row + 2 * sources, rest_ref.shape[1] - LANES :], axis=0, keepdims=True)
        for m in range(3):
            heads_ref[m : m + 1, :] = total[:, (m + 1) * heads : (m + 2) * heads]
    else:
        heads_ref[...] = jnp.zeros(heads_ref.shape, F32)


def halo_add_body(grad_ref, halo_ref, out_ref):
    out_ref[...] = grad_ref[...]
    for b in range(out_ref.shape[0] // SPAN):
        rows = slice((b + 1) * SPAN - HALO, (b + 1) * SPAN)
        out_ref[rows, :] = grad_ref[rows, :] + halo_ref[b * HALO : (b + 1) * HALO, :]


def on_device(
    layer_input,
    segment_ids,
    gain_in,
    in_weight,
    conv_weight,
    conv_bias,
    dt_bias,
    a_log,
    skip_gain,
    gain_out,
    out_weight,
    cotangent,
):
    shards, parts = lax.axis_size("fsdp"), lax.axis_size("seq")
    at_fsdp, at_seq = lax.axis_index("fsdp"), lax.axis_index("seq")
    _, batch, part_len, depth = layer_input.shape
    heads = dt_bias.shape[0]
    inner = heads * HEADDIM
    taps = conv_weight.shape[1]
    conv_chans = conv_weight.shape[0] * shards
    state = (conv_chans - inner) // 2
    assert part_len == SPAN and batch == 2 and state == LANES and taps == 4
    wide = conv_chans + LANES
    main = batch * SPAN
    chunk = depth // shards
    up = [(i, i + 1) for i in range(parts - 1)]
    down = [(i + 1, i) for i in range(parts - 1)]

    custom = shards == 8 and chunk % (2 * HALO) == 0
    rows_out = inner // shards
    line = lambda v: v.reshape(1, -1)
    w_rest = vmem_call(
        partial(pack_body, heads, inner),
        sds((chunk, wide), BF16),
        [in_weight, gain_in, conv_weight.T, conv_bias, gain_out],
        scratch=[
            pltpu.VMEM((chunk, LANES), F32),
            *[pltpu.VMEM(v.shape, BF16) for v in (in_weight, gain_in, conv_weight.T, conv_bias, gain_out)],
            pltpu.SemaphoreType.DMA((5,)),
        ],
        hbm=True,
        mib=60,
    )
    segs = jnp.pad(segment_ids[0], ((0, 0), (HALO, 0)), constant_values=-1).astype(F32)
    segs = lax.dynamic_slice_in_dim(segs, at_seq * SPAN, HALO + SPAN, 1)
    seg_row = jnp.pad(segs[:, HALO:], ((0, 8 - batch), (0, 0)))
    segs = jnp.pad(segs, ((0, LANES - batch), (0, -(HALO + SPAN) % LANES)))
    spread, seg_col, head_rows = vmem_call(
        partial(prep_body, heads),
        (sds((2 * LANES, inner), BF16), sds((HALO + SPAN, LANES), F32), sds((8, LANES), F32)),
        [segs, line(dt_bias), line(a_log), line(skip_gain)],
        after=[w_rest],
    )
    w_pair = jnp.concatenate([out_weight, in_weight[:, : inner // 2], in_weight[:, inner // 2 : inner]], axis=0)
    exact = shards * parts if custom and 3 * (taps + 1) + 1 + 2 * shards * parts <= chunk else 0
    me = (at_seq * shards + at_fsdp).astype(jnp.int32)
    idx = jnp.stack([at_fsdp.astype(jnp.int32) if custom else jnp.int32(0), me])
    z_idx = at_seq.astype(jnp.int32).reshape(1)
    halo_in = lax.ppermute(layer_input[0, :, SPAN - HALO :, :], "seq", up).reshape(batch * HALO, depth)
    if custom:
        side, down_w = swap(w_rest, 2), swap(w_rest, 4)
        early = (side, down_w, seg_col, seg_row, head_rows, idx, z_idx, w_pair, halo_in)
        side, down_w, seg_col, seg_row, head_rows, idx, z_idx, w_pair, halo_in = lax.optimization_barrier(early)
        top, low = swap(down_w[: chunk // 2], 2), swap(side[chunk // 2 :], 4)
        near = stack([w_rest, side, down_w])
        near_other = swap(near, 1)
        far = vmem_call(rows_body, sds((chunk, wide), BF16), [top, low], after=[near])
        far_other = swap(far, 1)
        rest_pieces = [
            (w_rest, [(None, 0, 0)]),
            (side, [(None, 2, 0)]),
            (down_w, [(None, 4, 0)]),
            (far, [(None, 6, 0)]),
            (near_other, [(0, 1, 0), (1, 3, 0), (2, 5, 0)]),
            (far_other, [(None, 7, 0)]),
        ]
        w_pair, _ = lax.optimization_barrier((w_pair, far))
        side, down_w = swap(w_pair, 2), swap(w_pair, 4)
        pair_own = [w_pair, side, down_w]
    else:
        rest_pieces = [(lax.all_gather(w_rest, "fsdp", axis=0, tiled=True), [(None, 0, 0)])]
        whole = lax.all_gather(w_pair, "fsdp", axis=0)
        pair_own = [
            jnp.concatenate(
                [
                    whole[:, :rows_out].reshape(inner, depth),
                    whole[:, rows_out : rows_out + chunk].reshape(depth, depth),
                    whole[:, rows_out + chunk :].reshape(depth, depth),
                ],
                axis=0,
            )
        ]
    tokens = layer_input.reshape(main, depth)
    cot = cotangent.reshape(main, depth)
    both = range(batch)

    rows = main + batch * HALO
    rest_values, layout = layout_of(rest_pieces)
    each = lambda shape, dtype: tuple(sds(shape, dtype) for _ in both)
    proj = vmem_call(
        partial(proj_body, layout, batch, heads, shards, state),
        (
            sds((depth, wide), BF16),
            sds((rows, depth), BF16),
            sds((1, depth), F32),
            sds((8, conv_chans), F32),
            sds((1, inner), F32),
            each((HALO + SPAN, conv_chans), BF16),
            each((SPAN, LANES), F32),
            each((SPAN, inner), F32),
            each((SPAN, 2 * state), BF16),
            each((SPAN, inner), BF16),
            each((SPAN, LANES), F32),
            each((SPAN, LANES), F32),
            each((LANES, SPAN), F32),
            each((state, inner), F32),
            each((state, inner), BF16),
            each((8, inner), F32),
            each((SPAN, conv_chans), BF16),
        ),
        [tokens, halo_in, head_rows, seg_col, spread] + rest_values,
        idx=idx,
        scratch=[
            pltpu.VMEM((HALO + SPAN, WIDE), F32),
            pltpu.VMEM((batch * (2 * SPAN + HALO), 2 * LANES), BF16),
            pltpu.VMEM((depth, LANES), F32),
            pltpu.VMEM((batch, state, SPAN), BF16),
        ],
        us=10,
    )
    (w_all, normed, gain_front, convw, gain_back, conv_in, dt_raw, x_all, bc_all) = proj[:9]
    (xdt_all, dt_all, s_all, st_all, fresh, send, decay, slope_all) = proj[9:]

    if custom:
        far_w, pair_own[1], _ = lax.optimization_barrier((pair_own[2], pair_own[1], w_all))
        pair_own.append(swap(far_w, 2))

    hops = len(up)
    forth = [Chain(fresh[0], send[0], decay[0], up)]
    second, forth[0].got = lax.optimization_barrier((send[1], forth[0].got))
    forth.append(Chain(fresh[1], second, decay[1], up))
    forth[0].step(us=0.05)
    y_in = []
    for b in both:
        y_in.append(
            vmem_call(
                partial(intra_body, state, b),
                sds((SPAN, inner), F32),
                [bc_all[b], xdt_all[b], s_all[b], st_all[b], seg_col, seg_row],
                after=[forth[0].state, pair_own[2]] if custom else [forth[0].state],
                us=2,
            )
        )
    forth[0].step(after=[forth[1].step(after=y_in, us=0.05)], us=0.05)
    if custom:
        *pair_own, _ = lax.optimization_barrier((*pair_own, forth[0].state))
        pair_pieces = [(v, [(None, 2 * m, 0)]) for m, v in enumerate(pair_own)]
        pair_pieces += [(swap(v, 1), [(None, 2 * m + 1, 0)]) for m, v in enumerate(pair_own)]
    else:
        pair_pieces = [(pair_own[0], [(None, 0, 0)])]
    pair_values, layout2 = layout_of(pair_pieces)
    w_out, w_gate, gating, d_outn, turned = vmem_call(
        partial(dense_body, layout2, inner),
        (sds((inner, depth), BF16), sds((depth, inner), BF16), sds((main, inner), F32), sds((main, inner), F32), sds((depth, rows), BF16)),
        [normed, cot] + pair_values,
        idx=idx,
        scratch=[pltpu.VMEM((depth, rows), BF16)],
        after=[forth[0].state],
        us=3,
    )
    forth[1].step(after=[gating])
    for hop in range(2, hops - 1):
        forth[1].step(after=[forth[0].step(after=[forth[1].state])])
    forth[0].step(after=[forth[1].state])

    gated, ebb = [], []
    for b in both:
        gated.append(
            vmem_call(
                partial(gate_body, state, b),
                (
                    sds((SPAN, inner), BF16),
                    sds((SPAN, inner), BF16),
                    sds((SPAN, inner), BF16),
                    sds((SPAN, inner), BF16),
                    sds((SPAN, LANES), F32),
                    sds((state, inner), F32),
                    sds((state, inner), BF16),
                    sds((8, LANES), F32),
                ),
                [y_in[b], forth[b].state, bc_all[b], s_all[b], seg_col, x_all[b], gating, d_outn, gain_back, head_rows, spread],
                scratch=[*[pltpu.VMEM((SPAN, inner), F32)] * 4, pltpu.VMEM((SPAN, inner), BF16)],
                mib=12,
                us=4,
            )
        )
        ebb.append(Chain(gated[b][5], gated[b][6], decay[b], down[::-1]))
        if b == 0:
            forth[1].step(after=[gated[0][4]])
    carry = [forth[b].state for b in both]
    def inner_back_of(b, after):
        return vmem_call(
            partial(intra_back_body, state, b),
            (sds((SPAN, inner), F32), sds((SPAN, 2 * state), F32)),
            [bc_all[b], xdt_all[b], gated[b][1], gated[b][2], carry[b], s_all[b], st_all[b], seg_col, seg_row],
            scratch=[pltpu.VMEM((SPAN, SPAN), F32)],
            after=after,
            us=0.05,
        )

    inner_back = [inner_back_of(0, [gated[1][4]])]
    ebb[0].step(after=[inner_back[0][1]])
    ways = shards if custom else 1
    pair_rows = (inner + 2 * depth) // ways
    halves = lambda r, c: tuple(sds((max(ways // 2, 1), r, c), BF16) for _ in range(min(ways, 2)))
    pair_grads = vmem_call(
        partial(out_grad_body, ways),
        halves(pair_rows, depth)[:1] + tuple(sds((pair_rows, depth), BF16) for _ in range(ways // 2)),
        [gated[0][0], gated[1][0], cot, gated[0][3], gated[1][3], normed],
        idx=idx,
        scratch=[pltpu.VMEM((inner, depth), F32), pltpu.VMEM((depth, inner), F32)],
        mib=20,
        us=4,
    )
    ebb[0].step(after=[ebb[1].step(after=[pair_grads[0]], us=0.05)], us=20)
    inner_back.append(inner_back_of(1, [ebb[0].state]))
    waits = [inner_back[1][1]]
    if custom:
        first = Reduce(*pair_grads)
        waits.append(first.pair(after=[ebb[0].state]))
    ebb[1].step(after=waits)
    waits = [ebb[1].state]
    if custom:
        waits = [first.relay(after=waits)]
    for hop in range(2, hops - 1):
        ebb[1].step(after=[ebb[0].step(after=waits)])

    back = []
    ebb[0].step(after=waits)
    for b in both:
        if b == 1:
            ebb[1].step(after=[back[0][0]])
        back.append(
            vmem_call(
                partial(mixer_back_body, state, b),
                (sds((SPAN, wide), BF16), sds((HALO, wide), BF16), sds((8, conv_chans), F32), sds((8, LANES), F32)),
                [
                    conv_in[b],
                    dt_raw[b],
                    x_all[b],
                    bc_all[b],
                    xdt_all[b],
                    dt_all[b],
                    s_all[b],
                    seg_col,
                    convw,
                    head_rows,
                    inner_back[b][0],
                    inner_back[b][1],
                    gated[b][1],
                    gated[b][4],
                    carry[b],
                    ebb[b].state,
                    spread,
                    slope_all[b],
                ],
                scratch=[pltpu.VMEM((2 * HALO + SPAN, WIDE), F32), pltpu.VMEM((2 * HALO + SPAN, LANES), F32)],
                us=6,
            )
        )
    d_rows = [back[0][0], back[1][0], back[0][1], back[1][1]]
    waits = [first.step(z_idx, parts, after=[back[1][0]])] if custom else []
    rest_grads = vmem_call(
        partial(in_grad_body, shards, heads, taps, exact),
        halves(depth // ways, wide),
        d_rows + [turned, back[0][2], back[1][2], back[0][3], back[1][3], gated[0][7], gated[1][7]],
        idx=idx,
        scratch=[pltpu.VMEM((rows, wide), BF16), pltpu.VMEM((depth, LANES), F32), pltpu.VMEM((8, LANES), F32)],
        after=waits,
        mib=14,
        us=4,
    )
    if custom:
        rest = Reduce(*rest_grads)
        sent = rest.pair()
    out_rows = vmem_call(
        out_body,
        sds((main, depth), BF16),
        [gated[0][0], gated[1][0], tokens, w_out],
        after=[sent] if custom else [rest_grads[0]],
        us=3,
    )
    if custom:
        sent = rest.relay(after=[out_rows])
        sent = first.step(z_idx, parts, after=[sent])
    in_grad, halo_grad = vmem_call(
        in_back_body,
        (sds((main, depth), F32), sds((batch * HALO, depth), F32)),
        d_rows + [w_all, gated[0][3], gated[1][3], w_gate, cot, tokens, halo_in, gain_front],
        scratch=[pltpu.VMEM((rows, wide), BF16)],
        after=[sent] if custom else [],
        mib=12,
        us=0.05,
    )
    halo_back = lax.ppermute(halo_grad, "seq", down)
    if custom:
        sent = first.step(z_idx, parts, after=[in_grad])
        sent = rest.spread(z_idx, parts, after=[sent])
        sent = first.step(z_idx, parts, after=[sent])
        sent = rest.collect(after=[sent])
        pair_sum = first.step(z_idx, parts, after=[sent])
        rest_parts = rest.quarters if parts == 4 else [rest.total]
    else:
        whole = pair_grads[0][0]
        cuts = ((0, inner), (inner, inner + depth), (inner + depth, inner + 2 * depth))
        shard_sum = lambda v: lax.psum_scatter(v, "fsdp", scatter_dimension=0, tiled=True)
        pair_sum = lax.psum(jnp.concatenate([shard_sum(whole[lo:hi]) for lo, hi in cuts], axis=0).astype(F32), "seq")
        rest_parts = [lax.psum(shard_sum(rest_grads[0][0]).astype(F32), "seq")]
    input_grad = vmem_call(
        halo_add_body, sds(in_grad.shape, F32), [in_grad, halo_back], after=[sent] if custom else []
    ).reshape(1, batch, SPAN, depth)
    width = conv_chans // shards
    grad_in_weight, grad_out_weight, grad_gain, grad_back, grad_conv, grad_bias, head_sums = vmem_call(
        partial(final_body, heads, taps, exact),
        (
            sds((chunk, in_weight.shape[1]), F32),
            sds((rows_out, depth), F32),
            sds((1, chunk), F32),
            sds((1, rows_out), F32),
            sds((taps, width), F32),
            sds((1, width), F32),
            sds((3, heads), F32),
        ),
        [in_weight, line(gain_in), out_weight, line(gain_out), pair_sum] + rest_parts,
        idx=z_idx,
        scratch=[pltpu.VMEM((chunk, wide), F32), pltpu.VMEM((-(-rows_out // LANES) * LANES, LANES), F32)],
    )
    if not exact:
        three = back[0][3] + back[1][3] + gated[0][7] + gated[1][7]
        head_sums = lax.psum(three[:3, :heads], ("fsdp", "seq"))
    return (
        out_rows.reshape(1, batch, SPAN, depth),
        input_grad,
        grad_gain[0],
        grad_in_weight,
        grad_conv.T,
        grad_bias[0],
        head_sums[0],
        head_sums[1],
        head_sums[2],
        grad_back[0],
        grad_out_weight,
    )


def solution(mesh):
    tokens = P("fsdp", None, "seq", None)
    row, matrix = P("fsdp"), P("fsdp", None)
    return jax.shard_map(
        on_device,
        mesh=mesh,
        in_specs=(tokens, P("fsdp", None, None), row, matrix, matrix, row, P(), P(), P(), row, matrix, tokens),
        out_specs=(tokens, tokens, row, matrix, matrix, row, P(), P(), P(), row, matrix),
        check_vma=False,
    )
```

```python
from functools import partial

import jax
import jax.numpy as jnp
from jax import lax
from jax.experimental import pallas as pl
from jax.experimental.pallas import tpu as pltpu
from jax.sharding import PartitionSpec as P

SPAN = 256
HEADDIM = 64
LANES = 128
HALO = 16
WIDE = 256
EPS_NORM = 1e-05
COST = 1e9
OFF = -10000.0
F32 = jnp.float32
BF16 = jnp.bfloat16


def nn(a, b):
    return lax.dot_general(a, b, (((1,), (0,)), ((), ())), preferred_element_type=F32)


def nt(a, b):
    return lax.dot_general(a, b, (((1,), (1,)), ((), ())), preferred_element_type=F32)


def tn(a, b):
    return lax.dot_general(a, b, (((0,), (0,)), ((), ())), preferred_element_type=F32)


def iota(shape, dim):
    return lax.broadcasted_iota(jnp.int32, shape, dim)


def ones_where(cond):
    return jnp.where(cond, 1.0, 0.0)


def split2(v):
    high = v.astype(BF16)
    low = (v - high.astype(F32)).astype(BF16)
    return jnp.concatenate([high, low], axis=1)


def to_heads(values, picks):
    parts = []
    for v in values:
        high = v.astype(BF16)
        parts += [high, (v - high.astype(F32)).astype(BF16)]
    sums = nt(jnp.concatenate(parts, axis=0), picks)
    out, at = [], 0
    for v in values:
        rows = v.shape[0]
        out.append(sums[at : at + rows] + sums[at + rows : at + 2 * rows])
        at += 2 * rows
    return out


def running_sum(tri, v):
    high = v.astype(BF16)
    rest = v - high.astype(F32)
    mid = rest.astype(BF16)
    low = (rest - mid.astype(F32)).astype(BF16)
    return nn(tri, high) + nn(tri, mid) + nn(tri, low)


def sigmoid(v):
    return 0.5 * jnp.tanh(0.5 * v) + 0.5


def silu_slope(v, sig):
    return sig * (1.0 + v * (1.0 - sig))


def softplus(v):
    return jnp.maximum(v, 0.0) + jnp.log1p(jnp.exp(-jnp.abs(v)))


def row_masks(seg_ref, b, taps):
    here = segs_of(seg_ref, b)
    return [ones_where(seg_ref[pl.ds(HALO - j, SPAN), b : b + 1] == here) for j in range(1, taps)]


def segs_of(seg_ref, b):
    return seg_ref[pl.ds(HALO, SPAN), b : b + 1]


def seg_before(seg_ref, b):
    return seg_ref[HALO - 1 : HALO, b : b + 1]


def seg_last(seg_ref, b):
    return seg_ref[HALO + SPAN - 1 : HALO + SPAN, b : b + 1]


def conv_pre(ext_ref, cols, convw_ref, masks):
    taps = len(masks) + 1
    total = convw_ref[taps : taps + 1, cols] + convw_ref[taps - 1 : taps, cols] * ext_ref[pl.ds(HALO, SPAN), :]
    for j in range(1, taps):
        total = total + convw_ref[taps - 1 - j : taps - j, cols] * (
            ext_ref[pl.ds(HALO - j, SPAN), :] * masks[j - 1]
        )
    return total


def vmem_call(body, out_shape, operands, idx=None, scratch=(), mib=8, after=(), us=0.05, hbm=False):
    vm = pl.BlockSpec(memory_space=pltpu.VMEM)
    smem = [] if idx is None else [idx]
    head, tail = len(smem) + len(operands), len(after)

    def run(*refs):
        body(*refs[:head], *refs[head + tail :])

    return pl.pallas_call(
        run,
        out_shape=out_shape,
        in_specs=[pl.BlockSpec(memory_space=pltpu.SMEM)] * len(smem)
        + [pl.BlockSpec(memory_space=pltpu.HBM) if hbm else vm] * len(operands)
        + [pl.BlockSpec(memory_space=pl.ANY)] * tail,
        out_specs=jax.tree.map(lambda _: vm, out_shape),
        scratch_shapes=list(scratch),
        compiler_params=pltpu.CompilerParams(vmem_limit_bytes=mib * 1024 * 1024),
        cost_estimate=pl.CostEstimate(flops=int(us * COST), bytes_accessed=0, transcendentals=0),
        name=body.func.__name__ if isinstance(body, partial) else body.__name__,
    )(*smem, *operands, *after)


def sds(shape, dtype):
    return jax.ShapeDtypeStruct(shape, dtype)


def prep_body(heads, segs_ref, dtb_ref, alog_ref, skip_ref, spread_ref, seg_ref, heads_ref):
    for c0 in range(0, spread_ref.shape[1], WIDE):
        shape = (2 * LANES, WIDE)
        hit = (iota(shape, 0) & (LANES - 1)) == ((iota(shape, 1) + c0) >> 6)
        spread_ref[:, c0 : c0 + WIDE] = ones_where(hit).astype(BF16)
    seg_ref[...] = segs_ref[...].T[0 : HALO + SPAN, :]
    heads_ref[...] = jnp.zeros(heads_ref.shape, F32)
    heads_ref[0:1, :] = jnp.full((1, LANES), OFF, F32)
    for row, ref in enumerate((dtb_ref, alog_ref, skip_ref)):
        heads_ref[row : row + 1, 0:heads] = ref[...].astype(F32)


def small_rows(taps, width):
    third = -(-width // 3)
    return [
        (t, 3 * t + m, m * third, min(third, width - m * third)) for t in range(taps + 1) for m in range(3)
    ]


def pack_body(heads, inner, *refs):
    given, out_ref, end_ref, sems = refs[:5], refs[5], refs[6], refs[-1]
    copies = [pltpu.make_async_copy(a, b, sems.at[i]) for i, (a, b) in enumerate(zip(given, refs[7:12]))]
    for copy in copies:
        copy.start()
    for copy in copies:
        copy.wait()
    w_ref, gain_ref, conv_ref, bias_ref, back_ref = refs[7:12]
    full = w_ref.shape[1] - inner - heads
    taps, width = conv_ref.shape
    flat = lambda ref: ref[...].astype(F32).reshape(1, ref.shape[0])
    out_ref[:, 0:full] = w_ref[:, inner : inner + full]
    end_ref[...] = jnp.zeros(end_ref.shape, F32)
    end_ref[:, 0:heads] = w_ref[:, inner + full :].astype(F32)
    conv, bias, back = conv_ref[...].astype(F32), flat(bias_ref), flat(back_ref)
    for t, row, first, size in small_rows(taps, width):
        value = conv[t : t + 1] if t < taps else bias
        end_ref[row : row + 1, heads : heads + size] = value[:, first : first + size]
    row = 3 * (taps + 1)
    chunk, half = gain_ref.shape[0], back_ref.shape[0] // 2
    end_ref[row : row + 1, heads : heads + chunk] = flat(gain_ref)
    for m in range(2):
        end_ref[row + 1 + m : row + 2 + m, heads : heads + half] = back[:, m * half : (m + 1) * half]
    out_ref[:, full:] = end_ref[...].astype(BF16)


def unpack(heads, taps, shards, end_ref, gain_ref, conv_ref, back_ref):
    chunk = end_ref.shape[0] // shards
    width, half = conv_ref.shape[1] // shards, back_ref.shape[1] // shards // 2
    conv_ref[taps + 1 :, :] = jnp.zeros((7 - taps, conv_ref.shape[1]), F32)
    for i in range(shards):
        at = i * chunk
        for t, row, first, size in small_rows(taps, width):
            conv_ref[t : t + 1, i * width + first : i * width + first + size] = end_ref[
                at + row : at + row + 1, heads : heads + size
            ]
        row = at + 3 * (taps + 1)
        gain_ref[:, i * chunk : (i + 1) * chunk] = end_ref[row : row + 1, heads : heads + chunk]
        for m in range(2):
            first = (2 * i + m) * half
            back_ref[:, first : first + half] = end_ref[row + 1 + m : row + 2 + m, heads : heads + half]


def proj_body(layout, batch, heads, shards, state, *refs):
    idx_ref, tokens_ref, halo_ref, heads_ref, seg_ref, spread_ref = refs[:6]
    pieces = refs[6 : 6 + len(layout)]
    w_ref, normed_ref, gain_ref, convw_ref, back_ref, convin_ref, dtraw_ref = refs[6 + len(layout) : 13 + len(layout)]
    outs = refs[13 + len(layout) : 23 + len(layout)]
    ext_ref, heads_all_ref, end_ref, turned_ref = refs[23 + len(layout) :]
    inner = heads * HEADDIM
    chunk = w_ref.shape[0] // (1 if len(layout) == 1 else 8)

    def store(first, off, view):
        w_ref[pl.ds(pl.multiple_of(first, HALO), view.shape[0]), :] = view[...]

    put_pieces(layout, pieces, idx_ref[0], chunk, store)
    conv_chans = inner + 2 * state
    taps = 4
    end_ref[...] = w_ref[:, conv_chans:].astype(F32)
    unpack(heads, taps, shards, end_ref, gain_ref, convw_ref, back_ref)
    w_ref[:, conv_chans:] = jnp.where(iota(end_ref.shape, 1) < heads, end_ref[...], 0.0).astype(BF16)
    main = tokens_ref.shape[0]
    for ref, first in ((tokens_ref, 0), (halo_ref, main)):
        v = ref[...].astype(F32)
        scale = lax.rsqrt(jnp.mean(v * v, axis=1, keepdims=True) + EPS_NORM)
        normed_ref[pl.ds(first, ref.shape[0]), :] = (v * scale * gain_ref[...]).astype(BF16)
    normed = normed_ref[...]
    raw = nn(normed, w_ref[:, conv_chans : conv_chans + LANES])
    for b in range(batch):
        dtraw_ref[b][...] = raw[b * SPAN : (b + 1) * SPAN].astype(BF16).astype(F32)
    mixer = MixerInput(0, heads_ref, seg_ref, spread_ref, dtraw_ref[0], convin_ref[0], convw_ref, outs)
    mixer.steps(heads_all_ref)
    for c0 in [inner] + list(range(0, inner, WIDE)):
        cols = slice(c0, c0 + WIDE)
        projected = nn(normed, w_ref[:, cols]).astype(BF16)
        for b in range(batch):
            halo0 = batch * SPAN + b * HALO
            convin_ref[b][0:HALO, cols] = projected[halo0 : halo0 + HALO]
            convin_ref[b][HALO : HALO + SPAN, cols] = projected[b * SPAN : (b + 1) * SPAN]
        mixer.columns(c0, inner, state, ext_ref, heads_all_ref, turned_ref)


def second_body(b, inner, state, *refs):
    heads_ref, seg_ref, spread_ref, dtraw_ref, convin_ref, convw_ref = refs[:6]
    ext_ref, heads_all_ref, turned_ref = refs[16:]
    mixer = MixerInput(b, heads_ref, seg_ref, spread_ref, dtraw_ref, convin_ref, convw_ref, refs[6:16])
    mixer.steps(heads_all_ref)
    for c0 in [inner] + list(range(0, inner, WIDE)):
        mixer.columns(c0, inner, state, ext_ref, heads_all_ref, turned_ref)


class MixerInput:
    def __init__(self, b, heads_ref, seg_ref, spread_ref, dtraw_ref, convin_ref, convw_ref, outs):
        self.b, self.heads, self.seg, self.spread = b, heads_ref, seg_ref, spread_ref
        self.dtraw, self.convin, self.convw, self.outs = dtraw_ref, convin_ref, convw_ref, outs

    def steps(self, heads_all_ref):
        b, heads_ref, seg_ref = self.b, self.heads, self.seg
        dt_ref, s_ref, st_ref = self.outs[3:6]
        tri = ones_where(iota((SPAN, SPAN), 0) >= iota((SPAN, SPAN), 1)).astype(BF16)
        self.masks = row_masks(seg_ref, b, 4)
        dt = softplus(self.dtraw[...] + heads_ref[0:1, :])
        dt_ref[...] = dt
        logs = running_sum(tri, dt * -jnp.exp(heads_ref[1:2, :]))
        s_ref[...] = logs
        st_ref[...] = logs.T
        last = logs[SPAN - 1 : SPAN, :]
        same_last = ones_where(segs_of(seg_ref, b) == seg_last(seg_ref, b))
        keep = ones_where(seg_last(seg_ref, b) == seg_before(seg_ref, b))
        heads_all_ref[0:SPAN, :] = split2(dt)
        heads_all_ref[SPAN : 2 * SPAN, :] = split2(jnp.exp(last - logs) * same_last)
        heads_all_ref[2 * SPAN :, :] = split2(jnp.broadcast_to(jnp.exp(last) * keep, (HALO, LANES)))

    def columns(self, c0, inner, state, ext_ref, heads_all_ref, turned_ref):
        x_ref, bc_ref, xdt_ref, _, _, _, fresh_ref, send_ref, decay_ref, slope_ref = self.outs
        cols = slice(c0, c0 + WIDE)
        ext_ref[...] = self.convin[:, cols].astype(F32)
        pre = conv_pre(ext_ref, cols, self.convw, self.masks)
        sig = sigmoid(pre)
        act = pre * sig
        slope_ref[:, cols] = silu_slope(pre, sig).astype(BF16)
        if c0 == inner:
            bc_ref[...] = act.astype(BF16)
            turned_ref[...] = bc_ref[:, 0:state].T
            return
        wide = nn(heads_all_ref[...], self.spread[:, cols])
        x_ref[:, cols] = act
        xdt = (wide[0:SPAN] * act).astype(BF16)
        xdt_ref[:, cols] = xdt
        xt = (wide[SPAN : 2 * SPAN] * xdt.astype(F32)).astype(BF16)
        decay_ref[:, cols] = wide[2 * SPAN : 2 * SPAN + 8]
        fresh = nn(turned_ref[...], xt)
        fresh_ref[:, cols] = fresh
        send_ref[:, cols] = fresh.astype(BF16)


def inside_mask(seg_ref, segr_ref, b, flipped):
    rows, cols = iota((SPAN, SPAN), 0), iota((SPAN, SPAN), 1)
    ordered = rows <= cols if flipped else rows >= cols
    return ordered & (segs_of(seg_ref, b) == segr_ref[b : b + 1, :])


def head_halves(block):
    low = iota(block.shape, 1) < HEADDIM
    zero = jnp.zeros_like(block)
    return jnp.where(low, block, zero), jnp.where(low, zero, block)


def intra_body(state, b, bc_ref, xdt_ref, s_ref, st_ref, seg_ref, segr_ref, y_ref):
    scores = nt(bc_ref[:, state : 2 * state], bc_ref[:, 0:state])
    scores = jnp.where(inside_mask(seg_ref, segr_ref, b, False), scores, 0.0)
    for pair in range(xdt_ref.shape[1] // LANES):
        cols = slice(pair * LANES, (pair + 1) * LANES)
        total = None
        for half, values in enumerate(head_halves(xdt_ref[:, cols])):
            h = 2 * pair + half
            decay = jnp.exp(jnp.minimum(s_ref[:, h : h + 1] - st_ref[h : h + 1, :], 0.0))
            part = nn((scores * decay).astype(BF16), values)
            total = part if total is None else total + part
        y_ref[:, cols] = total


def dense_body(layout, inner, *refs):
    idx_ref, normed_ref, cot_ref = refs[:3]
    pieces = refs[3 : 3 + len(layout)]
    wout_ref, wgate_ref, gating_ref, dout_ref, turned_ref, turn_ref = refs[3 + len(layout) :]
    depth = wgate_ref.shape[0]
    shards = 1 if len(layout) == 1 else 8
    ochunk, gchunk = inner // shards, depth // shards
    half_cols = inner // 2
    def store(owner, off, view):
        wout_ref[pl.ds(pl.multiple_of(owner * ochunk, HALO), ochunk), :] = view[0:ochunk, :]
        for side in range(2):
            wgate_ref[
                pl.ds(pl.multiple_of(owner * gchunk, HALO), gchunk), side * half_cols : (side + 1) * half_cols
            ] = view[ochunk + side * gchunk : ochunk + (side + 1) * gchunk, :]

    put_pieces(layout, pieces, idx_ref[0], 1, store)
    for r0 in range(0, depth, WIDE):
        turn_ref[r0 : r0 + WIDE, :] = normed_ref[:, r0 : r0 + WIDE].T
    for k in range(shards):
        turned_ref[k * gchunk : (k + 1) * gchunk, :] = turn_ref[
            pl.ds(pl.multiple_of((idx_ref[0] ^ k) * gchunk, HALO), gchunk), :
        ]
    normed = normed_ref[0 : cot_ref.shape[0], :]
    cot = cot_ref[...]
    for c0 in range(0, inner, WIDE):
        gating_ref[:, c0 : c0 + WIDE] = nn(normed, wgate_ref[:, c0 : c0 + WIDE])
        dout_ref[:, c0 : c0 + WIDE] = nt(cot, wout_ref[c0 : c0 + WIDE, :])


def gate_body(state, b, *refs):
    (yin_ref, carry_ref, bc_ref, s_ref, seg_ref, x_ref, gating_ref, dout_ref, gain_ref, heads_ref, spread_ref) = refs[:11]
    (outn_ref, dy_ref, ey_ref, dgat_ref, rowterm_ref, grad_ref, send_ref, small_ref) = refs[11:19]
    y_ref, gated_ref, sig_ref, wide_ref, mixed_ref = refs[19:]
    inner = x_ref.shape[1]
    rows = pl.ds(b * SPAN, SPAN)
    c_mat = bc_ref[:, state : 2 * state]
    c_turned = c_mat.T
    carried = ones_where(segs_of(seg_ref, b) == seg_before(seg_ref, b))
    factor = split2(jnp.exp(s_ref[...]) * carried)
    factor = jnp.concatenate([factor, split2(jnp.broadcast_to(heads_ref[2:3, :], (HALO, LANES)))], axis=0)
    sumsq = jnp.zeros((SPAN, 1), F32)
    sumeg = jnp.zeros((SPAN, 1), F32)
    for c0 in range(0, inner, WIDE):
        cols = slice(c0, c0 + WIDE)
        spread = spread_ref[:, cols]
        both = nn(factor, spread)
        wide = both[0:SPAN]
        wide_ref[:, cols] = wide
        y = yin_ref[:, cols] + wide * nn(c_mat, carry_ref[:, cols])
        y_ref[:, cols] = y
        low = (y + both[SPAN : SPAN + 1] * x_ref[:, cols]).astype(BF16)
        mixed_ref[:, cols] = low
        mixed = low.astype(F32)
        gate = gating_ref[rows, cols]
        sig = sigmoid(gate)
        sig_ref[:, cols] = sig
        gated = mixed * (gate * sig)
        gated_ref[:, cols] = gated
        sumsq = sumsq + jnp.sum(gated * gated, axis=1, keepdims=True)
        sumeg = sumeg + jnp.sum(dout_ref[rows, cols] * gain_ref[:, cols] * gated, axis=1, keepdims=True)
    r = lax.rsqrt(sumsq / inner + EPS_NORM)
    coef = r * r * r * (sumeg / inner)
    terms = jnp.zeros((SPAN, LANES), F32)
    skips = jnp.zeros((8, LANES), F32)
    for c0 in range(0, inner, WIDE):
        cols = slice(c0, c0 + WIDE)
        gated = gated_ref[:, cols]
        gain = gain_ref[:, cols]
        dout = dout_ref[rows, cols]
        normal = gated * r
        outn_ref[:, cols] = (normal * gain).astype(BF16)
        y = y_ref[:, cols]
        x = x_ref[:, cols]
        d_gated = r * (dout * gain) - gated * coef
        gate = gating_ref[rows, cols]
        sig = sig_ref[:, cols]
        mixed = mixed_ref[:, cols].astype(F32)
        dgat_ref[:, cols] = (d_gated * mixed * silu_slope(gate, sig)).astype(BF16)
        dy = (d_gated * (gate * sig)).astype(BF16)
        dy_ref[:, cols] = dy
        dyf = dy.astype(F32)
        ey = (wide_ref[:, cols] * dyf).astype(BF16)
        ey_ref[:, cols] = ey
        skip_sum = jnp.broadcast_to(jnp.sum(dyf * x, axis=0, keepdims=True), (HALO, WIDE))
        term, skip = to_heads([dyf * y, skip_sum], spread_ref[0:LANES, cols])
        terms = terms + term
        skips = skips + skip[0:8]
        grad = nn(c_turned, ey)
        grad_ref[:, cols] = grad
        send_ref[:, cols] = grad.astype(BF16)
    rowterm_ref[...] = terms
    small_ref[...] = jnp.where(iota(skips.shape, 0) == 2, skips, 0.0)


def intra_back_body(state, b, *refs):
    (bc_ref, xdt_ref, dy_ref, ey_ref, carry_ref, s_ref, st_ref, seg_ref, segr_ref) = refs[:9]
    dxdt_ref, dbc_ref = refs[9:11]
    acc_ref = refs[11]
    b_mat = bc_ref[:, 0:state]
    c_mat = bc_ref[:, state : 2 * state]
    mask = inside_mask(seg_ref, segr_ref, b, True)
    scores = jnp.where(mask, nt(b_mat, c_mat), 0.0)
    for pair in range(xdt_ref.shape[1] // LANES):
        cols = slice(pair * LANES, (pair + 1) * LANES)
        total = None
        dy_block = dy_ref[:, cols]
        for half, (values, grads) in enumerate(zip(head_halves(xdt_ref[:, cols]), head_halves(dy_block))):
            h = 2 * pair + half
            decay = jnp.exp(jnp.minimum(st_ref[h : h + 1, :] - s_ref[:, h : h + 1], 0.0))
            part = nn((scores * decay).astype(BF16), grads)
            total = part if total is None else total + part
            d_weight = nt(values, dy_block) * decay
            if h == 0:
                acc_ref[...] = d_weight
            else:
                acc_ref[...] += d_weight
        dxdt_ref[:, cols] = total
    d_scores = jnp.where(mask, acc_ref[...], 0.0).astype(BF16)
    dbc_ref[:, 0:state] = nn(d_scores, c_mat)
    dbc_ref[:, state : 2 * state] = tn(d_scores, b_mat) + nt(ey_ref[...], carry_ref[...])


def mixer_back_body(state, b, *refs):
    (convin_ref, dtraw_ref, x_ref, bc_ref, xdt_ref, dt_ref, s_ref, seg_ref, convw_ref, heads_ref) = refs[:10]
    (dxdt_ref, dbc_ref, dy_ref, rowterm_ref, carry_ref, dcarry_ref, spread_ref, slope_ref) = refs[10:18]
    (dmain_ref, dhalo_ref, small_ref, hsmall_ref) = refs[18:22]
    dpre_ref, segs_ref = refs[22:]
    inner = x_ref.shape[1]
    taps = 4
    conv_chans = inner + 2 * state
    rows = HALO + SPAN
    segs_ref[0:rows, :] = seg_ref[...]
    segs_ref[rows:, :] = jnp.zeros((HALO, LANES), F32)
    here = segs_ref[0:rows, b : b + 1]
    masks = [ones_where(segs_ref[pl.ds(j, rows), b : b + 1] == here) for j in range(1, taps)]
    b_mat = bc_ref[:, 0:state]
    logs = s_ref[...]
    dt = dt_ref[...]
    rate = -jnp.exp(heads_ref[1:2, :])
    last = logs[SPAN - 1 : SPAN, :]
    same_last = ones_where(segs_of(seg_ref, b) == seg_last(seg_ref, b))
    keep = ones_where(seg_last(seg_ref, b) == seg_before(seg_ref, b))
    heads_all = jnp.concatenate(
        [
            split2(jnp.exp(last - logs) * same_last),
            split2(dt),
            split2(jnp.broadcast_to(heads_ref[2:3, :], (HALO, LANES))),
        ],
        axis=0,
    )
    col_term = jnp.zeros((SPAN, LANES), F32)
    direct = jnp.zeros((SPAN, LANES), F32)
    last_term = jnp.zeros((HALO, LANES), F32)
    d_b = dbc_ref[:, 0:state]
    dpre_ref[0:HALO, :] = jnp.zeros((HALO, WIDE), F32)
    dpre_ref[HALO + SPAN : HALO + SPAN + HALO, :] = jnp.zeros((HALO, WIDE), F32)
    small_ref[taps + 1 : 8, :] = jnp.zeros((7 - taps, conv_chans), F32)

    def conv_back(cols, d_act):
        ext = convin_ref[:, cols].astype(F32)
        d_pre = d_act * slope_ref[:, cols].astype(F32)
        dpre_ref[pl.ds(HALO, SPAN), :] = d_pre
        small_ref[taps : taps + 1, cols] = jnp.sum(d_pre, axis=0, keepdims=True)
        small_ref[taps - 1 : taps, cols] = jnp.sum(d_pre * ext[HALO:], axis=0, keepdims=True)
        total = convw_ref[taps - 1 : taps, cols] * dpre_ref[pl.ds(0, rows), :]
        for j in range(1, taps):
            moved = masks[j - 1] * dpre_ref[pl.ds(j, rows), :]
            small_ref[taps - 1 - j : taps - j, cols] = jnp.sum(moved * ext, axis=0, keepdims=True)
            total = total + convw_ref[taps - 1 - j : taps - j, cols] * moved
        total = total.astype(BF16)
        dhalo_ref[:, cols] = total[0:HALO]
        dmain_ref[:, cols] = total[HALO : HALO + SPAN]

    for c0 in range(0, inner, WIDE):
        cols = slice(c0, c0 + WIDE)
        spread = spread_ref[:, cols]
        picks = spread_ref[0:LANES, cols]
        d_carry = dcarry_ref[:, cols]
        wide = nn(heads_all, spread)
        tails = wide[0:SPAN]
        xdt = xdt_ref[:, cols].astype(F32)
        d_tail = tails * nn(b_mat, d_carry)
        d_xdt = dxdt_ref[:, cols] + d_tail
        x = x_ref[:, cols]
        from_tail = jnp.sum(xdt * d_tail, axis=0, keepdims=True)
        through = jnp.sum(d_carry.astype(F32) * carry_ref[:, cols].astype(F32), axis=0, keepdims=True)
        both = jnp.concatenate([from_tail, through, jnp.zeros((HALO - 2, WIDE), F32)], axis=0)
        cols_sum, direct_sum, both = to_heads([xdt * d_xdt, x * d_xdt, both], picks)
        col_term = col_term + cols_sum
        direct = direct + direct_sum
        last_term = last_term + both
        d_b = d_b + nt((tails * xdt).astype(BF16), d_carry)
        d_x = wide[SPAN : 2 * SPAN] * d_xdt + wide[2 * SPAN : 2 * SPAN + 1] * dy_ref[:, cols].astype(F32)
        conv_back(cols, d_x)
    conv_back(slice(inner, conv_chans), jnp.concatenate([d_b, dbc_ref[:, state : 2 * state]], axis=1))
    at_end = last_term[0:1, :] + last_term[1:2, :] * (jnp.exp(last) * keep)
    upper = ones_where(iota((SPAN, SPAN), 0) <= iota((SPAN, SPAN), 1)).astype(BF16)
    d_logs = running_sum(upper, rowterm_ref[...] - col_term) + at_end
    d_dt = direct + rate * d_logs
    d_raw = d_dt * sigmoid(dtraw_ref[...] + heads_ref[0:1, :])
    dmain_ref[:, conv_chans : conv_chans + LANES] = d_raw.astype(BF16)
    dhalo_ref[:, conv_chans : conv_chans + LANES] = jnp.zeros((HALO, LANES), BF16)
    hsmall_ref[0:1, :] = jnp.sum(d_raw, axis=0, keepdims=True)
    hsmall_ref[1:2, :] = jnp.sum(dt * d_logs, axis=0, keepdims=True) * rate
    hsmall_ref[2:8, :] = jnp.zeros((6, LANES), F32)


def out_grad_body(shards, *refs):
    (idx_ref, on0_ref, on1_ref, cot_ref, dg0_ref, dg1_ref, normed_ref) = refs[:7]
    outs = refs[7:-2]
    gout_ref, ggate_ref = refs[-2:]
    main = cot_ref.shape[0]
    inner, width = gout_ref.shape
    outn = jnp.concatenate([on0_ref[...], on1_ref[...]], axis=0)
    dgat = jnp.concatenate([dg0_ref[...], dg1_ref[...]], axis=0)
    normed = normed_ref[0:main, :]
    gout_ref[...] = tn(outn, cot_ref[...])
    for c0 in range(0, inner, width):
        ggate_ref[:, c0 : c0 + width] = tn(normed, dgat[:, c0 : c0 + width])
    ochunk, gchunk = inner // shards, width // shards
    for k in range(shards):
        owner = idx_ref[0] ^ k
        ref = outs[0].at[k // 2] if k % 2 == 0 else outs[1 + k // 2]
        ref[0:ochunk, :] = gout_ref[pl.ds(pl.multiple_of(owner * ochunk, HALO), ochunk), :].astype(BF16)
        for side in range(2):
            ref[ochunk + side * gchunk : ochunk + (side + 1) * gchunk, :] = ggate_ref[
                pl.ds(pl.multiple_of(owner * gchunk, HALO), gchunk), side * width : (side + 1) * width
            ].astype(BF16)


def out_body(on0_ref, on1_ref, xin_ref, wout_ref, lout_ref, done_ref):
    done_ref[...] = jnp.zeros(done_ref.shape, F32)
    for b, outn_ref in enumerate((on0_ref, on1_ref)):
        rows = slice(b * SPAN, (b + 1) * SPAN)
        lout_ref[rows, :] = (xin_ref[rows, :].astype(F32) + nn(outn_ref[...], wout_ref[...])).astype(BF16)


def join_rows(m0_ref, m1_ref, h0_ref, h1_ref, all_ref):
    all_ref[0:SPAN, :] = m0_ref[...]
    all_ref[SPAN : 2 * SPAN, :] = m1_ref[...]
    all_ref[2 * SPAN : 2 * SPAN + HALO, :] = h0_ref[...]
    all_ref[2 * SPAN + HALO : 2 * SPAN + 2 * HALO, :] = h1_ref[...]


def in_grad_body(shards, heads, taps, exact, *refs):
    idx_ref, m0_ref, m1_ref, h0_ref, h1_ref, normed_ref = refs[:6]
    conv0_ref, conv1_ref, head0_ref, head1_ref, skip0_ref, skip1_ref = refs[6:12]
    outs = refs[12:-3]
    all_ref, ends_ref, line_ref = refs[-3:]
    join_rows(m0_ref, m1_ref, h0_ref, h1_ref, all_ref)
    depth, wide = normed_ref.shape[0], all_ref.shape[1]
    conv = conv0_ref[...] + conv1_ref[...]
    three = head0_ref[...] + head1_ref[...] + skip0_ref[...] + skip1_ref[...]
    chunk, width = depth // shards, conv.shape[1] // shards
    ends_ref[...] = jnp.zeros(ends_ref.shape, F32)
    for i in range(shards):
        for t, row, first, size in small_rows(taps, width):
            at = i * chunk + row
            ends_ref[at : at + 1, heads : heads + size] = conv[t : t + 1, i * width + first : i * width + first + size]
    if exact:
        line_ref[...] = jnp.zeros(line_ref.shape, F32)
        for m in range(3):
            line_ref[0:1, (m + 1) * heads : (m + 2) * heads] = three[m : m + 1, 0:heads]
        value = line_ref[0:1, :]
        high = value.astype(BF16).astype(F32)
        rows = iota((2 * exact, LANES), 0)
        mine = jnp.where(rows == 2 * idx_ref[1], high, 0.0) + jnp.where(rows == 2 * idx_ref[1] + 1, value - high, 0.0)
        for i in range(shards):
            at = i * chunk + 3 * (taps + 1) + 1
            ends_ref[at : at + 2 * exact, :] = mine
    ways = 1 if len(outs) == 1 else shards
    part = depth // ways
    for c0 in range(0, wide, 384):
        cols = slice(c0, c0 + 384)
        grad = nn(normed_ref[...], all_ref[:, cols])
        for k in range(ways):
            share = grad[k * part : (k + 1) * part]
            out_ref = outs[k % 2].at[k // 2]
            if c0 + 384 < wide:
                out_ref[:, cols] = share.astype(BF16)
                continue
            out_ref[:, c0 : wide - LANES] = share[:, : 384 - LANES].astype(BF16)
            first = pl.multiple_of((idx_ref[0] ^ k) * part, 8)
            out_ref[:, wide - LANES :] = (share[:, 384 - LANES :] + ends_ref[pl.ds(first, part), :]).astype(BF16)


def in_back_body(*refs):
    m0_ref, m1_ref, h0_ref, h1_ref, w_ref, dg0_ref, dg1_ref, wgate_ref, cot_ref, xin_ref, halo_ref, gain_ref = refs[:12]
    igrad_ref, hgrad_ref, all_ref = refs[12:]
    main = cot_ref.shape[0]
    join_rows(m0_ref, m1_ref, h0_ref, h1_ref, all_ref)
    d_normed = nt(all_ref[...], w_ref[...])
    gain = gain_ref[...]

    def back(dn, v):
        q = lax.rsqrt(jnp.mean(v * v, axis=1, keepdims=True) + EPS_NORM)
        e = dn * gain
        return q * e - v * (q * q * q * jnp.mean(e * v, axis=1, keepdims=True))

    for b, dgat_ref in enumerate((dg0_ref, dg1_ref)):
        rows = slice(b * SPAN, (b + 1) * SPAN)
        d_both = d_normed[rows] + nt(dgat_ref[...], wgate_ref[...])
        igrad_ref[rows, :] = cot_ref[rows, :].astype(F32) + back(d_both, xin_ref[rows, :].astype(F32))
    hgrad_ref[...] = back(d_normed[main:], halo_ref[...].astype(F32))


def xor_pairs(size, k):
    return [(i, i ^ k) for i in range(size)]


def stack_body(*refs):
    out_ref = refs[-1]
    for i, ref in enumerate(refs[:-1]):
        out_ref[i] = ref[...]


def rows_body(top_ref, low_ref, out_ref):
    half = top_ref.shape[0]
    out_ref[0:half, :] = top_ref[...]
    out_ref[half:, :] = low_ref[...]


def stack(parts, after=()):
    return vmem_call(stack_body, sds((len(parts),) + parts[0].shape, BF16), parts, after=after)


def layout_of(pieces):
    return [v for v, _ in pieces], tuple(places for _, places in pieces)


def put_pieces(layout, refs, idx, chunk, store):
    for ref, places in zip(refs, layout):
        for sub, k, off in places:
            view = ref if sub is None else ref.at[sub]
            store((idx ^ k) * chunk + off, off, view)


def combine_body(last, *refs):
    if last:
        got_ref, carry_ref, out_ref = refs
        out_ref[...] = got_ref[...] + carry_ref[...]
        return
    first = len(refs) == 5
    got_ref, fresh_ref, decay_ref = refs[:3]
    out_ref, send_ref = refs[-2:]
    state = got_ref[...] if first else got_ref[...] + refs[3][...]
    out_ref[...] = state
    send_ref[...] = (fresh_ref[...] + decay_ref[0:1, :] * state.astype(F32)).astype(BF16)


class Chain:
    def __init__(self, fresh, send, decay, pairs):
        self.fresh, self.send, self.decay, self.pairs = fresh, send, decay, pairs
        self.state = None
        self.hop = 0
        self.start()

    def start(self):
        self.got = lax.ppermute(self.send, "seq", [self.pairs[self.hop]])

    def step(self, after=(), us=0.05):
        shape = sds(self.got.shape, BF16)
        prior = [] if self.state is None else [self.state]
        if self.hop == len(self.pairs) - 1:
            if prior:
                self.state = vmem_call(partial(combine_body, True), shape, [self.got] + prior, after=after)
            else:
                self.state = self.got
            return self.state
        self.state, self.send = vmem_call(
            partial(combine_body, False),
            (shape, shape),
            [self.got, self.fresh, self.decay] + prior,
            after=after,
            us=us,
        )
        self.hop += 1
        self.start()
        return self.state


def swap(v, k):
    return lax.ppermute(v, "fsdp", xor_pairs(8, k))


def pair_body(even_ref, *refs):
    own_ref, side_ref, down_ref, top_ref, low_ref = refs[-5:]
    got = refs[:-5] if len(refs) > 6 else [refs[0].at[i] for i in range(4)]
    half = top_ref.shape[0]
    add = lambda s: even_ref[s].astype(F32) + got[s][...].astype(F32)
    far = add(3).astype(BF16)
    top_ref[...] = far[0:half]
    low_ref[...] = far[half:]
    own_ref[...] = add(0)
    side_ref[...] = add(1)
    down_ref[...] = add(2)


def relay_body(side_ref, down_ref, top_ref, low_ref, side_out, down_out):
    half = top_ref.shape[0]
    side_out[0:half, :] = side_ref[0:half, :].astype(BF16)
    side_out[half:, :] = (side_ref[half:, :] + low_ref[...].astype(F32)).astype(BF16)
    down_out[0:half, :] = (down_ref[0:half, :] + top_ref[...].astype(F32)).astype(BF16)
    down_out[half:, :] = down_ref[half:, :].astype(BF16)


class Reduce:
    def __init__(self, even, *odd):
        self.even, self.stage = even, 0
        self.got = [swap(v, 1) for v in odd]

    def pair(self, after=()):
        _, rows, cols = self.even.shape
        full, half = sds((rows, cols), F32), sds((rows // 2, cols), BF16)
        self.own, self.side, self.down, top, low = vmem_call(
            pair_body, (full, full, full, half, half), [self.even] + self.got, after=after
        )
        self.top, self.low = swap(top, 2), swap(low, 4)
        return self.own

    def relay(self, after=()):
        shape = sds(self.own.shape, BF16)
        side, down = vmem_call(relay_body, (shape, shape), [self.side, self.down, self.top, self.low], after=after)
        self.side, self.down = swap(side, 2), swap(down, 4)
        return side

    def step(self, z, parts, after=()):
        rows, cols = self.own.shape
        along = lambda v, k: lax.ppermute(v, "seq", xor_pairs(parts, k))
        stage, self.stage = self.stage, self.stage + 1
        if parts != 4:
            if stage == 0:
                total = self.own + self.side.astype(F32) + self.down.astype(F32)
                self.total = lax.psum(total, "seq")
            return self.total
        f32, bf16 = lambda n: sds((n, cols), F32), lambda n: sds((n, cols), BF16)
        whole, half = pltpu.VMEM((rows, cols), F32), pltpu.VMEM((rows // 2, cols), F32)
        if stage == 0:
            given = [self.own, self.side, self.down]
            self.keep, send = vmem_call(
                halve_body, (f32(rows // 2), bf16(rows // 2)), given, idx=z, scratch=[whole], after=after
            )
            self.got = along(send, 1)
            return self.keep
        if stage == 1:
            given = [self.keep, self.got]
            self.keep, send = vmem_call(
                fold_body, (f32(rows // 4), bf16(rows // 4)), given, idx=z, scratch=[half], after=after
            )
            self.got = along(send, 2)
            return self.keep
        if stage == 2:
            self.keep = vmem_call(total_body, bf16(rows // 4), [self.keep, self.got], after=after)
            self.got = along(self.keep, 2)
            return self.keep
        if stage == 3:
            given = [self.keep, self.got]
            self.keep = vmem_call(partial(unfold_body, 1), bf16(rows // 2), given, idx=z, scratch=[half], after=after)
            self.got = along(self.keep, 1)
            return self.keep
        given = [self.keep, self.got]
        return vmem_call(partial(unfold_body, 0), f32(rows), given, idx=z, scratch=[whole], after=after)

    def spread(self, z, parts, after=()):
        rows, cols = self.own.shape
        self.parts, self.z = parts, z
        if parts != 4:
            total = self.own + self.side.astype(F32) + self.down.astype(F32)
            self.total = lax.psum(total, "seq")
            return self.total
        cut = sds((rows // 4, cols), BF16)
        mine, *others = vmem_call(
            spread_body,
            (sds((rows // 4, cols), F32), cut, cut, cut),
            [self.own, self.side, self.down],
            idx=z,
            scratch=[pltpu.VMEM((rows, cols), F32)],
            after=after,
        )
        self.mine = mine
        self.others = [lax.ppermute(v, "seq", xor_pairs(4, k + 1)) for k, v in enumerate(others)]
        return mine

    def collect(self, after=()):
        if self.parts != 4:
            return self.total
        part = vmem_call(collect_body, sds(self.mine.shape, BF16), [self.mine] + self.others, after=after, us=30)
        self.quarters = [part] + [lax.ppermute(part, "seq", xor_pairs(4, k)) for k in (1, 2, 3)]
        return part


def halve_body(z_ref, own_ref, side_ref, down_ref, keep_ref, send_ref, all_ref):
    all_ref[...] = own_ref[...] + side_ref[...].astype(F32) + down_ref[...].astype(F32)
    rows = keep_ref.shape[0]
    bit = z_ref[0] & 1
    keep_ref[...] = all_ref[pl.ds(pl.multiple_of(bit * rows, 8), rows), :]
    send_ref[...] = all_ref[pl.ds(pl.multiple_of((1 - bit) * rows, 8), rows), :].astype(BF16)


def fold_body(z_ref, half_ref, got_ref, keep_ref, send_ref, all_ref):
    all_ref[...] = half_ref[...] + got_ref[...].astype(F32)
    rows = keep_ref.shape[0]
    bit = (z_ref[0] >> 1) & 1
    keep_ref[...] = all_ref[pl.ds(pl.multiple_of(bit * rows, 8), rows), :]
    send_ref[...] = all_ref[pl.ds(pl.multiple_of((1 - bit) * rows, 8), rows), :].astype(BF16)


def total_body(keep_ref, got_ref, out_ref):
    out_ref[...] = (keep_ref[...] + got_ref[...].astype(F32)).astype(BF16)


def unfold_body(shift, z_ref, mine_ref, got_ref, out_ref, all_ref):
    rows = mine_ref.shape[0]
    bit = (z_ref[0] >> shift) & 1
    all_ref[pl.ds(pl.multiple_of(bit * rows, 8), rows), :] = mine_ref[...].astype(F32)
    all_ref[pl.ds(pl.multiple_of((1 - bit) * rows, 8), rows), :] = got_ref[...].astype(F32)
    out_ref[...] = all_ref[...].astype(out_ref.dtype)


def spread_body(z_ref, own_ref, side_ref, down_ref, mine_ref, one_ref, two_ref, three_ref, all_ref):
    all_ref[...] = own_ref[...] + side_ref[...].astype(F32) + down_ref[...].astype(F32)
    rows = mine_ref.shape[0]
    for k, ref in enumerate((mine_ref, one_ref, two_ref, three_ref)):
        first = pl.multiple_of((z_ref[0] ^ k) * rows, 8)
        ref[...] = all_ref[pl.ds(first, rows), :].astype(ref.dtype)


def collect_body(mine_ref, one_ref, two_ref, three_ref, out_ref):
    total = mine_ref[...] + one_ref[...].astype(F32) + two_ref[...].astype(F32) + three_ref[...].astype(F32)
    out_ref[...] = total.astype(BF16)


def final_body(heads, taps, sources, idx_ref, *refs):
    w_ref, gain_ref, wout_ref, back_ref, pair_ref = refs[:5]
    quarters = refs[5:-9]
    grad_ref, gout_ref, ggain_ref, gback_ref, conv_ref, bias_ref, heads_ref = refs[-9:-2]
    rest_ref, sums_ref = refs[-2:]
    rows = quarters[0].shape[0]
    for k, ref in enumerate(quarters):
        first = pl.multiple_of((idx_ref[0] ^ k) * rows, 8) if len(quarters) > 1 else 0
        rest_ref[pl.ds(first, rows), :] = ref[...].astype(F32)
    chunk, half = grad_ref.shape[0], pair_ref.shape[1]
    rows_out = gout_ref.shape[0]
    grad_ref[:, 0:half] = pair_ref[rows_out : rows_out + chunk, :]
    grad_ref[:, half : 2 * half] = pair_ref[rows_out + chunk : rows_out + 2 * chunk, :]
    grad_ref[:, 2 * half :] = rest_ref[:, 0 : grad_ref.shape[1] - 2 * half]
    gout_ref[...] = pair_ref[0:rows_out, :]
    total = jnp.sum(w_ref[...].astype(F32) * grad_ref[...], axis=1, keepdims=True)
    sums_ref[0:chunk, :] = jnp.broadcast_to(total, (chunk, LANES))
    ggain_ref[...] = sums_ref[...].T[0:1, 0:chunk] / gain_ref[...].astype(F32)
    total = jnp.sum(wout_ref[...].astype(F32) * gout_ref[...], axis=1, keepdims=True)
    sums_ref[0:rows_out, :] = jnp.broadcast_to(total, (rows_out, LANES))
    gback_ref[...] = sums_ref[...].T[0:1, 0:rows_out] / back_ref[...].astype(F32)
    width = conv_ref.shape[1]
    lane0 = rest_ref.shape[1] - LANES + heads
    for t, row, first, size in small_rows(taps, width):
        value = rest_ref[row : row + 1, lane0 : lane0 + size]
        if t < taps:
            conv_ref[t : t + 1, first : first + size] = value
        else:
            bias_ref[:, first : first + size] = value
    if sources:
        row = 3 * (taps + 1) + 1
        total = jnp.sum(rest_ref[row : row + 2 * sources, rest_ref.shape[1] - LANES :], axis=0, keepdims=True)
        for m in range(3):
            heads_ref[m : m + 1, :] = total[:, (m + 1) * heads : (m + 2) * heads]
    else:
        heads_ref[...] = jnp.zeros(heads_ref.shape, F32)


def halo_add_body(grad_ref, halo_ref, out_ref):
    out_ref[...] = grad_ref[...]
    for b in range(out_ref.shape[0] // SPAN):
        rows = slice((b + 1) * SPAN - HALO, (b + 1) * SPAN)
        out_ref[rows, :] = grad_ref[rows, :] + halo_ref[b * HALO : (b + 1) * HALO, :]


def on_device(
    layer_input,
    segment_ids,
    gain_in,
    in_weight,
    conv_weight,
    conv_bias,
    dt_bias,
    a_log,
    skip_gain,
    gain_out,
    out_weight,
    cotangent,
):
    shards, parts = lax.axis_size("fsdp"), lax.axis_size("seq")
    at_fsdp, at_seq = lax.axis_index("fsdp"), lax.axis_index("seq")
    _, batch, part_len, depth = layer_input.shape
    heads = dt_bias.shape[0]
    inner = heads * HEADDIM
    taps = conv_weight.shape[1]
    conv_chans = conv_weight.shape[0] * shards
    state = (conv_chans - inner) // 2
    assert part_len == SPAN and batch == 2 and state == LANES and taps == 4
    wide = conv_chans + LANES
    main = batch * SPAN
    chunk = depth // shards
    up = [(i, i + 1) for i in range(parts - 1)]
    down = [(i + 1, i) for i in range(parts - 1)]

    custom = shards == 8 and chunk % (2 * HALO) == 0
    rows_out = inner // shards
    line = lambda v: v.reshape(1, -1)
    w_rest = vmem_call(
        partial(pack_body, heads, inner),
        sds((chunk, wide), BF16),
        [in_weight, gain_in, conv_weight.T, conv_bias, gain_out],
        scratch=[
            pltpu.VMEM((chunk, LANES), F32),
            *[pltpu.VMEM(v.shape, BF16) for v in (in_weight, gain_in, conv_weight.T, conv_bias, gain_out)],
            pltpu.SemaphoreType.DMA((5,)),
        ],
        hbm=True,
        mib=60,
    )
    segs = jnp.pad(segment_ids[0], ((0, 0), (HALO, 0)), constant_values=-1).astype(F32)
    segs = lax.dynamic_slice_in_dim(segs, at_seq * SPAN, HALO + SPAN, 1)
    seg_row = jnp.pad(segs[:, HALO:], ((0, 8 - batch), (0, 0)))
    segs = jnp.pad(segs, ((0, LANES - batch), (0, -(HALO + SPAN) % LANES)))
    spread, seg_col, head_rows = vmem_call(
        partial(prep_body, heads),
        (sds((2 * LANES, inner), BF16), sds((HALO + SPAN, LANES), F32), sds((8, LANES), F32)),
        [segs, line(dt_bias), line(a_log), line(skip_gain)],
        after=[w_rest],
    )
    w_pair = jnp.concatenate([out_weight, in_weight[:, : inner // 2], in_weight[:, inner // 2 : inner]], axis=0)
    exact = shards * parts if custom and 3 * (taps + 1) + 1 + 2 * shards * parts <= chunk else 0
    me = (at_seq * shards + at_fsdp).astype(jnp.int32)
    idx = jnp.stack([at_fsdp.astype(jnp.int32) if custom else jnp.int32(0), me])
    z_idx = at_seq.astype(jnp.int32).reshape(1)
    halo_in = lax.ppermute(layer_input[0, :, SPAN - HALO :, :], "seq", up).reshape(batch * HALO, depth)
    if custom:
        side, down_w = swap(w_rest, 2), swap(w_rest, 4)
        early = (side, down_w, seg_col, seg_row, head_rows, idx, z_idx, w_pair, halo_in)
        side, down_w, seg_col, seg_row, head_rows, idx, z_idx, w_pair, halo_in = lax.optimization_barrier(early)
        top, low = swap(down_w[: chunk // 2], 2), swap(side[chunk // 2 :], 4)
        near = stack([w_rest, side, down_w])
        near_other = swap(near, 1)
        far = vmem_call(rows_body, sds((chunk, wide), BF16), [top, low], after=[near])
        far_other = swap(far, 1)
        rest_pieces = [
            (w_rest, [(None, 0, 0)]),
            (side, [(None, 2, 0)]),
            (down_w, [(None, 4, 0)]),
            (far, [(None, 6, 0)]),
            (near_other, [(0, 1, 0), (1, 3, 0), (2, 5, 0)]),
            (far_other, [(None, 7, 0)]),
        ]
        w_pair, _ = lax.optimization_barrier((w_pair, far))
        side, down_w = swap(w_pair, 2), swap(w_pair, 4)
        pair_own = [w_pair, side, down_w]
    else:
        rest_pieces = [(lax.all_gather(w_rest, "fsdp", axis=0, tiled=True), [(None, 0, 0)])]
        whole = lax.all_gather(w_pair, "fsdp", axis=0)
        pair_own = [
            jnp.concatenate(
                [
                    whole[:, :rows_out].reshape(inner, depth),
                    whole[:, rows_out : rows_out + chunk].reshape(depth, depth),
                    whole[:, rows_out + chunk :].reshape(depth, depth),
                ],
                axis=0,
            )
        ]
    tokens = layer_input.reshape(main, depth)
    cot = cotangent.reshape(main, depth)
    both = range(batch)

    rows = main + batch * HALO
    rest_values, layout = layout_of(rest_pieces)
    each = lambda shape, dtype: tuple(sds(shape, dtype) for _ in both)
    mixed_shapes = [
        sds((SPAN, inner), F32),
        sds((SPAN, 2 * state), BF16),
        sds((SPAN, inner), BF16),
        sds((SPAN, LANES), F32),
        sds((SPAN, LANES), F32),
        sds((LANES, SPAN), F32),
        sds((state, inner), F32),
        sds((state, inner), BF16),
        sds((8, inner), F32),
        sds((SPAN, conv_chans), BF16),
    ]
    ext = pltpu.VMEM((HALO + SPAN, WIDE), F32)
    heads_all = pltpu.VMEM((2 * SPAN + HALO, 2 * LANES), BF16)
    turned = pltpu.VMEM((state, SPAN), BF16)
    proj = vmem_call(
        partial(proj_body, layout, batch, heads, shards, state),
        (
            sds((depth, wide), BF16),
            sds((rows, depth), BF16),
            sds((1, depth), F32),
            sds((8, conv_chans), F32),
            sds((1, inner), F32),
            each((HALO + SPAN, conv_chans), BF16),
            each((SPAN, LANES), F32),
            *mixed_shapes,
        ),
        [tokens, halo_in, head_rows, seg_col, spread] + rest_values,
        idx=idx,
        scratch=[ext, heads_all, pltpu.VMEM((depth, LANES), F32), turned],
        us=10,
    )
    w_all, normed, gain_front, convw, gain_back, conv_in, dt_raw = proj[:7]
    forth = [Chain(proj[13], proj[14], proj[15], up)]
    other = vmem_call(
        partial(second_body, 1, inner, state),
        tuple(mixed_shapes),
        [head_rows, seg_col, spread, dt_raw[1], conv_in[1], convw],
        scratch=[ext, heads_all, turned],
        us=3,
    )
    x_all, bc_all, xdt_all, dt_all, s_all, st_all, fresh, send, decay, slope_all = zip(proj[7:], other)

    if custom:
        far_w, pair_own[1], _ = lax.optimization_barrier((pair_own[2], pair_own[1], w_all))
        pair_own.append(swap(far_w, 2))

    hops = len(up)
    second, forth[0].got = lax.optimization_barrier((send[1], forth[0].got))
    forth.append(Chain(fresh[1], second, decay[1], up))
    forth[0].step(after=[send[1]], us=0.05)
    y_in = []
    for b in both:
        y_in.append(
            vmem_call(
                partial(intra_body, state, b),
                sds((SPAN, inner), F32),
                [bc_all[b], xdt_all[b], s_all[b], st_all[b], seg_col, seg_row],
                after=[forth[0].state, pair_own[2]] if custom else [forth[0].state],
                us=2,
            )
        )
    forth[0].step(after=[forth[1].step(after=y_in, us=0.05)], us=0.05)
    if custom:
        *pair_own, _ = lax.optimization_barrier((*pair_own, forth[0].state))
        pair_pieces = [(v, [(None, 2 * m, 0)]) for m, v in enumerate(pair_own)]
        pair_pieces += [(swap(v, 1), [(None, 2 * m + 1, 0)]) for m, v in enumerate(pair_own)]
    else:
        pair_pieces = [(pair_own[0], [(None, 0, 0)])]
    pair_values, layout2 = layout_of(pair_pieces)
    w_out, w_gate, gating, d_outn, turned = vmem_call(
        partial(dense_body, layout2, inner),
        (sds((inner, depth), BF16), sds((depth, inner), BF16), sds((main, inner), F32), sds((main, inner), F32), sds((depth, rows), BF16)),
        [normed, cot] + pair_values,
        idx=idx,
        scratch=[pltpu.VMEM((depth, rows), BF16)],
        after=[forth[0].state],
        us=3,
    )
    forth[1].step(after=[gating])
    for hop in range(2, hops - 1):
        forth[1].step(after=[forth[0].step(after=[forth[1].state])])
    forth[0].step(after=[forth[1].state])

    gated, ebb = [], []
    for b in both:
        gated.append(
            vmem_call(
                partial(gate_body, state, b),
                (
                    sds((SPAN, inner), BF16),
                    sds((SPAN, inner), BF16),
                    sds((SPAN, inner), BF16),
                    sds((SPAN, inner), BF16),
                    sds((SPAN, LANES), F32),
                    sds((state, inner), F32),
                    sds((state, inner), BF16),
                    sds((8, LANES), F32),
                ),
                [y_in[b], forth[b].state, bc_all[b], s_all[b], seg_col, x_all[b], gating, d_outn, gain_back, head_rows, spread],
                scratch=[*[pltpu.VMEM((SPAN, inner), F32)] * 4, pltpu.VMEM((SPAN, inner), BF16)],
                mib=12,
                us=4,
            )
        )
        ebb.append(Chain(gated[b][5], gated[b][6], decay[b], down[::-1]))
        if b == 0:
            forth[1].step(after=[gated[0][4]])
    carry = [forth[b].state for b in both]
    def inner_back_of(b, after):
        return vmem_call(
            partial(intra_back_body, state, b),
            (sds((SPAN, inner), F32), sds((SPAN, 2 * state), F32)),
            [bc_all[b], xdt_all[b], gated[b][1], gated[b][2], carry[b], s_all[b], st_all[b], seg_col, seg_row],
            scratch=[pltpu.VMEM((SPAN, SPAN), F32)],
            after=after,
            us=0.05,
        )

    inner_back = [inner_back_of(0, [gated[1][4]])]
    ebb[0].step(after=[inner_back[0][1]])
    ways = shards if custom else 1
    pair_rows = (inner + 2 * depth) // ways
    halves = lambda r, c: tuple(sds((max(ways // 2, 1), r, c), BF16) for _ in range(min(ways, 2)))
    pair_grads = vmem_call(
        partial(out_grad_body, ways),
        halves(pair_rows, depth)[:1] + tuple(sds((pair_rows, depth), BF16) for _ in range(ways // 2)),
        [gated[0][0], gated[1][0], cot, gated[0][3], gated[1][3], normed],
        idx=idx,
        scratch=[pltpu.VMEM((inner, depth), F32), pltpu.VMEM((depth, inner), F32)],
        mib=20,
        us=4,
    )
    ebb[0].step(after=[ebb[1].step(after=[pair_grads[0]], us=0.05)], us=20)
    inner_back.append(inner_back_of(1, [ebb[0].state]))
    waits = [inner_back[1][1]]
    if custom:
        first = Reduce(*pair_grads)
        waits.append(first.pair(after=[ebb[0].state]))
    ebb[1].step(after=waits)
    waits = [ebb[1].state]
    if custom:
        waits = [first.relay(after=waits)]
    for hop in range(2, hops - 1):
        ebb[1].step(after=[ebb[0].step(after=waits)])

    back = []
    ebb[0].step(after=waits)
    for b in both:
        if b == 1:
            ebb[1].step(after=[back[0][0]])
        back.append(
            vmem_call(
                partial(mixer_back_body, state, b),
                (sds((SPAN, wide), BF16), sds((HALO, wide), BF16), sds((8, conv_chans), F32), sds((8, LANES), F32)),
                [
                    conv_in[b],
                    dt_raw[b],
                    x_all[b],
                    bc_all[b],
                    xdt_all[b],
                    dt_all[b],
                    s_all[b],
                    seg_col,
                    convw,
                    head_rows,
                    inner_back[b][0],
                    inner_back[b][1],
                    gated[b][1],
                    gated[b][4],
                    carry[b],
                    ebb[b].state,
                    spread,
                    slope_all[b],
                ],
                scratch=[pltpu.VMEM((2 * HALO + SPAN, WIDE), F32), pltpu.VMEM((2 * HALO + SPAN, LANES), F32)],
                us=6,
            )
        )
    d_rows = [back[0][0], back[1][0], back[0][1], back[1][1]]
    waits = [first.step(z_idx, parts, after=[back[1][0]])] if custom else []
    rest_grads = vmem_call(
        partial(in_grad_body, shards, heads, taps, exact),
        halves(depth // ways, wide),
        d_rows + [turned, back[0][2], back[1][2], back[0][3], back[1][3], gated[0][7], gated[1][7]],
        idx=idx,
        scratch=[pltpu.VMEM((rows, wide), BF16), pltpu.VMEM((depth, LANES), F32), pltpu.VMEM((8, LANES), F32)],
        after=waits,
        mib=14,
        us=4,
    )
    if custom:
        rest = Reduce(*rest_grads)
        sent = rest.pair()
    out_rows, out_done = vmem_call(
        out_body,
        (sds((main, depth), BF16), sds((8, LANES), F32)),
        [gated[0][0], gated[1][0], tokens, w_out],
        after=[sent] if custom else [rest_grads[0]],
        us=3,
    )
    if custom:
        sent = rest.relay(after=[out_done])
        sent = first.step(z_idx, parts, after=[sent])
    in_grad, halo_grad = vmem_call(
        in_back_body,
        (sds((main, depth), F32), sds((batch * HALO, depth), F32)),
        d_rows + [w_all, gated[0][3], gated[1][3], w_gate, cot, tokens, halo_in, gain_front],
        scratch=[pltpu.VMEM((rows, wide), BF16)],
        after=[sent] if custom else [],
        mib=12,
        us=0.05,
    )
    halo_back = lax.ppermute(halo_grad, "seq", down)
    if custom:
        sent = first.step(z_idx, parts, after=[in_grad])
        sent = rest.spread(z_idx, parts, after=[sent])
        sent = first.step(z_idx, parts, after=[sent])
        sent = rest.collect(after=[sent])
        pair_sum = first.step(z_idx, parts, after=[sent])
        rest_parts = rest.quarters if parts == 4 else [rest.total]
    else:
        whole = pair_grads[0][0]
        cuts = ((0, inner), (inner, inner + depth), (inner + depth, inner + 2 * depth))
        shard_sum = lambda v: lax.psum_scatter(v, "fsdp", scatter_dimension=0, tiled=True)
        pair_sum = lax.psum(jnp.concatenate([shard_sum(whole[lo:hi]) for lo, hi in cuts], axis=0).astype(F32), "seq")
        rest_parts = [lax.psum(shard_sum(rest_grads[0][0]).astype(F32), "seq")]
    input_grad = vmem_call(
        halo_add_body, sds(in_grad.shape, F32), [in_grad, halo_back], after=[sent] if custom else []
    ).reshape(1, batch, SPAN, depth)
    width = conv_chans // shards
    grad_in_weight, grad_out_weight, grad_gain, grad_back, grad_conv, grad_bias, head_sums = vmem_call(
        partial(final_body, heads, taps, exact),
        (
            sds((chunk, in_weight.shape[1]), F32),
            sds((rows_out, depth), F32),
            sds((1, chunk), F32),
            sds((1, rows_out), F32),
            sds((taps, width), F32),
            sds((1, width), F32),
            sds((3, heads), F32),
        ),
        [in_weight, line(gain_in), out_weight, line(gain_out), pair_sum] + rest_parts,
        idx=z_idx,
        scratch=[pltpu.VMEM((chunk, wide), F32), pltpu.VMEM((-(-rows_out // LANES) * LANES, LANES), F32)],
    )
    if not exact:
        three = back[0][3] + back[1][3] + gated[0][7] + gated[1][7]
        head_sums = lax.psum(three[:3, :heads], ("fsdp", "seq"))
    return (
        out_rows.reshape(1, batch, SPAN, depth),
        input_grad,
        grad_gain[0],
        grad_in_weight,
        grad_conv.T,
        grad_bias[0],
        head_sums[0],
        head_sums[1],
        head_sums[2],
        grad_back[0],
        grad_out_weight,
    )


def solution(mesh):
    tokens = P("fsdp", None, "seq", None)
    row, matrix = P("fsdp"), P("fsdp", None)
    return jax.shard_map(
        on_device,
        mesh=mesh,
        in_specs=(tokens, P("fsdp", None, None), row, matrix, matrix, row, P(), P(), P(), row, matrix, tokens),
        out_specs=(tokens, tokens, row, matrix, matrix, row, P(), P(), P(), row, matrix),
        check_vma=False,
    )
```

```python
from functools import partial

import jax
import jax.numpy as jnp
from jax import lax
from jax.experimental import pallas as pl
from jax.experimental.pallas import tpu as pltpu
from jax.sharding import PartitionSpec as P

SPAN = 256
HEADDIM = 64
LANES = 128
HALO = 16
WIDE = 256
EPS_NORM = 1e-05
COST = 1e9
OFF = -10000.0
F32 = jnp.float32
BF16 = jnp.bfloat16


def nn(a, b):
    return lax.dot_general(a, b, (((1,), (0,)), ((), ())), preferred_element_type=F32)


def nt(a, b):
    return lax.dot_general(a, b, (((1,), (1,)), ((), ())), preferred_element_type=F32)


def tn(a, b):
    return lax.dot_general(a, b, (((0,), (0,)), ((), ())), preferred_element_type=F32)


def iota(shape, dim):
    return lax.broadcasted_iota(jnp.int32, shape, dim)


def ones_where(cond):
    return jnp.where(cond, 1.0, 0.0)


def split2(v):
    high = v.astype(BF16)
    low = (v - high.astype(F32)).astype(BF16)
    return jnp.concatenate([high, low], axis=1)


def to_heads(values, picks):
    parts = []
    for v in values:
        high = v.astype(BF16)
        parts += [high, (v - high.astype(F32)).astype(BF16)]
    sums = nt(jnp.concatenate(parts, axis=0), picks)
    out, at = [], 0
    for v in values:
        rows = v.shape[0]
        out.append(sums[at : at + rows] + sums[at + rows : at + 2 * rows])
        at += 2 * rows
    return out


def running_sum(tri, v):
    high = v.astype(BF16)
    rest = v - high.astype(F32)
    mid = rest.astype(BF16)
    low = (rest - mid.astype(F32)).astype(BF16)
    return nn(tri, high) + nn(tri, mid) + nn(tri, low)


def sigmoid(v):
    return 0.5 * jnp.tanh(0.5 * v) + 0.5


def silu_slope(v, sig):
    return sig * (1.0 + v * (1.0 - sig))


def softplus(v):
    return jnp.maximum(v, 0.0) + jnp.log1p(jnp.exp(-jnp.abs(v)))


def row_masks(seg_ref, b, taps):
    here = segs_of(seg_ref, b)
    return [ones_where(seg_ref[pl.ds(HALO - j, SPAN), b : b + 1] == here) for j in range(1, taps)]


def segs_of(seg_ref, b):
    return seg_ref[pl.ds(HALO, SPAN), b : b + 1]


def seg_before(seg_ref, b):
    return seg_ref[HALO - 1 : HALO, b : b + 1]


def seg_last(seg_ref, b):
    return seg_ref[HALO + SPAN - 1 : HALO + SPAN, b : b + 1]


def conv_pre(ext_ref, cols, convw_ref, masks):
    taps = len(masks) + 1
    total = convw_ref[taps : taps + 1, cols] + convw_ref[taps - 1 : taps, cols] * ext_ref[pl.ds(HALO, SPAN), :]
    for j in range(1, taps):
        total = total + convw_ref[taps - 1 - j : taps - j, cols] * (
            ext_ref[pl.ds(HALO - j, SPAN), :] * masks[j - 1]
        )
    return total


def vmem_call(body, out_shape, operands, idx=None, scratch=(), mib=8, after=(), us=0.05, hbm=False):
    vm = pl.BlockSpec(memory_space=pltpu.VMEM)
    smem = [] if idx is None else [idx]
    head, tail = len(smem) + len(operands), len(after)

    def run(*refs):
        body(*refs[:head], *refs[head + tail :])

    return pl.pallas_call(
        run,
        out_shape=out_shape,
        in_specs=[pl.BlockSpec(memory_space=pltpu.SMEM)] * len(smem)
        + [pl.BlockSpec(memory_space=pltpu.HBM) if hbm else vm] * len(operands)
        + [pl.BlockSpec(memory_space=pl.ANY)] * tail,
        out_specs=jax.tree.map(lambda _: vm, out_shape),
        scratch_shapes=list(scratch),
        compiler_params=pltpu.CompilerParams(vmem_limit_bytes=mib * 1024 * 1024),
        cost_estimate=pl.CostEstimate(flops=int(us * COST), bytes_accessed=0, transcendentals=0),
        name=body.func.__name__ if isinstance(body, partial) else body.__name__,
    )(*smem, *operands, *after)


def sds(shape, dtype):
    return jax.ShapeDtypeStruct(shape, dtype)


def prep_body(heads, segs_ref, dtb_ref, alog_ref, skip_ref, spread_ref, seg_ref, heads_ref):
    for c0 in range(0, spread_ref.shape[1], WIDE):
        shape = (2 * LANES, WIDE)
        hit = (iota(shape, 0) & (LANES - 1)) == ((iota(shape, 1) + c0) >> 6)
        spread_ref[:, c0 : c0 + WIDE] = ones_where(hit).astype(BF16)
    seg_ref[...] = segs_ref[...].T[0 : HALO + SPAN, :]
    heads_ref[...] = jnp.zeros(heads_ref.shape, F32)
    heads_ref[0:1, :] = jnp.full((1, LANES), OFF, F32)
    for row, ref in enumerate((dtb_ref, alog_ref, skip_ref)):
        heads_ref[row : row + 1, 0:heads] = ref[...].astype(F32)


def small_rows(taps, width):
    third = -(-width // 3)
    return [
        (t, 3 * t + m, m * third, min(third, width - m * third)) for t in range(taps + 1) for m in range(3)
    ]


def pack_body(heads, inner, *refs):
    given, out_ref, end_ref, sems = refs[:5], refs[5], refs[6], refs[-1]
    copies = [pltpu.make_async_copy(a, b, sems.at[i]) for i, (a, b) in enumerate(zip(given, refs[7:12]))]
    for copy in copies:
        copy.start()
    for copy in copies:
        copy.wait()
    w_ref, gain_ref, conv_ref, bias_ref, back_ref = refs[7:12]
    full = w_ref.shape[1] - inner - heads
    taps, width = conv_ref.shape
    flat = lambda ref: ref[...].astype(F32).reshape(1, ref.shape[0])
    out_ref[:, 0:full] = w_ref[:, inner : inner + full]
    end_ref[...] = jnp.zeros(end_ref.shape, F32)
    end_ref[:, 0:heads] = w_ref[:, inner + full :].astype(F32)
    conv, bias, back = conv_ref[...].astype(F32), flat(bias_ref), flat(back_ref)
    for t, row, first, size in small_rows(taps, width):
        value = conv[t : t + 1] if t < taps else bias
        end_ref[row : row + 1, heads : heads + size] = value[:, first : first + size]
    row = 3 * (taps + 1)
    chunk, half = gain_ref.shape[0], back_ref.shape[0] // 2
    end_ref[row : row + 1, heads : heads + chunk] = flat(gain_ref)
    for m in range(2):
        end_ref[row + 1 + m : row + 2 + m, heads : heads + half] = back[:, m * half : (m + 1) * half]
    out_ref[:, full:] = end_ref[...].astype(BF16)


def unpack(heads, taps, shards, end_ref, gain_ref, conv_ref, back_ref):
    chunk = end_ref.shape[0] // shards
    width, half = conv_ref.shape[1] // shards, back_ref.shape[1] // shards // 2
    conv_ref[taps + 1 :, :] = jnp.zeros((7 - taps, conv_ref.shape[1]), F32)
    for i in range(shards):
        at = i * chunk
        for t, row, first, size in small_rows(taps, width):
            conv_ref[t : t + 1, i * width + first : i * width + first + size] = end_ref[
                at + row : at + row + 1, heads : heads + size
            ]
        row = at + 3 * (taps + 1)
        gain_ref[:, i * chunk : (i + 1) * chunk] = end_ref[row : row + 1, heads : heads + chunk]
        for m in range(2):
            first = (2 * i + m) * half
            back_ref[:, first : first + half] = end_ref[row + 1 + m : row + 2 + m, heads : heads + half]


def proj_body(layout, batch, heads, shards, state, *refs):
    idx_ref, tokens_ref, halo_ref, heads_ref, seg_ref, spread_ref = refs[:6]
    pieces = refs[6 : 6 + len(layout)]
    w_ref, normed_ref, gain_ref, convw_ref, back_ref, convin_ref, dtraw_ref = refs[6 + len(layout) : 13 + len(layout)]
    outs = refs[13 + len(layout) : 23 + len(layout)]
    ext_ref, heads_all_ref, end_ref, turned_ref = refs[23 + len(layout) :]
    inner = heads * HEADDIM
    chunk = w_ref.shape[0] // (1 if len(layout) == 1 else 8)

    def store(first, off, view):
        w_ref[pl.ds(pl.multiple_of(first, HALO), view.shape[0]), :] = view[...]

    put_pieces(layout, pieces, idx_ref[0], chunk, store)
    conv_chans = inner + 2 * state
    taps = 4
    end_ref[...] = w_ref[:, conv_chans:].astype(F32)
    unpack(heads, taps, shards, end_ref, gain_ref, convw_ref, back_ref)
    w_ref[:, conv_chans:] = jnp.where(iota(end_ref.shape, 1) < heads, end_ref[...], 0.0).astype(BF16)
    main = tokens_ref.shape[0]
    for ref, first in ((tokens_ref, 0), (halo_ref, main)):
        v = ref[...].astype(F32)
        scale = lax.rsqrt(jnp.mean(v * v, axis=1, keepdims=True) + EPS_NORM)
        normed_ref[pl.ds(first, ref.shape[0]), :] = (v * scale * gain_ref[...]).astype(BF16)
    normed = normed_ref[...]
    raw = nn(normed, w_ref[:, conv_chans : conv_chans + LANES])
    for b in range(batch):
        dtraw_ref[b][...] = raw[b * SPAN : (b + 1) * SPAN].astype(BF16).astype(F32)
    mixer = MixerInput(0, heads_ref, seg_ref, spread_ref, dtraw_ref[0], convin_ref[0], convw_ref, outs)
    mixer.steps(heads_all_ref)
    for c0 in [inner] + list(range(0, inner, WIDE)):
        cols = slice(c0, c0 + WIDE)
        projected = nn(normed, w_ref[:, cols]).astype(BF16)
        for b in range(batch):
            halo0 = batch * SPAN + b * HALO
            convin_ref[b][0:HALO, cols] = projected[halo0 : halo0 + HALO]
            convin_ref[b][HALO : HALO + SPAN, cols] = projected[b * SPAN : (b + 1) * SPAN]
        mixer.columns(c0, inner, state, ext_ref, heads_all_ref, turned_ref)


def second_body(b, inner, state, *refs):
    heads_ref, seg_ref, spread_ref, dtraw_ref, convin_ref, convw_ref = refs[:6]
    ext_ref, heads_all_ref, turned_ref = refs[16:]
    mixer = MixerInput(b, heads_ref, seg_ref, spread_ref, dtraw_ref, convin_ref, convw_ref, refs[6:16])
    mixer.steps(heads_all_ref)
    for c0 in [inner] + list(range(0, inner, WIDE)):
        mixer.columns(c0, inner, state, ext_ref, heads_all_ref, turned_ref)


class MixerInput:
    def __init__(self, b, heads_ref, seg_ref, spread_ref, dtraw_ref, convin_ref, convw_ref, outs):
        self.b, self.heads, self.seg, self.spread = b, heads_ref, seg_ref, spread_ref
        self.dtraw, self.convin, self.convw, self.outs = dtraw_ref, convin_ref, convw_ref, outs

    def steps(self, heads_all_ref):
        b, heads_ref, seg_ref = self.b, self.heads, self.seg
        dt_ref, s_ref, st_ref = self.outs[3:6]
        tri = ones_where(iota((SPAN, SPAN), 0) >= iota((SPAN, SPAN), 1)).astype(BF16)
        self.masks = row_masks(seg_ref, b, 4)
        dt = softplus(self.dtraw[...] + heads_ref[0:1, :])
        dt_ref[...] = dt
        logs = running_sum(tri, dt * -jnp.exp(heads_ref[1:2, :]))
        s_ref[...] = logs
        st_ref[...] = logs.T
        last = logs[SPAN - 1 : SPAN, :]
        same_last = ones_where(segs_of(seg_ref, b) == seg_last(seg_ref, b))
        keep = ones_where(seg_last(seg_ref, b) == seg_before(seg_ref, b))
        heads_all_ref[0:SPAN, :] = split2(dt)
        heads_all_ref[SPAN : 2 * SPAN, :] = split2(jnp.exp(last - logs) * same_last)
        heads_all_ref[2 * SPAN :, :] = split2(jnp.broadcast_to(jnp.exp(last) * keep, (HALO, LANES)))

    def columns(self, c0, inner, state, ext_ref, heads_all_ref, turned_ref):
        x_ref, bc_ref, xdt_ref, _, _, _, fresh_ref, send_ref, decay_ref, slope_ref = self.outs
        cols = slice(c0, c0 + WIDE)
        ext_ref[...] = self.convin[:, cols].astype(F32)
        pre = conv_pre(ext_ref, cols, self.convw, self.masks)
        sig = sigmoid(pre)
        act = pre * sig
        slope_ref[:, cols] = silu_slope(pre, sig).astype(BF16)
        if c0 == inner:
            bc_ref[...] = act.astype(BF16)
            turned_ref[...] = bc_ref[:, 0:state].T
            return
        wide = nn(heads_all_ref[...], self.spread[:, cols])
        x_ref[:, cols] = act
        xdt = (wide[0:SPAN] * act).astype(BF16)
        xdt_ref[:, cols] = xdt
        xt = (wide[SPAN : 2 * SPAN] * xdt.astype(F32)).astype(BF16)
        decay_ref[:, cols] = wide[2 * SPAN : 2 * SPAN + 8]
        fresh = nn(turned_ref[...], xt)
        fresh_ref[:, cols] = fresh
        send_ref[:, cols] = fresh.astype(BF16)


def inside_mask(seg_ref, segr_ref, b, flipped):
    rows, cols = iota((SPAN, SPAN), 0), iota((SPAN, SPAN), 1)
    ordered = rows <= cols if flipped else rows >= cols
    return ordered & (segs_of(seg_ref, b) == segr_ref[b : b + 1, :])


def head_halves(block):
    low = iota(block.shape, 1) < HEADDIM
    zero = jnp.zeros_like(block)
    return jnp.where(low, block, zero), jnp.where(low, zero, block)


def intra_body(state, b, bc_ref, xdt_ref, s_ref, st_ref, seg_ref, segr_ref, y_ref):
    scores = nt(bc_ref[:, state : 2 * state], bc_ref[:, 0:state])
    scores = jnp.where(inside_mask(seg_ref, segr_ref, b, False), scores, 0.0)
    for pair in range(xdt_ref.shape[1] // LANES):
        cols = slice(pair * LANES, (pair + 1) * LANES)
        total = None
        for half, values in enumerate(head_halves(xdt_ref[:, cols])):
            h = 2 * pair + half
            decay = jnp.exp(jnp.minimum(s_ref[:, h : h + 1] - st_ref[h : h + 1, :], 0.0))
            part = nn((scores * decay).astype(BF16), values)
            total = part if total is None else total + part
        y_ref[:, cols] = total


def dense_body(layout, inner, *refs):
    idx_ref, normed_ref, cot_ref = refs[:3]
    pieces = refs[3 : 3 + len(layout)]
    wout_ref, wgate_ref, gating_ref, dout_ref, turned_ref, turn_ref = refs[3 + len(layout) :]
    depth = wgate_ref.shape[0]
    shards = 1 if len(layout) == 1 else 8
    ochunk, gchunk = inner // shards, depth // shards
    half_cols = inner // 2
    def store(owner, off, view):
        wout_ref[pl.ds(pl.multiple_of(owner * ochunk, HALO), ochunk), :] = view[0:ochunk, :]
        for side in range(2):
            wgate_ref[
                pl.ds(pl.multiple_of(owner * gchunk, HALO), gchunk), side * half_cols : (side + 1) * half_cols
            ] = view[ochunk + side * gchunk : ochunk + (side + 1) * gchunk, :]

    put_pieces(layout, pieces, idx_ref[0], 1, store)
    for r0 in range(0, depth, WIDE):
        turn_ref[r0 : r0 + WIDE, :] = normed_ref[:, r0 : r0 + WIDE].T
    for k in range(shards):
        turned_ref[k * gchunk : (k + 1) * gchunk, :] = turn_ref[
            pl.ds(pl.multiple_of((idx_ref[0] ^ k) * gchunk, HALO), gchunk), :
        ]
    normed = normed_ref[0 : cot_ref.shape[0], :]
    cot = cot_ref[...]
    for c0 in range(0, inner, WIDE):
        gating_ref[:, c0 : c0 + WIDE] = nn(normed, wgate_ref[:, c0 : c0 + WIDE])
        dout_ref[:, c0 : c0 + WIDE] = nt(cot, wout_ref[c0 : c0 + WIDE, :])


def gate_body(state, b, *refs):
    (yin_ref, carry_ref, bc_ref, s_ref, seg_ref, x_ref, gating_ref, dout_ref, gain_ref, heads_ref, spread_ref) = refs[:11]
    (outn_ref, dy_ref, ey_ref, dgat_ref, rowterm_ref, grad_ref, send_ref, small_ref) = refs[11:19]
    y_ref, gated_ref, sig_ref, wide_ref, mixed_ref = refs[19:]
    inner = x_ref.shape[1]
    rows = pl.ds(b * SPAN, SPAN)
    c_mat = bc_ref[:, state : 2 * state]
    c_turned = c_mat.T
    carried = ones_where(segs_of(seg_ref, b) == seg_before(seg_ref, b))
    factor = split2(jnp.exp(s_ref[...]) * carried)
    factor = jnp.concatenate([factor, split2(jnp.broadcast_to(heads_ref[2:3, :], (HALO, LANES)))], axis=0)
    sumsq = jnp.zeros((SPAN, 1), F32)
    sumeg = jnp.zeros((SPAN, 1), F32)
    for c0 in range(0, inner, WIDE):
        cols = slice(c0, c0 + WIDE)
        spread = spread_ref[:, cols]
        both = nn(factor, spread)
        wide = both[0:SPAN]
        wide_ref[:, cols] = wide
        y = yin_ref[:, cols] + wide * nn(c_mat, carry_ref[:, cols])
        y_ref[:, cols] = y
        low = (y + both[SPAN : SPAN + 1] * x_ref[:, cols]).astype(BF16)
        mixed_ref[:, cols] = low
        mixed = low.astype(F32)
        gate = gating_ref[rows, cols]
        sig = sigmoid(gate)
        sig_ref[:, cols] = sig
        gated = mixed * (gate * sig)
        gated_ref[:, cols] = gated
        sumsq = sumsq + jnp.sum(gated * gated, axis=1, keepdims=True)
        sumeg = sumeg + jnp.sum(dout_ref[rows, cols] * gain_ref[:, cols] * gated, axis=1, keepdims=True)
    r = lax.rsqrt(sumsq / inner + EPS_NORM)
    coef = r * r * r * (sumeg / inner)
    terms = jnp.zeros((SPAN, LANES), F32)
    skips = jnp.zeros((8, LANES), F32)
    for c0 in range(0, inner, WIDE):
        cols = slice(c0, c0 + WIDE)
        gated = gated_ref[:, cols]
        gain = gain_ref[:, cols]
        dout = dout_ref[rows, cols]
        normal = gated * r
        outn_ref[:, cols] = (normal * gain).astype(BF16)
        y = y_ref[:, cols]
        x = x_ref[:, cols]
        d_gated = r * (dout * gain) - gated * coef
        gate = gating_ref[rows, cols]
        sig = sig_ref[:, cols]
        mixed = mixed_ref[:, cols].astype(F32)
        dgat_ref[:, cols] = (d_gated * mixed * silu_slope(gate, sig)).astype(BF16)
        dy = (d_gated * (gate * sig)).astype(BF16)
        dy_ref[:, cols] = dy
        dyf = dy.astype(F32)
        ey = (wide_ref[:, cols] * dyf).astype(BF16)
        ey_ref[:, cols] = ey
        skip_sum = jnp.broadcast_to(jnp.sum(dyf * x, axis=0, keepdims=True), (HALO, WIDE))
        term, skip = to_heads([dyf * y, skip_sum], spread_ref[0:LANES, cols])
        terms = terms + term
        skips = skips + skip[0:8]
        grad = nn(c_turned, ey)
        grad_ref[:, cols] = grad
        send_ref[:, cols] = grad.astype(BF16)
    rowterm_ref[...] = terms
    small_ref[...] = jnp.where(iota(skips.shape, 0) == 2, skips, 0.0)


def intra_back_body(state, b, *refs):
    (bc_ref, xdt_ref, dy_ref, ey_ref, carry_ref, s_ref, st_ref, seg_ref, segr_ref) = refs[:9]
    dxdt_ref, dbc_ref = refs[9:11]
    acc_ref = refs[11]
    b_mat = bc_ref[:, 0:state]
    c_mat = bc_ref[:, state : 2 * state]
    mask = inside_mask(seg_ref, segr_ref, b, True)
    scores = jnp.where(mask, nt(b_mat, c_mat), 0.0)
    for pair in range(xdt_ref.shape[1] // LANES):
        cols = slice(pair * LANES, (pair + 1) * LANES)
        total = None
        dy_block = dy_ref[:, cols]
        for half, (values, grads) in enumerate(zip(head_halves(xdt_ref[:, cols]), head_halves(dy_block))):
            h = 2 * pair + half
            decay = jnp.exp(jnp.minimum(st_ref[h : h + 1, :] - s_ref[:, h : h + 1], 0.0))
            part = nn((scores * decay).astype(BF16), grads)
            total = part if total is None else total + part
            d_weight = nt(values, dy_block) * decay
            if h == 0:
                acc_ref[...] = d_weight
            else:
                acc_ref[...] += d_weight
        dxdt_ref[:, cols] = total
    d_scores = jnp.where(mask, acc_ref[...], 0.0).astype(BF16)
    dbc_ref[:, 0:state] = nn(d_scores, c_mat)
    dbc_ref[:, state : 2 * state] = tn(d_scores, b_mat) + nt(ey_ref[...], carry_ref[...])


def mixer_back_body(state, b, *refs):
    (convin_ref, dtraw_ref, x_ref, bc_ref, xdt_ref, dt_ref, s_ref, seg_ref, convw_ref, heads_ref) = refs[:10]
    (dxdt_ref, dbc_ref, dy_ref, rowterm_ref, carry_ref, dcarry_ref, spread_ref, slope_ref) = refs[10:18]
    (dmain_ref, dhalo_ref, small_ref, hsmall_ref) = refs[18:22]
    dpre_ref, segs_ref = refs[22:]
    inner = x_ref.shape[1]
    taps = 4
    conv_chans = inner + 2 * state
    rows = HALO + SPAN
    segs_ref[0:rows, :] = seg_ref[...]
    segs_ref[rows:, :] = jnp.zeros((HALO, LANES), F32)
    here = segs_ref[0:rows, b : b + 1]
    masks = [ones_where(segs_ref[pl.ds(j, rows), b : b + 1] == here) for j in range(1, taps)]
    b_mat = bc_ref[:, 0:state]
    logs = s_ref[...]
    dt = dt_ref[...]
    rate = -jnp.exp(heads_ref[1:2, :])
    last = logs[SPAN - 1 : SPAN, :]
    same_last = ones_where(segs_of(seg_ref, b) == seg_last(seg_ref, b))
    keep = ones_where(seg_last(seg_ref, b) == seg_before(seg_ref, b))
    heads_all = jnp.concatenate(
        [
            split2(jnp.exp(last - logs) * same_last),
            split2(dt),
            split2(jnp.broadcast_to(heads_ref[2:3, :], (HALO, LANES))),
        ],
        axis=0,
    )
    col_term = jnp.zeros((SPAN, LANES), F32)
    direct = jnp.zeros((SPAN, LANES), F32)
    last_term = jnp.zeros((HALO, LANES), F32)
    d_b = dbc_ref[:, 0:state]
    dpre_ref[0:HALO, :] = jnp.zeros((HALO, WIDE), F32)
    dpre_ref[HALO + SPAN : HALO + SPAN + HALO, :] = jnp.zeros((HALO, WIDE), F32)
    small_ref[taps + 1 : 8, :] = jnp.zeros((7 - taps, conv_chans), F32)

    def conv_back(cols, d_act):
        ext = convin_ref[:, cols].astype(F32)
        d_pre = d_act * slope_ref[:, cols].astype(F32)
        dpre_ref[pl.ds(HALO, SPAN), :] = d_pre
        small_ref[taps : taps + 1, cols] = jnp.sum(d_pre, axis=0, keepdims=True)
        small_ref[taps - 1 : taps, cols] = jnp.sum(d_pre * ext[HALO:], axis=0, keepdims=True)
        total = convw_ref[taps - 1 : taps, cols] * dpre_ref[pl.ds(0, rows), :]
        for j in range(1, taps):
            moved = masks[j - 1] * dpre_ref[pl.ds(j, rows), :]
            small_ref[taps - 1 - j : taps - j, cols] = jnp.sum(moved * ext, axis=0, keepdims=True)
            total = total + convw_ref[taps - 1 - j : taps - j, cols] * moved
        total = total.astype(BF16)
        dhalo_ref[:, cols] = total[0:HALO]
        dmain_ref[:, cols] = total[HALO : HALO + SPAN]

    for c0 in range(0, inner, WIDE):
        cols = slice(c0, c0 + WIDE)
        spread = spread_ref[:, cols]
        picks = spread_ref[0:LANES, cols]
        d_carry = dcarry_ref[:, cols]
        wide = nn(heads_all, spread)
        tails = wide[0:SPAN]
        xdt = xdt_ref[:, cols].astype(F32)
        d_tail = tails * nn(b_mat, d_carry)
        d_xdt = dxdt_ref[:, cols] + d_tail
        x = x_ref[:, cols]
        from_tail = jnp.sum(xdt * d_tail, axis=0, keepdims=True)
        through = jnp.sum(d_carry.astype(F32) * carry_ref[:, cols].astype(F32), axis=0, keepdims=True)
        both = jnp.concatenate([from_tail, through, jnp.zeros((HALO - 2, WIDE), F32)], axis=0)
        cols_sum, direct_sum, both = to_heads([xdt * d_xdt, x * d_xdt, both], picks)
        col_term = col_term + cols_sum
        direct = direct + direct_sum
        last_term = last_term + both
        d_b = d_b + nt((tails * xdt).astype(BF16), d_carry)
        d_x = wide[SPAN : 2 * SPAN] * d_xdt + wide[2 * SPAN : 2 * SPAN + 1] * dy_ref[:, cols].astype(F32)
        conv_back(cols, d_x)
    conv_back(slice(inner, conv_chans), jnp.concatenate([d_b, dbc_ref[:, state : 2 * state]], axis=1))
    at_end = last_term[0:1, :] + last_term[1:2, :] * (jnp.exp(last) * keep)
    upper = ones_where(iota((SPAN, SPAN), 0) <= iota((SPAN, SPAN), 1)).astype(BF16)
    d_logs = running_sum(upper, rowterm_ref[...] - col_term) + at_end
    d_dt = direct + rate * d_logs
    d_raw = d_dt * sigmoid(dtraw_ref[...] + heads_ref[0:1, :])
    dmain_ref[:, conv_chans : conv_chans + LANES] = d_raw.astype(BF16)
    dhalo_ref[:, conv_chans : conv_chans + LANES] = jnp.zeros((HALO, LANES), BF16)
    hsmall_ref[0:1, :] = jnp.sum(d_raw, axis=0, keepdims=True)
    hsmall_ref[1:2, :] = jnp.sum(dt * d_logs, axis=0, keepdims=True) * rate
    hsmall_ref[2:8, :] = jnp.zeros((6, LANES), F32)


def out_grad_body(shards, *refs):
    (idx_ref, on0_ref, on1_ref, cot_ref, dg0_ref, dg1_ref, normed_ref) = refs[:7]
    outs = refs[7:-2]
    gout_ref, ggate_ref = refs[-2:]
    main = cot_ref.shape[0]
    inner, width = gout_ref.shape
    outn = jnp.concatenate([on0_ref[...], on1_ref[...]], axis=0)
    dgat = jnp.concatenate([dg0_ref[...], dg1_ref[...]], axis=0)
    normed = normed_ref[0:main, :]
    gout_ref[...] = tn(outn, cot_ref[...])
    for c0 in range(0, inner, width):
        ggate_ref[:, c0 : c0 + width] = tn(normed, dgat[:, c0 : c0 + width])
    ochunk, gchunk = inner // shards, width // shards
    for k in range(shards):
        owner = idx_ref[0] ^ k
        ref = outs[0].at[k // 2] if k % 2 == 0 else outs[1 + k // 2]
        ref[0:ochunk, :] = gout_ref[pl.ds(pl.multiple_of(owner * ochunk, HALO), ochunk), :].astype(BF16)
        for side in range(2):
            ref[ochunk + side * gchunk : ochunk + (side + 1) * gchunk, :] = ggate_ref[
                pl.ds(pl.multiple_of(owner * gchunk, HALO), gchunk), side * width : (side + 1) * width
            ].astype(BF16)


def out_body(on0_ref, on1_ref, xin_ref, wout_ref, lout_ref, done_ref):
    done_ref[...] = jnp.zeros(done_ref.shape, F32)
    for b, outn_ref in enumerate((on0_ref, on1_ref)):
        rows = slice(b * SPAN, (b + 1) * SPAN)
        lout_ref[rows, :] = (xin_ref[rows, :].astype(F32) + nn(outn_ref[...], wout_ref[...])).astype(BF16)


def join_rows(m0_ref, m1_ref, h0_ref, h1_ref, all_ref):
    all_ref[0:SPAN, :] = m0_ref[...]
    all_ref[SPAN : 2 * SPAN, :] = m1_ref[...]
    all_ref[2 * SPAN : 2 * SPAN + HALO, :] = h0_ref[...]
    all_ref[2 * SPAN + HALO : 2 * SPAN + 2 * HALO, :] = h1_ref[...]


def in_grad_body(shards, heads, taps, exact, *refs):
    idx_ref, m0_ref, m1_ref, h0_ref, h1_ref, normed_ref = refs[:6]
    conv0_ref, conv1_ref, head0_ref, head1_ref, skip0_ref, skip1_ref = refs[6:12]
    outs = refs[12:-3]
    all_ref, ends_ref, line_ref = refs[-3:]
    join_rows(m0_ref, m1_ref, h0_ref, h1_ref, all_ref)
    depth, wide = normed_ref.shape[0], all_ref.shape[1]
    conv = conv0_ref[...] + conv1_ref[...]
    three = head0_ref[...] + head1_ref[...] + skip0_ref[...] + skip1_ref[...]
    chunk, width = depth // shards, conv.shape[1] // shards
    ends_ref[...] = jnp.zeros(ends_ref.shape, F32)
    for i in range(shards):
        for t, row, first, size in small_rows(taps, width):
            at = i * chunk + row
            ends_ref[at : at + 1, heads : heads + size] = conv[t : t + 1, i * width + first : i * width + first + size]
    if exact:
        line_ref[...] = jnp.zeros(line_ref.shape, F32)
        for m in range(3):
            line_ref[0:1, (m + 1) * heads : (m + 2) * heads] = three[m : m + 1, 0:heads]
        value = line_ref[0:1, :]
        high = value.astype(BF16).astype(F32)
        rows = iota((2 * exact, LANES), 0)
        mine = jnp.where(rows == 2 * idx_ref[1], high, 0.0) + jnp.where(rows == 2 * idx_ref[1] + 1, value - high, 0.0)
        for i in range(shards):
            at = i * chunk + 3 * (taps + 1) + 1
            ends_ref[at : at + 2 * exact, :] = mine
    ways = 1 if len(outs) == 1 else shards
    part = depth // ways
    for c0 in range(0, wide, 384):
        cols = slice(c0, c0 + 384)
        grad = nn(normed_ref[...], all_ref[:, cols])
        for k in range(ways):
            share = grad[k * part : (k + 1) * part]
            out_ref = outs[k % 2].at[k // 2]
            if c0 + 384 < wide:
                out_ref[:, cols] = share.astype(BF16)
                continue
            out_ref[:, c0 : wide - LANES] = share[:, : 384 - LANES].astype(BF16)
            first = pl.multiple_of((idx_ref[0] ^ k) * part, 8)
            out_ref[:, wide - LANES :] = (share[:, 384 - LANES :] + ends_ref[pl.ds(first, part), :]).astype(BF16)


def in_back_body(*refs):
    m0_ref, m1_ref, h0_ref, h1_ref, w_ref, dg0_ref, dg1_ref, wgate_ref, cot_ref, xin_ref, halo_ref, gain_ref = refs[:12]
    igrad_ref, hgrad_ref, all_ref = refs[12:]
    main = cot_ref.shape[0]
    join_rows(m0_ref, m1_ref, h0_ref, h1_ref, all_ref)
    d_normed = nt(all_ref[...], w_ref[...])
    gain = gain_ref[...]

    def back(dn, v):
        q = lax.rsqrt(jnp.mean(v * v, axis=1, keepdims=True) + EPS_NORM)
        e = dn * gain
        return q * e - v * (q * q * q * jnp.mean(e * v, axis=1, keepdims=True))

    for b, dgat_ref in enumerate((dg0_ref, dg1_ref)):
        rows = slice(b * SPAN, (b + 1) * SPAN)
        d_both = d_normed[rows] + nt(dgat_ref[...], wgate_ref[...])
        igrad_ref[rows, :] = cot_ref[rows, :].astype(F32) + back(d_both, xin_ref[rows, :].astype(F32))
    d_halo = back(d_normed[main:], halo_ref[...].astype(F32))
    sent = hgrad_ref.shape[0] // 2
    for b in range(2):
        hgrad_ref[b * sent : (b + 1) * sent, :] = d_halo[(b + 1) * HALO - sent : (b + 1) * HALO]


def xor_pairs(size, k):
    return [(i, i ^ k) for i in range(size)]


def stack_body(*refs):
    out_ref = refs[-1]
    for i, ref in enumerate(refs[:-1]):
        out_ref[i] = ref[...]


def rows_body(top_ref, low_ref, out_ref):
    half = top_ref.shape[0]
    out_ref[0:half, :] = top_ref[...]
    out_ref[half:, :] = low_ref[...]


def stack(parts, after=()):
    return vmem_call(stack_body, sds((len(parts),) + parts[0].shape, BF16), parts, after=after)


def layout_of(pieces):
    return [v for v, _ in pieces], tuple(places for _, places in pieces)


def put_pieces(layout, refs, idx, chunk, store):
    for ref, places in zip(refs, layout):
        for sub, k, off in places:
            view = ref if sub is None else ref.at[sub]
            store((idx ^ k) * chunk + off, off, view)


def combine_body(last, *refs):
    if last:
        got_ref, carry_ref, out_ref = refs
        out_ref[...] = got_ref[...] + carry_ref[...]
        return
    first = len(refs) == 5
    got_ref, fresh_ref, decay_ref = refs[:3]
    out_ref, send_ref = refs[-2:]
    state = got_ref[...] if first else got_ref[...] + refs[3][...]
    out_ref[...] = state
    send_ref[...] = (fresh_ref[...] + decay_ref[0:1, :] * state.astype(F32)).astype(BF16)


class Chain:
    def __init__(self, fresh, send, decay, pairs):
        self.fresh, self.send, self.decay, self.pairs = fresh, send, decay, pairs
        self.state = None
        self.hop = 0
        self.start()

    def start(self):
        self.got = lax.ppermute(self.send, "seq", [self.pairs[self.hop]])

    def step(self, after=(), us=0.05):
        shape = sds(self.got.shape, BF16)
        prior = [] if self.state is None else [self.state]
        if self.hop == len(self.pairs) - 1:
            if prior:
                self.state = vmem_call(partial(combine_body, True), shape, [self.got] + prior, after=after)
            else:
                self.state = self.got
            return self.state
        self.state, self.send = vmem_call(
            partial(combine_body, False),
            (shape, shape),
            [self.got, self.fresh, self.decay] + prior,
            after=after,
            us=us,
        )
        self.hop += 1
        self.start()
        return self.state


def swap(v, k):
    return lax.ppermute(v, "fsdp", xor_pairs(8, k))


def pair_body(even_ref, *refs):
    own_ref, side_ref, down_ref, top_ref, low_ref = refs[-5:]
    got = refs[:-5] if len(refs) > 6 else [refs[0].at[i] for i in range(4)]
    half = top_ref.shape[0]
    add = lambda s: even_ref[s].astype(F32) + got[s][...].astype(F32)
    far = add(3).astype(BF16)
    top_ref[...] = far[0:half]
    low_ref[...] = far[half:]
    own_ref[...] = add(0)
    side_ref[...] = add(1)
    down_ref[...] = add(2)


def relay_body(side_ref, down_ref, top_ref, low_ref, side_out, down_out):
    half = top_ref.shape[0]
    side_out[0:half, :] = side_ref[0:half, :].astype(BF16)
    side_out[half:, :] = (side_ref[half:, :] + low_ref[...].astype(F32)).astype(BF16)
    down_out[0:half, :] = (down_ref[0:half, :] + top_ref[...].astype(F32)).astype(BF16)
    down_out[half:, :] = down_ref[half:, :].astype(BF16)


class Reduce:
    def __init__(self, even, *odd):
        self.even, self.stage = even, 0
        self.got = [swap(v, 1) for v in odd]

    def pair(self, after=()):
        _, rows, cols = self.even.shape
        full, half = sds((rows, cols), F32), sds((rows // 2, cols), BF16)
        self.own, self.side, self.down, top, low = vmem_call(
            pair_body, (full, full, full, half, half), [self.even] + self.got, after=after
        )
        self.top, self.low = swap(top, 2), swap(low, 4)
        return self.own

    def relay(self, after=()):
        shape = sds(self.own.shape, BF16)
        side, down = vmem_call(relay_body, (shape, shape), [self.side, self.down, self.top, self.low], after=after)
        self.side, self.down = swap(side, 2), swap(down, 4)
        return side

    def step(self, z, parts, after=()):
        rows, cols = self.own.shape
        along = lambda v, k: lax.ppermute(v, "seq", xor_pairs(parts, k))
        stage, self.stage = self.stage, self.stage + 1
        if parts != 4:
            if stage == 0:
                total = self.own + self.side.astype(F32) + self.down.astype(F32)
                self.total = lax.psum(total, "seq")
            return self.total
        f32, bf16 = lambda n: sds((n, cols), F32), lambda n: sds((n, cols), BF16)
        whole, half = pltpu.VMEM((rows, cols), F32), pltpu.VMEM((rows // 2, cols), F32)
        if stage == 0:
            given = [self.own, self.side, self.down]
            self.keep, send = vmem_call(
                halve_body, (f32(rows // 2), bf16(rows // 2)), given, idx=z, scratch=[whole], after=after
            )
            self.got = along(send, 1)
            return self.keep
        if stage == 1:
            given = [self.keep, self.got]
            self.keep, send = vmem_call(
                fold_body, (f32(rows // 4), bf16(rows // 4)), given, idx=z, scratch=[half], after=after
            )
            self.got = along(send, 2)
            return self.keep
        if stage == 2:
            self.keep = vmem_call(total_body, bf16(rows // 4), [self.keep, self.got], after=after)
            self.got = along(self.keep, 2)
            return self.keep
        if stage == 3:
            given = [self.keep, self.got]
            self.keep = vmem_call(partial(unfold_body, 1), bf16(rows // 2), given, idx=z, scratch=[half], after=after)
            self.got = along(self.keep, 1)
            return self.keep
        given = [self.keep, self.got]
        return vmem_call(partial(unfold_body, 0), f32(rows), given, idx=z, scratch=[whole], after=after)

    def spread(self, z, parts, after=()):
        rows, cols = self.own.shape
        self.parts, self.z = parts, z
        if parts != 4:
            total = self.own + self.side.astype(F32) + self.down.astype(F32)
            self.total = lax.psum(total, "seq")
            return self.total
        cut = sds((rows // 4, cols), BF16)
        mine, *others = vmem_call(
            spread_body,
            (sds((rows // 4, cols), F32), cut, cut, cut),
            [self.own, self.side, self.down],
            idx=z,
            scratch=[pltpu.VMEM((rows, cols), F32)],
            after=after,
        )
        self.mine = mine
        self.others = [lax.ppermute(v, "seq", xor_pairs(4, k + 1)) for k, v in enumerate(others)]
        return mine

    def collect(self, after=()):
        if self.parts != 4:
            return self.total
        part = vmem_call(collect_body, sds(self.mine.shape, BF16), [self.mine] + self.others, after=after, us=30)
        self.quarters = [part] + [lax.ppermute(part, "seq", xor_pairs(4, k)) for k in (1, 2, 3)]
        return part


def halve_body(z_ref, own_ref, side_ref, down_ref, keep_ref, send_ref, all_ref):
    all_ref[...] = own_ref[...] + side_ref[...].astype(F32) + down_ref[...].astype(F32)
    rows = keep_ref.shape[0]
    bit = z_ref[0] & 1
    keep_ref[...] = all_ref[pl.ds(pl.multiple_of(bit * rows, 8), rows), :]
    send_ref[...] = all_ref[pl.ds(pl.multiple_of((1 - bit) * rows, 8), rows), :].astype(BF16)


def fold_body(z_ref, half_ref, got_ref, keep_ref, send_ref, all_ref):
    all_ref[...] = half_ref[...] + got_ref[...].astype(F32)
    rows = keep_ref.shape[0]
    bit = (z_ref[0] >> 1) & 1
    keep_ref[...] = all_ref[pl.ds(pl.multiple_of(bit * rows, 8), rows), :]
    send_ref[...] = all_ref[pl.ds(pl.multiple_of((1 - bit) * rows, 8), rows), :].astype(BF16)


def total_body(keep_ref, got_ref, out_ref):
    out_ref[...] = (keep_ref[...] + got_ref[...].astype(F32)).astype(BF16)


def unfold_body(shift, z_ref, mine_ref, got_ref, out_ref, all_ref):
    rows = mine_ref.shape[0]
    bit = (z_ref[0] >> shift) & 1
    all_ref[pl.ds(pl.multiple_of(bit * rows, 8), rows), :] = mine_ref[...].astype(F32)
    all_ref[pl.ds(pl.multiple_of((1 - bit) * rows, 8), rows), :] = got_ref[...].astype(F32)
    out_ref[...] = all_ref[...].astype(out_ref.dtype)


def spread_body(z_ref, own_ref, side_ref, down_ref, mine_ref, one_ref, two_ref, three_ref, all_ref):
    all_ref[...] = own_ref[...] + side_ref[...].astype(F32) + down_ref[...].astype(F32)
    rows = mine_ref.shape[0]
    for k, ref in enumerate((mine_ref, one_ref, two_ref, three_ref)):
        first = pl.multiple_of((z_ref[0] ^ k) * rows, 8)
        ref[...] = all_ref[pl.ds(first, rows), :].astype(ref.dtype)


def collect_body(mine_ref, one_ref, two_ref, three_ref, out_ref):
    total = mine_ref[...] + one_ref[...].astype(F32) + two_ref[...].astype(F32) + three_ref[...].astype(F32)
    out_ref[...] = total.astype(BF16)


def final_body(heads, taps, sources, idx_ref, *refs):
    w_ref, gain_ref, wout_ref, back_ref, pair_ref = refs[:5]
    quarters = refs[5:-9]
    grad_ref, gout_ref, ggain_ref, gback_ref, conv_ref, bias_ref, heads_ref = refs[-9:-2]
    rest_ref, sums_ref = refs[-2:]
    rows = quarters[0].shape[0]
    for k, ref in enumerate(quarters):
        first = pl.multiple_of((idx_ref[0] ^ k) * rows, 8) if len(quarters) > 1 else 0
        rest_ref[pl.ds(first, rows), :] = ref[...].astype(F32)
    chunk, half = grad_ref.shape[0], pair_ref.shape[1]
    rows_out = gout_ref.shape[0]
    grad_ref[:, 0:half] = pair_ref[rows_out : rows_out + chunk, :]
    grad_ref[:, half : 2 * half] = pair_ref[rows_out + chunk : rows_out + 2 * chunk, :]
    grad_ref[:, 2 * half :] = rest_ref[:, 0 : grad_ref.shape[1] - 2 * half]
    gout_ref[...] = pair_ref[0:rows_out, :]
    total = jnp.sum(w_ref[...].astype(F32) * grad_ref[...], axis=1, keepdims=True)
    sums_ref[0:chunk, :] = jnp.broadcast_to(total, (chunk, LANES))
    ggain_ref[...] = sums_ref[...].T[0:1, 0:chunk] / gain_ref[...].astype(F32)
    total = jnp.sum(wout_ref[...].astype(F32) * gout_ref[...], axis=1, keepdims=True)
    sums_ref[0:rows_out, :] = jnp.broadcast_to(total, (rows_out, LANES))
    gback_ref[...] = sums_ref[...].T[0:1, 0:rows_out] / back_ref[...].astype(F32)
    width = conv_ref.shape[1]
    lane0 = rest_ref.shape[1] - LANES + heads
    for t, row, first, size in small_rows(taps, width):
        value = rest_ref[row : row + 1, lane0 : lane0 + size]
        if t < taps:
            conv_ref[t : t + 1, first : first + size] = value
        else:
            bias_ref[:, first : first + size] = value
    if sources:
        row = 3 * (taps + 1) + 1
        total = jnp.sum(rest_ref[row : row + 2 * sources, rest_ref.shape[1] - LANES :], axis=0, keepdims=True)
        for m in range(3):
            heads_ref[m : m + 1, :] = total[:, (m + 1) * heads : (m + 2) * heads]
    else:
        heads_ref[...] = jnp.zeros(heads_ref.shape, F32)


def halo_add_body(grad_ref, halo_ref, out_ref):
    out_ref[...] = grad_ref[...]
    for b in range(out_ref.shape[0] // SPAN):
        sent = HALO // 2
        rows = slice((b + 1) * SPAN - sent, (b + 1) * SPAN)
        out_ref[rows, :] = grad_ref[rows, :] + halo_ref[b * sent : (b + 1) * sent, :]


def on_device(
    layer_input,
    segment_ids,
    gain_in,
    in_weight,
    conv_weight,
    conv_bias,
    dt_bias,
    a_log,
    skip_gain,
    gain_out,
    out_weight,
    cotangent,
):
    shards, parts = lax.axis_size("fsdp"), lax.axis_size("seq")
    at_fsdp, at_seq = lax.axis_index("fsdp"), lax.axis_index("seq")
    _, batch, part_len, depth = layer_input.shape
    heads = dt_bias.shape[0]
    inner = heads * HEADDIM
    taps = conv_weight.shape[1]
    conv_chans = conv_weight.shape[0] * shards
    state = (conv_chans - inner) // 2
    assert part_len == SPAN and batch == 2 and state == LANES and taps == 4
    wide = conv_chans + LANES
    main = batch * SPAN
    chunk = depth // shards
    up = [(i, i + 1) for i in range(parts - 1)]
    down = [(i + 1, i) for i in range(parts - 1)]

    custom = shards == 8 and chunk % (2 * HALO) == 0
    rows_out = inner // shards
    line = lambda v: v.reshape(1, -1)
    w_rest = vmem_call(
        partial(pack_body, heads, inner),
        sds((chunk, wide), BF16),
        [in_weight, gain_in, conv_weight.T, conv_bias, gain_out],
        scratch=[
            pltpu.VMEM((chunk, LANES), F32),
            *[pltpu.VMEM(v.shape, BF16) for v in (in_weight, gain_in, conv_weight.T, conv_bias, gain_out)],
            pltpu.SemaphoreType.DMA((5,)),
        ],
        hbm=True,
        mib=60,
    )
    segs = jnp.pad(segment_ids[0], ((0, 0), (HALO, 0)), constant_values=-1).astype(F32)
    segs = lax.dynamic_slice_in_dim(segs, at_seq * SPAN, HALO + SPAN, 1)
    seg_row = jnp.pad(segs[:, HALO:], ((0, 8 - batch), (0, 0)))
    segs = jnp.pad(segs, ((0, LANES - batch), (0, -(HALO + SPAN) % LANES)))
    spread, seg_col, head_rows = vmem_call(
        partial(prep_body, heads),
        (sds((2 * LANES, inner), BF16), sds((HALO + SPAN, LANES), F32), sds((8, LANES), F32)),
        [segs, line(dt_bias), line(a_log), line(skip_gain)],
        after=[w_rest],
    )
    w_pair = jnp.concatenate([out_weight, in_weight[:, : inner // 2], in_weight[:, inner // 2 : inner]], axis=0)
    exact = shards * parts if custom and 3 * (taps + 1) + 1 + 2 * shards * parts <= chunk else 0
    me = (at_seq * shards + at_fsdp).astype(jnp.int32)
    idx = jnp.stack([at_fsdp.astype(jnp.int32) if custom else jnp.int32(0), me])
    z_idx = at_seq.astype(jnp.int32).reshape(1)
    halo_in = lax.ppermute(layer_input[0, :, SPAN - HALO :, :], "seq", up).reshape(batch * HALO, depth)
    if custom:
        side, down_w = swap(w_rest, 2), swap(w_rest, 4)
        early = (side, down_w, seg_col, seg_row, head_rows, idx, z_idx, w_pair, halo_in)
        side, down_w, seg_col, seg_row, head_rows, idx, z_idx, w_pair, halo_in = lax.optimization_barrier(early)
        top, low = swap(down_w[: chunk // 2], 2), swap(side[chunk // 2 :], 4)
        near = stack([w_rest, side, down_w])
        near_other = swap(near, 1)
        far = vmem_call(rows_body, sds((chunk, wide), BF16), [top, low], after=[near])
        far_other = swap(far, 1)
        rest_pieces = [
            (w_rest, [(None, 0, 0)]),
            (side, [(None, 2, 0)]),
            (down_w, [(None, 4, 0)]),
            (far, [(None, 6, 0)]),
            (near_other, [(0, 1, 0), (1, 3, 0), (2, 5, 0)]),
            (far_other, [(None, 7, 0)]),
        ]
        w_pair, _ = lax.optimization_barrier((w_pair, far))
        side, down_w = swap(w_pair, 2), swap(w_pair, 4)
        pair_own = [w_pair, side, down_w]
    else:
        rest_pieces = [(lax.all_gather(w_rest, "fsdp", axis=0, tiled=True), [(None, 0, 0)])]
        whole = lax.all_gather(w_pair, "fsdp", axis=0)
        pair_own = [
            jnp.concatenate(
                [
                    whole[:, :rows_out].reshape(inner, depth),
                    whole[:, rows_out : rows_out + chunk].reshape(depth, depth),
                    whole[:, rows_out + chunk :].reshape(depth, depth),
                ],
                axis=0,
            )
        ]
    tokens = layer_input.reshape(main, depth)
    cot = cotangent.reshape(main, depth)
    both = range(batch)

    rows = main + batch * HALO
    rest_values, layout = layout_of(rest_pieces)
    each = lambda shape, dtype: tuple(sds(shape, dtype) for _ in both)
    mixed_shapes = [
        sds((SPAN, inner), F32),
        sds((SPAN, 2 * state), BF16),
        sds((SPAN, inner), BF16),
        sds((SPAN, LANES), F32),
        sds((SPAN, LANES), F32),
        sds((LANES, SPAN), F32),
        sds((state, inner), F32),
        sds((state, inner), BF16),
        sds((8, inner), F32),
        sds((SPAN, conv_chans), BF16),
    ]
    ext = pltpu.VMEM((HALO + SPAN, WIDE), F32)
    heads_all = pltpu.VMEM((2 * SPAN + HALO, 2 * LANES), BF16)
    turned = pltpu.VMEM((state, SPAN), BF16)
    proj = vmem_call(
        partial(proj_body, layout, batch, heads, shards, state),
        (
            sds((depth, wide), BF16),
            sds((rows, depth), BF16),
            sds((1, depth), F32),
            sds((8, conv_chans), F32),
            sds((1, inner), F32),
            each((HALO + SPAN, conv_chans), BF16),
            each((SPAN, LANES), F32),
            *mixed_shapes,
        ),
        [tokens, halo_in, head_rows, seg_col, spread] + rest_values,
        idx=idx,
        scratch=[ext, heads_all, pltpu.VMEM((depth, LANES), F32), turned],
        us=10,
    )
    w_all, normed, gain_front, convw, gain_back, conv_in, dt_raw = proj[:7]
    forth = [Chain(proj[13], proj[14], proj[15], up)]
    other = vmem_call(
        partial(second_body, 1, inner, state),
        tuple(mixed_shapes),
        [head_rows, seg_col, spread, dt_raw[1], conv_in[1], convw],
        scratch=[ext, heads_all, turned],
        us=3,
    )
    x_all, bc_all, xdt_all, dt_all, s_all, st_all, fresh, send, decay, slope_all = zip(proj[7:], other)

    if custom:
        far_w, pair_own[1], _ = lax.optimization_barrier((pair_own[2], pair_own[1], w_all))
        pair_own.append(swap(far_w, 2))

    hops = len(up)
    second, forth[0].got = lax.optimization_barrier((send[1], forth[0].got))
    forth.append(Chain(fresh[1], second, decay[1], up))
    forth[0].step(after=[send[1]], us=0.05)
    y_in = []
    for b in both:
        y_in.append(
            vmem_call(
                partial(intra_body, state, b),
                sds((SPAN, inner), F32),
                [bc_all[b], xdt_all[b], s_all[b], st_all[b], seg_col, seg_row],
                after=[forth[0].state, pair_own[2]] if custom else [forth[0].state],
                us=2,
            )
        )
    forth[0].step(after=[forth[1].step(after=y_in, us=0.05)], us=0.05)
    if custom:
        *pair_own, _ = lax.optimization_barrier((*pair_own, forth[0].state))
        pair_pieces = [(v, [(None, 2 * m, 0)]) for m, v in enumerate(pair_own)]
        pair_pieces += [(swap(v, 1), [(None, 2 * m + 1, 0)]) for m, v in enumerate(pair_own)]
    else:
        pair_pieces = [(pair_own[0], [(None, 0, 0)])]
    pair_values, layout2 = layout_of(pair_pieces)
    w_out, w_gate, gating, d_outn, turned = vmem_call(
        partial(dense_body, layout2, inner),
        (sds((inner, depth), BF16), sds((depth, inner), BF16), sds((main, inner), F32), sds((main, inner), F32), sds((depth, rows), BF16)),
        [normed, cot] + pair_values,
        idx=idx,
        scratch=[pltpu.VMEM((depth, rows), BF16)],
        after=[forth[0].state],
        us=3,
    )
    forth[1].step(after=[gating])
    for hop in range(2, hops - 1):
        forth[1].step(after=[forth[0].step(after=[forth[1].state])])
    forth[0].step(after=[forth[1].state])

    gated, ebb = [], []
    for b in both:
        gated.append(
            vmem_call(
                partial(gate_body, state, b),
                (
                    sds((SPAN, inner), BF16),
                    sds((SPAN, inner), BF16),
                    sds((SPAN, inner), BF16),
                    sds((SPAN, inner), BF16),
                    sds((SPAN, LANES), F32),
                    sds((state, inner), F32),
                    sds((state, inner), BF16),
                    sds((8, LANES), F32),
                ),
                [y_in[b], forth[b].state, bc_all[b], s_all[b], seg_col, x_all[b], gating, d_outn, gain_back, head_rows, spread],
                scratch=[*[pltpu.VMEM((SPAN, inner), F32)] * 4, pltpu.VMEM((SPAN, inner), BF16)],
                mib=12,
                us=4,
            )
        )
        ebb.append(Chain(gated[b][5], gated[b][6], decay[b], down[::-1]))
        if b == 0:
            forth[1].step(after=[gated[0][4]])
    carry = [forth[b].state for b in both]
    def inner_back_of(b, after):
        return vmem_call(
            partial(intra_back_body, state, b),
            (sds((SPAN, inner), F32), sds((SPAN, 2 * state), F32)),
            [bc_all[b], xdt_all[b], gated[b][1], gated[b][2], carry[b], s_all[b], st_all[b], seg_col, seg_row],
            scratch=[pltpu.VMEM((SPAN, SPAN), F32)],
            after=after,
            us=0.05,
        )

    inner_back = [inner_back_of(0, [gated[1][4]])]
    ebb[0].step(after=[inner_back[0][1]])
    ways = shards if custom else 1
    pair_rows = (inner + 2 * depth) // ways
    halves = lambda r, c: tuple(sds((max(ways // 2, 1), r, c), BF16) for _ in range(min(ways, 2)))
    pair_grads = vmem_call(
        partial(out_grad_body, ways),
        halves(pair_rows, depth)[:1] + tuple(sds((pair_rows, depth), BF16) for _ in range(ways // 2)),
        [gated[0][0], gated[1][0], cot, gated[0][3], gated[1][3], normed],
        idx=idx,
        scratch=[pltpu.VMEM((inner, depth), F32), pltpu.VMEM((depth, inner), F32)],
        mib=20,
        us=4,
    )
    ebb[0].step(after=[ebb[1].step(after=[pair_grads[0]], us=0.05)], us=20)
    inner_back.append(inner_back_of(1, [ebb[0].state]))
    waits = [inner_back[1][1]]
    if custom:
        first = Reduce(*pair_grads)
        waits.append(first.pair(after=[ebb[0].state]))
    ebb[1].step(after=waits)
    waits = [ebb[1].state]
    if custom:
        waits = [first.relay(after=waits)]
    for hop in range(2, hops - 1):
        ebb[1].step(after=[ebb[0].step(after=waits)])

    back = []
    ebb[0].step(after=waits)
    for b in both:
        if b == 1:
            ebb[1].step(after=[back[0][0]])
        back.append(
            vmem_call(
                partial(mixer_back_body, state, b),
                (sds((SPAN, wide), BF16), sds((HALO, wide), BF16), sds((8, conv_chans), F32), sds((8, LANES), F32)),
                [
                    conv_in[b],
                    dt_raw[b],
                    x_all[b],
                    bc_all[b],
                    xdt_all[b],
                    dt_all[b],
                    s_all[b],
                    seg_col,
                    convw,
                    head_rows,
                    inner_back[b][0],
                    inner_back[b][1],
                    gated[b][1],
                    gated[b][4],
                    carry[b],
                    ebb[b].state,
                    spread,
                    slope_all[b],
                ],
                scratch=[pltpu.VMEM((2 * HALO + SPAN, WIDE), F32), pltpu.VMEM((2 * HALO + SPAN, LANES), F32)],
                us=6,
            )
        )
    d_rows = [back[0][0], back[1][0], back[0][1], back[1][1]]
    waits = [first.step(z_idx, parts, after=[back[1][0]])] if custom else []
    rest_grads = vmem_call(
        partial(in_grad_body, shards, heads, taps, exact),
        halves(depth // ways, wide),
        d_rows + [turned, back[0][2], back[1][2], back[0][3], back[1][3], gated[0][7], gated[1][7]],
        idx=idx,
        scratch=[pltpu.VMEM((rows, wide), BF16), pltpu.VMEM((depth, LANES), F32), pltpu.VMEM((8, LANES), F32)],
        after=waits,
        mib=14,
        us=4,
    )
    if custom:
        rest = Reduce(*rest_grads)
        sent = rest.pair()
    out_rows, out_done = vmem_call(
        out_body,
        (sds((main, depth), BF16), sds((8, LANES), F32)),
        [gated[0][0], gated[1][0], tokens, w_out],
        after=[sent] if custom else [rest_grads[0]],
        us=3,
    )
    if custom:
        sent = rest.relay(after=[out_done])
        sent = first.step(z_idx, parts, after=[sent])
    in_grad, halo_grad = vmem_call(
        in_back_body,
        (sds((main, depth), F32), sds((batch * HALO // 2, depth), F32)),
        d_rows + [w_all, gated[0][3], gated[1][3], w_gate, cot, tokens, halo_in, gain_front],
        scratch=[pltpu.VMEM((rows, wide), BF16)],
        after=[sent] if custom else [],
        mib=12,
        us=0.05,
    )
    halo_back = lax.ppermute(halo_grad, "seq", down)
    if custom:
        sent = first.step(z_idx, parts, after=[in_grad])
        sent = rest.spread(z_idx, parts, after=[sent])
        sent = first.step(z_idx, parts, after=[sent])
        sent = rest.collect(after=[sent])
        pair_sum = first.step(z_idx, parts, after=[sent])
        rest_parts = rest.quarters if parts == 4 else [rest.total]
    else:
        whole = pair_grads[0][0]
        cuts = ((0, inner), (inner, inner + depth), (inner + depth, inner + 2 * depth))
        shard_sum = lambda v: lax.psum_scatter(v, "fsdp", scatter_dimension=0, tiled=True)
        pair_sum = lax.psum(jnp.concatenate([shard_sum(whole[lo:hi]) for lo, hi in cuts], axis=0).astype(F32), "seq")
        rest_parts = [lax.psum(shard_sum(rest_grads[0][0]).astype(F32), "seq")]
    input_grad = vmem_call(
        halo_add_body, sds(in_grad.shape, F32), [in_grad, halo_back], after=[sent] if custom else []
    ).reshape(1, batch, SPAN, depth)
    width = conv_chans // shards
    grad_in_weight, grad_out_weight, grad_gain, grad_back, grad_conv, grad_bias, head_sums = vmem_call(
        partial(final_body, heads, taps, exact),
        (
            sds((chunk, in_weight.shape[1]), F32),
            sds((rows_out, depth), F32),
            sds((1, chunk), F32),
            sds((1, rows_out), F32),
            sds((taps, width), F32),
            sds((1, width), F32),
            sds((3, heads), F32),
        ),
        [in_weight, line(gain_in), out_weight, line(gain_out), pair_sum] + rest_parts,
        idx=z_idx,
        scratch=[pltpu.VMEM((chunk, wide), F32), pltpu.VMEM((-(-rows_out // LANES) * LANES, LANES), F32)],
    )
    if not exact:
        three = back[0][3] + back[1][3] + gated[0][7] + gated[1][7]
        head_sums = lax.psum(three[:3, :heads], ("fsdp", "seq"))
    return (
        out_rows.reshape(1, batch, SPAN, depth),
        input_grad,
        grad_gain[0],
        grad_in_weight,
        grad_conv.T,
        grad_bias[0],
        head_sums[0],
        head_sums[1],
        head_sums[2],
        grad_back[0],
        grad_out_weight,
    )


def solution(mesh):
    tokens = P("fsdp", None, "seq", None)
    row, matrix = P("fsdp"), P("fsdp", None)
    return jax.shard_map(
        on_device,
        mesh=mesh,
        in_specs=(tokens, P("fsdp", None, None), row, matrix, matrix, row, P(), P(), P(), row, matrix, tokens),
        out_specs=(tokens, tokens, row, matrix, matrix, row, P(), P(), P(), row, matrix),
        check_vma=False,
    )
```
